128 devices in a mesh: wide: 8 (over z, core), narrow: 16 (over x, y).
Axes of the slice: x: 4, y: 4, z: 4, core: 2. Of those that a mesh axis runs over, the one named last changes fastest.
Arguments:
- feat_a: bfloat16 [8, 16, 2048, 512], P('wide', 'narrow')
- feat_b: bfloat16 [8, 16, 2048, 512], P('wide', 'narrow')
- w_hidden: bfloat16 [512, 512], replicated, may hold values from -0.25 to 0.25
- w_out: bfloat16 [512, 256], replicated, may hold values from -0.25 to 0.25
- send_rows: int32 [8, 16, 16, 128], P('wide', 'narrow'), may hold values from 0 to 2047, as said below
- dest_rows: int32 [8, 16, 16, 128], P('wide', 'narrow'), may hold values from 0 to 2047, as said below
- counts: int32 [8, 16, 16], P('wide', 'narrow'), may hold values from 16 to 128, as said below
- neg_rows: int32 [8, 16, 128], P('wide', 'narrow'), may hold values from 0 to 2047
Outputs:
- loss: float32 [], replicated
- grad_feat_a: bfloat16 [8, 16, 2048, 512], P('wide', 'narrow')
- grad_feat_b: bfloat16 [8, 16, 2048, 512], P('wide', 'narrow')
- grad_w_hidden: float32 [512, 512], replicated
- grad_w_out: float32 [512, 256], replicated
The draws below stay inside these ranges and needn't reach their ends.
Inputs may be any that keep to these rules, and one draw needn't show every extreme that they name: `counts`: in every draw some destination gets all 128 slots live from every source of its group, and some source fills all 128 slots for every destination. `send_rows`: on each device every view-B row stands in exactly one of its slots to the destinations. `dest_rows`: on each destination every view-A row is named by exactly one of the slots arriving from the sources of its group.
All inputs are finite; a program needn't handle non-finite values.
Results may differ from the reference program's by a relative error of at most 0.04.
Values may be sent and summed in bfloat16 or wider, within the bound.
A program may use at most 128 MiB of HBM per device.

```python
import jax
import jax.numpy as jnp
from jax import lax

D = 512
HID = 512
EMB = 256
PTS = 2048
NEG = 128
CAP = 128
N_WIDE = 8
N_NARROW = 16


def shuffled(key_one):
    return jax.random.permutation(key_one, PTS)


def match_plan(key):
    send_keys = jax.random.split(jax.random.fold_in(key, 201), N_WIDE * N_NARROW)
    dest_keys = jax.random.split(jax.random.fold_in(key, 202), N_WIDE * N_NARROW)
    send_plan = jax.vmap(shuffled)(send_keys).astype(jnp.int32).reshape(N_WIDE, N_NARROW, N_NARROW, CAP)
    dest_order = jax.vmap(shuffled)(dest_keys).astype(jnp.int32).reshape(N_WIDE, N_NARROW, PTS)
    dest_plan = dest_order.reshape(N_WIDE, N_NARROW, N_NARROW, CAP).transpose(0, 2, 1, 3)
    return (send_plan, dest_plan, dest_order)


def view_b_noise(key):
    return jax.random.normal(jax.random.fold_in(key, 203), (N_WIDE, N_NARROW, PTS, D), jnp.float32)


def finish_points(blended, key):
    devices = N_WIDE * N_NARROW
    device_place = jnp.arange(devices, dtype=jnp.float32).reshape(N_WIDE, N_NARROW, 1, 1)
    device_ramp = 1.0 + 2.0 * device_place / max(devices - 1, 1)
    return blended * device_ramp


def pick_rows(source_table, row_index):
    return source_table[row_index]


def draw_feat_a(key, part):
    base_b = view_b_noise(key)
    send_plan, dest_plan, dest_order = match_plan(key)
    key = jax.random.fold_in(key, 3)
    slot_of_row = jnp.argsort(dest_order, axis=2).astype(jnp.int32)
    send_by_target = send_plan.transpose(0, 2, 1, 3).reshape(N_WIDE, N_NARROW, PTS)
    source_row = jnp.take_along_axis(send_by_target, slot_of_row, axis=2)
    flat_index = slot_of_row // CAP * PTS + source_row
    matched = jax.vmap(pick_rows)(base_b.reshape(N_WIDE, N_NARROW * PTS, D), flat_index.reshape(N_WIDE, N_NARROW * PTS))
    matched = matched.reshape(N_WIDE, N_NARROW, PTS, D)
    fresh_noise = jax.random.normal(jax.random.fold_in(key, 1), (N_WIDE, N_NARROW, PTS, D), jnp.float32)
    center = jax.random.uniform(jax.random.fold_in(key, 4), (N_WIDE, 1, 1, 1), jnp.float32, 0.72, 0.88)
    kinship = center + jax.random.uniform(jax.random.fold_in(key, 5), (N_WIDE, N_NARROW, PTS, 1), jnp.float32, -0.12, 0.09)
    blended = kinship * matched + jnp.sqrt(1.0 - kinship * kinship) * fresh_noise
    return finish_points(blended, key).astype(jnp.bfloat16)


def draw_feat_b(key, part):
    base_b = view_b_noise(key)
    key = jax.random.fold_in(key, 5)
    return finish_points(base_b, key).astype(jnp.bfloat16)


def draw_send_rows(key, part):
    send_plan, dest_plan, dest_order = match_plan(key)
    return send_plan


def draw_dest_rows(key, part):
    send_plan, dest_plan, dest_order = match_plan(key)
    return dest_plan


def draw_counts(key, part):
    key = jax.random.fold_in(key, 11)
    devices = N_WIDE * N_NARROW
    slot_shape = (N_WIDE, N_NARROW, N_NARROW)
    place = jnp.arange(devices, dtype=jnp.int32).reshape(N_WIDE, N_NARROW, 1)
    ceiling = CAP * (devices - 1 + 3 * place) // (4 * (devices - 1))
    floor_value = jnp.maximum(ceiling // 2, 1)
    spread = jax.random.randint(jax.random.fold_in(key, 1), slot_shape, 0, 1 << 20)
    filled = floor_value + spread % (ceiling - floor_value + 1)
    pick_group = jax.random.randint(jax.random.fold_in(key, 3), (), 0, N_WIDE)
    pick_target = jax.random.randint(jax.random.fold_in(key, 5), (), 0, N_NARROW)
    other_group = jax.random.randint(jax.random.fold_in(key, 6), (), 0, N_WIDE)
    pick_source = jax.random.randint(jax.random.fold_in(key, 4), (), 1, N_NARROW)
    least_target = (pick_target + 1) % N_NARROW
    filled = filled.at[0, 0, least_target].set(max(1, CAP // 8))
    filled = filled.at[pick_group, :, pick_target].set(CAP)
    filled = filled.at[other_group, pick_source, :].set(CAP)
    return filled.astype(jnp.int32)


def plant(values, stream_key, low, high):
    shape = values.shape
    spot = [jax.random.randint(jax.random.fold_in(stream_key, axis), (), 0, shape[axis]) for axis in range(len(shape))]
    values = values.at[tuple(spot)].set(low)
    longest = shape.index(max(shape))
    spot[longest] = (spot[longest] + 1) % shape[longest]
    return values.at[tuple(spot)].set(high)


def bell_draw(own_key, shape, width, bound, kind=jnp.bfloat16):
    drawn = jax.random.normal(own_key, shape, jnp.float32) * width
    return jnp.minimum(jnp.maximum(drawn, -bound), bound).astype(kind)


def setup_inputs(seed: int = 0) -> dict:
    streams_of = jax.random.split(jax.random.key(seed), 9)
    return {
        "feat_a": draw_feat_a(jax.random.fold_in(streams_of[8], 71), 0),
        "feat_b": draw_feat_b(jax.random.fold_in(streams_of[8], 71), 0),
        "w_hidden": bell_draw(streams_of[2], (D, HID), D ** -0.5, 0.25),
        "w_out": bell_draw(streams_of[3], (HID, EMB), HID ** -0.5, 0.25),
        "send_rows": draw_send_rows(jax.random.fold_in(streams_of[8], 71), 0),
        "dest_rows": draw_dest_rows(jax.random.fold_in(streams_of[8], 71), 0),
        "counts": draw_counts(jax.random.fold_in(streams_of[8], 71), 0),
        "neg_rows": plant(jax.random.randint(streams_of[7], (N_WIDE, N_NARROW, NEG), 0, PTS), jax.random.fold_in(streams_of[7], 1), 0, PTS - 1).astype(jnp.int32),
    }


sharpness_divisor = 0.07

def project(feat_rows, w_hidden, w_out):
    linear = jnp.dot(feat_rows, w_hidden, preferred_element_type=jnp.float32)
    count = linear.shape[0]
    mean_lin = lax.optimization_barrier(jnp.sum(linear, axis=0)) / count
    var_lin = lax.optimization_barrier(jnp.sum(linear * linear, axis=0)) / count - mean_lin * mean_lin
    inv_std = lax.rsqrt(var_lin + 1e-05)
    normed = (linear - mean_lin) * inv_std
    active = jnp.maximum(normed, 0.0).astype(jnp.bfloat16)
    out_rows = jnp.dot(active, w_out, preferred_element_type=jnp.float32)
    unit_scale = lax.rsqrt(lax.optimization_barrier(jnp.sum(out_rows * out_rows, axis=1, keepdims=True)) + 1e-06)
    unit = out_rows * unit_scale
    return (normed, inv_std, active, unit_scale, unit)

def pair_terms(probe_entry_count, key_rows, usable_pair_indicator, contrast_sample_entries, parameter_derivative):
    probe_embedding_matrix = probe_entry_count.astype(jnp.float32)
    anchor_embedding_matrix = key_rows.astype(jnp.float32)
    matched_similarity_score = lax.optimization_barrier(jnp.sum(probe_embedding_matrix * anchor_embedding_matrix, axis=1)) / sharpness_divisor
    compared_entry_count = jnp.dot(probe_entry_count, contrast_sample_entries.T, preferred_element_type=jnp.float32) / sharpness_divisor
    exp_pos = jnp.exp(matched_similarity_score)
    exp_neg = jnp.exp(compared_entry_count)
    denominator = exp_pos + lax.optimization_barrier(jnp.sum(exp_neg, axis=1))
    loss_sum = jnp.sum((jnp.log(denominator) - matched_similarity_score) * usable_pair_indicator)
    scaling_factor = parameter_derivative / sharpness_divisor * usable_pair_indicator
    pair_coeff = scaling_factor * (exp_pos / denominator - 1.0)
    neg_weight = (scaling_factor[:, None] * exp_neg / denominator[:, None]).astype(jnp.bfloat16)
    grad_query = pair_coeff[:, None] * anchor_embedding_matrix + jnp.dot(neg_weight, contrast_sample_entries, preferred_element_type=jnp.float32)
    grad_neg = jnp.dot(neg_weight.T, probe_entry_count, preferred_element_type=jnp.float32)
    grad_key = pair_coeff[:, None] * probe_embedding_matrix
    return (loss_sum, grad_query, grad_key, grad_neg)

def project_back(feat_rows, grad_embed, normed, inv_std, active, unit_scale, unit, w_hidden, w_out):
    inner_prod = lax.optimization_barrier(jnp.sum(unit * grad_embed, axis=1, keepdims=True))
    grad_out = (unit_scale * (grad_embed - unit * inner_prod)).astype(jnp.bfloat16)
    grad_wo = jnp.dot(active.T, grad_out, preferred_element_type=jnp.float32)
    grad_act = jnp.dot(grad_out, w_out.T, preferred_element_type=jnp.float32)
    grad_norm = jnp.where(normed > 0, grad_act, 0.0)
    count = normed.shape[0]
    mean_grad = lax.optimization_barrier(jnp.sum(grad_norm, axis=0)) / count
    mean_cross = lax.optimization_barrier(jnp.sum(grad_norm * normed, axis=0)) / count
    grad_linear = (inv_std * (grad_norm - mean_grad - normed * mean_cross)).astype(jnp.bfloat16)
    grad_wh = jnp.dot(feat_rows.T, grad_linear, preferred_element_type=jnp.float32)
    grad_feat = jnp.dot(grad_linear, w_hidden.T, preferred_element_type=jnp.float32).astype(jnp.bfloat16)
    return (grad_feat, grad_wh, grad_wo)

def take_rows(table, row_ids):
    return table[row_ids]

def reference(feat_a, feat_b, w_hidden, w_out, send_rows, dest_rows, counts, neg_rows):
    flat_a = feat_a.reshape(-1, D)
    flat_b = feat_b.reshape(-1, D)
    normed_a, inv_std_a, active_a, scale_a, unit_a = project(flat_a, w_hidden, w_out)
    normed_b, inv_std_b, active_b, scale_b, unit_b = project(flat_b, w_hidden, w_out)
    embed_a = unit_a.astype(jnp.bfloat16).reshape(N_WIDE, N_NARROW, PTS, EMB)
    embed_b = unit_b.astype(jnp.bfloat16).reshape(N_WIDE, N_NARROW, PTS, EMB)
    pair_total = jnp.sum(counts).astype(jnp.float32)
    parameter_derivative = jnp.float32(N_WIDE * N_NARROW * PTS) / pair_total
    slot_ids = jnp.arange(CAP)
    loss_all = jnp.zeros((), jnp.float32)
    grads_a = []
    grads_b = []
    for group_index in range(N_WIDE):
        group_a = embed_a[group_index]
        group_b = embed_b[group_index]
        group_send = send_rows[group_index]
        group_dest = dest_rows[group_index]
        group_counts = counts[group_index]
        group_neg = neg_rows[group_index]
        contrast_sample_entries = jax.vmap(take_rows)(group_b, group_neg).reshape(-1, EMB)

        def per_source(source):
            key_rows = group_b[source][group_send[source]].reshape(-1, EMB)
            probe_entry_count = jax.vmap(take_rows)(group_a, group_dest[source]).reshape(-1, EMB)
            usable_pair_indicator = (slot_ids[None, :] < group_counts[source][:, None]).astype(jnp.float32).reshape(-1)
            return pair_terms(probe_entry_count, key_rows, usable_pair_indicator, contrast_sample_entries, parameter_derivative)
        loss_src, grad_query, grad_key, grad_neg = lax.map(per_source, jnp.arange(N_NARROW))
        loss_all = loss_all + jnp.sum(loss_src)
        grad_query = grad_query.reshape(N_NARROW, N_NARROW, CAP, EMB)
        neg_total = lax.optimization_barrier(jnp.sum(grad_neg, axis=0)).reshape(N_NARROW, NEG, EMB)

        def to_target(target):
            rows_in = grad_query[:, target].reshape(-1, EMB)
            return jax.ops.segment_sum(rows_in, group_dest[:, target].reshape(-1), num_segments=PTS)

        def to_owner(key_grad, sent_ids, neg_grad, neg_ids):
            first = jax.ops.segment_sum(key_grad, sent_ids.reshape(-1), num_segments=PTS)
            return first + jax.ops.segment_sum(neg_grad, neg_ids, num_segments=PTS)
        grads_a.append(jax.vmap(to_target)(jnp.arange(N_NARROW)))
        grads_b.append(jax.vmap(to_owner)(grad_key, group_send, neg_total, group_neg))
    grad_embed_a = jnp.stack(grads_a).reshape(-1, EMB)
    grad_embed_b = jnp.stack(grads_b).reshape(-1, EMB)
    feat_grad_a, wh_a, wo_a = project_back(flat_a, grad_embed_a, normed_a, inv_std_a, active_a, scale_a, unit_a, w_hidden, w_out)
    feat_grad_b, wh_b, wo_b = project_back(flat_b, grad_embed_b, normed_b, inv_std_b, active_b, scale_b, unit_b, w_hidden, w_out)
    loss = loss_all / pair_total
    return (loss, feat_grad_a.reshape(feat_a.shape), feat_grad_b.reshape(feat_b.shape), wh_a + wh_b, wo_a + wo_b)
```

```python
import jax
import jax.numpy as jnp
from jax import lax
from jax.experimental import pallas as pl
from jax.experimental.pallas import tpu as pltpu
from jax.sharding import PartitionSpec as P

sharpness_divisor = 0.07
MESH = pl.DeviceIdType.MESH
GROUP = 16


def small_sum_kernel(x_ref, o_ref, near, part, far, send_n, recv_n, send_w, recv_w):
    w = lax.axis_index("wide")
    n = lax.axis_index("narrow")
    n_wide = far.shape[0]
    n_narrow = near.shape[0]
    barrier = pltpu.get_barrier_semaphore()
    for d in range(1, n_narrow):
        pl.semaphore_signal(
            barrier, inc=1, device_id=(w, lax.rem(n + d, n_narrow)), device_id_type=MESH
        )
    for d in range(1, n_wide):
        pl.semaphore_signal(
            barrier, inc=1, device_id=(lax.rem(w + d, n_wide), n), device_id_type=MESH
        )
    pl.semaphore_wait(barrier, n_narrow + n_wide - 2)
    first = [
        pltpu.make_async_remote_copy(
            src_ref=x_ref,
            dst_ref=near.at[n],
            send_sem=send_n.at[d],
            recv_sem=recv_n.at[d],
            device_id=(w, lax.rem(n + d, n_narrow)),
            device_id_type=MESH,
        )
        for d in range(1, n_narrow)
    ]
    for copy in first:
        copy.start()
    near[n] = x_ref[...]
    for copy in first:
        copy.wait()
    part[...] = jnp.sum(near[...], axis=0)
    second = [
        pltpu.make_async_remote_copy(
            src_ref=part,
            dst_ref=far.at[w],
            send_sem=send_w.at[d],
            recv_sem=recv_w.at[d],
            device_id=(lax.rem(w + d, n_wide), n),
            device_id_type=MESH,
        )
        for d in range(1, n_wide)
    ]
    for copy in second:
        copy.start()
    far[w] = part[...]
    for copy in second:
        copy.wait()
    o_ref[...] = jnp.sum(far[...], axis=0)


def small_sum(x, collective_id):
    n_wide, n_narrow = lax.axis_size("wide"), lax.axis_size("narrow")
    vmem = pl.BlockSpec(memory_space=pltpu.VMEM)
    return pl.pallas_call(
        small_sum_kernel,
        out_shape=jax.ShapeDtypeStruct(x.shape, x.dtype),
        in_specs=[vmem],
        out_specs=vmem,
        scratch_shapes=[
            pltpu.VMEM((n_narrow,) + x.shape, x.dtype),
            pltpu.VMEM(x.shape, x.dtype),
            pltpu.VMEM((n_wide,) + x.shape, x.dtype),
            pltpu.SemaphoreType.DMA((n_narrow,)),
            pltpu.SemaphoreType.DMA((n_narrow,)),
            pltpu.SemaphoreType.DMA((n_wide,)),
            pltpu.SemaphoreType.DMA((n_wide,)),
        ],
        compiler_params=pltpu.CompilerParams(
            collective_id=collective_id, has_side_effects=True
        ),
        name=f"small_sum_{collective_id}",
    )(x)


def grad_sum_kernel(
    x_ref, o_ref, half, own, near, chunk, far, out, pair_sem, send_b, recv_b, send_c, recv_c, send_d, recv_d
):
    w = lax.axis_index("wide")
    n = lax.axis_index("narrow")
    n_narrow = near.shape[0]
    n_z = far.shape[0]
    rows = near.shape[1]
    span = n_narrow * rows
    z, c = w // 2, lax.rem(w, 2)
    partner = (2 * z + 1 - c, n)
    peers = [(w, lax.rem(n + d, n_narrow)) for d in range(1, n_narrow)]
    stack = [(2 * lax.rem(z + d, n_z) + c, n) for d in range(1, n_z)]
    barrier = pltpu.get_barrier_semaphore()
    for device in [partner] + peers + stack:
        pl.semaphore_signal(barrier, inc=1, device_id=device, device_id_type=MESH)
    pl.semaphore_wait(barrier, n_narrow + n_z - 1)

    def send(src, dst, send_sem, recv_sem, device):
        return pltpu.make_async_remote_copy(
            src_ref=src,
            dst_ref=dst,
            send_sem=send_sem,
            recv_sem=recv_sem,
            device_id=device,
            device_id_type=MESH,
        )

    mine = pl.multiple_of(c * span, span)
    other = pl.multiple_of((1 - c) * span, span)
    swap = send(x_ref.at[pl.ds(other, span)], half, pair_sem.at[0], pair_sem.at[1], partner)
    swap.start()
    swap.wait()
    own[...] = (
        x_ref[pl.ds(mine, span), :].astype(jnp.float32) + half[...].astype(jnp.float32)
    ).astype(jnp.bfloat16)
    copies = [
        send(
            own.at[pl.ds(pl.multiple_of(peer[1] * rows, rows), rows)],
            near.at[n],
            send_b.at[d],
            recv_b.at[d],
            peer,
        )
        for d, peer in enumerate(peers)
    ]
    for copy in copies:
        copy.start()
    near[n] = own[pl.ds(pl.multiple_of(n * rows, rows), rows), :]
    for copy in copies:
        copy.wait()
    chunk[...] = jnp.sum(near[...].astype(jnp.float32), axis=0).astype(jnp.bfloat16)
    copies = [
        send(chunk, far.at[z], send_c.at[d], recv_c.at[d], peer) for d, peer in enumerate(stack)
    ]
    for copy in copies:
        copy.start()
    far[z] = chunk[...]
    for copy in copies:
        copy.wait()
    place = pl.multiple_of(mine + n * rows, rows)
    out[pl.ds(place, rows), :] = jnp.sum(far[...].astype(jnp.float32), axis=0).astype(jnp.bfloat16)
    copies = [
        send(out.at[pl.ds(place, rows)], out.at[pl.ds(place, rows)], send_d.at[d], recv_d.at[d], peer)
        for d, peer in enumerate(peers)
    ]
    for copy in copies:
        copy.start()
    for copy in copies:
        copy.wait()
    swap = send(
        out.at[pl.ds(mine, span)], out.at[pl.ds(mine, span)], pair_sem.at[2], pair_sem.at[3], partner
    )
    swap.start()
    swap.wait()
    o_ref[...] = out[...].astype(jnp.float32)


def grad_sum(wh, wo, collective_id):
    n_narrow, n_z = lax.axis_size("narrow"), lax.axis_size("wide") // 2
    width = wo.shape[1]
    pieces = wh.shape[1] // width
    x = jnp.concatenate(
        [wh[:, i * width : (i + 1) * width] for i in range(pieces)] + [wo], axis=0
    ).astype(jnp.bfloat16)
    total = x.shape[0]
    span = total // 2
    rows = span // n_narrow
    vmem = pl.BlockSpec(memory_space=pltpu.VMEM)
    dma = pltpu.SemaphoreType.DMA
    bf16 = jnp.bfloat16
    got = pl.pallas_call(
        grad_sum_kernel,
        out_shape=jax.ShapeDtypeStruct(x.shape, jnp.float32),
        in_specs=[vmem],
        out_specs=vmem,
        scratch_shapes=[
            pltpu.VMEM((span, width), bf16),
            pltpu.VMEM((span, width), bf16),
            pltpu.VMEM((n_narrow, rows, width), bf16),
            pltpu.VMEM((rows, width), bf16),
            pltpu.VMEM((n_z, rows, width), bf16),
            pltpu.VMEM((total, width), bf16),
            dma((4,)),
            dma((n_narrow,)),
            dma((n_narrow,)),
            dma((n_z,)),
            dma((n_z,)),
            dma((n_narrow,)),
            dma((n_narrow,)),
        ],
        compiler_params=pltpu.CompilerParams(
            collective_id=collective_id, has_side_effects=True, vmem_limit_bytes=32 * 1024 * 1024
        ),
        name="grad_sum",
    )(x)
    depth = wh.shape[0]
    out_wh = jnp.concatenate([got[i * depth : (i + 1) * depth] for i in range(pieces)], axis=1)
    return out_wh, got[pieces * depth :]


def finish(linear, sum_lin, square_lin, all_points, w_out):
    mean_lin = sum_lin / all_points
    var_lin = square_lin / all_points - mean_lin * mean_lin
    inv_std = lax.rsqrt(var_lin + 1e-05)
    normed = (linear - mean_lin) * inv_std
    active = jnp.maximum(normed, 0.0).astype(jnp.bfloat16)
    out_rows = jnp.dot(active, w_out, preferred_element_type=jnp.float32)
    unit_scale = lax.rsqrt(jnp.sum(out_rows * out_rows, axis=1, keepdims=True) + 1e-06)
    return (normed, inv_std, active, unit_scale, out_rows * unit_scale)


def pair_terms(
    probe_entry_count,
    key_rows,
    usable_pair_indicator,
    contrast_sample_entries,
    parameter_derivative,
):
    probe_embedding_matrix = probe_entry_count.astype(jnp.float32)
    anchor_embedding_matrix = key_rows.astype(jnp.float32)
    matched_similarity_score = (
        jnp.sum(probe_embedding_matrix * anchor_embedding_matrix, axis=1) / sharpness_divisor
    )
    compared_entry_count = (
        lax.dot_general(
            probe_entry_count,
            contrast_sample_entries,
            (((1,), (1,)), ((), ())),
            preferred_element_type=jnp.float32,
        )
        / sharpness_divisor
    )
    exp_pos = jnp.exp(matched_similarity_score)
    exp_neg = jnp.exp(compared_entry_count)
    denominator = exp_pos + jnp.sum(exp_neg, axis=1)
    loss_sum = jnp.sum((jnp.log(denominator) - matched_similarity_score) * usable_pair_indicator)
    scaling_factor = parameter_derivative / sharpness_divisor * usable_pair_indicator
    pair_coeff = scaling_factor * (exp_pos / denominator - 1.0)
    neg_weight = (scaling_factor[:, None] * exp_neg / denominator[:, None]).astype(jnp.bfloat16)
    grad_query = pair_coeff[:, None] * anchor_embedding_matrix + jnp.dot(
        neg_weight, contrast_sample_entries, preferred_element_type=jnp.float32
    )
    grad_neg = lax.dot_general(
        neg_weight, probe_entry_count, (((0,), (0,)), ((), ())), preferred_element_type=jnp.float32
    )
    return (loss_sum, grad_query, pair_coeff, grad_neg)


def back_top(grad_embed, unit, unit_scale, active, normed, w_out):
    inner_prod = jnp.sum(unit * grad_embed, axis=1, keepdims=True)
    grad_out = (unit_scale * (grad_embed - unit * inner_prod)).astype(jnp.bfloat16)
    grad_wo = lax.dot_general(
        active, grad_out, (((0,), (0,)), ((), ())), preferred_element_type=jnp.float32
    )
    grad_act = lax.dot_general(
        grad_out, w_out, (((1,), (1,)), ((), ())), preferred_element_type=jnp.float32
    )
    return (grad_wo, jnp.where(normed > 0, grad_act, 0.0))


def back_bottom(feat_rows, grad_norm, normed, inv_std, sum_grad, sum_cross, all_points, w_hidden):
    mean_grad = sum_grad / all_points
    mean_cross = sum_cross / all_points
    grad_linear = (inv_std * (grad_norm - mean_grad - normed * mean_cross)).astype(jnp.bfloat16)
    grad_wh = lax.dot_general(
        feat_rows, grad_linear, (((0,), (0,)), ((), ())), preferred_element_type=jnp.float32
    )
    grad_feat = lax.dot_general(
        grad_linear, w_hidden, (((1,), (1,)), ((), ())), preferred_element_type=jnp.float32
    )
    return (grad_feat.astype(jnp.bfloat16), grad_wh)


def body(feat_a, feat_b, w_hidden, w_out, send_rows, dest_rows, counts, neg_rows):
    points = feat_a.shape[2]
    feat_width = feat_a.shape[3]
    embed_width = w_out.shape[1]
    group_size = lax.axis_size("narrow")
    slot_count = send_rows.shape[3]
    all_points = lax.axis_size("wide") * group_size * points
    rows_a = feat_a.reshape(points, feat_width)
    rows_b = feat_b.reshape(points, feat_width)
    linear_a = jnp.dot(rows_a, w_hidden, preferred_element_type=jnp.float32)
    linear_b = jnp.dot(rows_b, w_hidden, preferred_element_type=jnp.float32)
    moments = (
        jnp.sum(linear_a, axis=0),
        jnp.sum(linear_a * linear_a, axis=0),
        jnp.sum(linear_b, axis=0),
        jnp.sum(linear_b * linear_b, axis=0),
    )
    pair_count = jnp.sum(counts).astype(jnp.float32)
    zero = jnp.zeros((3, moments[0].shape[0]), jnp.float32)
    summed = small_sum(
        jnp.concatenate([jnp.stack(moments), jnp.full_like(zero[:1], pair_count), zero]), 1
    )
    sum_a, square_a, sum_b, square_b = summed[0], summed[1], summed[2], summed[3]
    normed_a, inv_std_a, active_a, scale_a, unit_a = finish(
        linear_a, sum_a, square_a, all_points, w_out
    )
    normed_b, inv_std_b, active_b, scale_b, unit_b = finish(
        linear_b, sum_b, square_b, all_points, w_out
    )
    embed_a = unit_a.astype(jnp.bfloat16)
    embed_b = unit_b.astype(jnp.bfloat16)
    sent_ids = send_rows.reshape(group_size * slot_count)
    keys_out = embed_b[sent_ids].reshape(group_size, slot_count, embed_width)
    got_keys, got_dest, got_count = (
        lax.all_to_all(keys_out, "narrow", split_axis=0, concat_axis=0, tiled=True),
        lax.all_to_all(
            dest_rows.reshape(group_size, slot_count),
            "narrow",
            split_axis=0,
            concat_axis=0,
            tiled=True,
        ),
        lax.all_to_all(
            counts.reshape(group_size), "narrow", split_axis=0, concat_axis=0, tiled=True
        ),
    )
    neg_ids = neg_rows.reshape(-1)
    contrast_sample_entries = lax.all_gather(embed_b[neg_ids], "narrow", axis=0, tiled=True)
    pair_total = summed[4, 0]
    parameter_derivative = jnp.float32(all_points) / pair_total
    pair_rows = group_size * slot_count
    usable_pair_indicator = (
        (jnp.arange(slot_count)[None, :] < got_count[:, None]).astype(jnp.float32).reshape(-1)
    )
    dest_flat = got_dest.reshape(-1)
    probe_entry_count = embed_a[dest_flat]
    key_rows = got_keys.reshape(pair_rows, embed_width)
    block_rows = min(1024, pair_rows)
    block_count = pair_rows // block_rows

    def one_block(running, part_rows):
        query_blk, key_blk, live_blk = part_rows
        loss_sum, grad_query, pair_coeff, grad_neg = pair_terms(
            query_blk, key_blk, live_blk, contrast_sample_entries, parameter_derivative
        )
        return ((running[0] + loss_sum, running[1] + grad_neg), (grad_query, pair_coeff))

    start_state = (
        jnp.zeros((), jnp.float32),
        jnp.zeros((contrast_sample_entries.shape[0], embed_width), jnp.float32),
    )
    blocks_in = (
        probe_entry_count.reshape(block_count, block_rows, embed_width),
        key_rows.reshape(block_count, block_rows, embed_width),
        usable_pair_indicator.reshape(block_count, block_rows),
    )
    (loss_local, grad_neg), (grad_query, pair_coeff) = lax.scan(one_block, start_state, blocks_in)
    grad_query = grad_query.reshape(pair_rows, embed_width)
    pair_coeff = pair_coeff.reshape(pair_rows)
    grad_embed_a = jax.ops.segment_sum(grad_query, dest_flat, num_segments=points)
    grad_sent = pair_coeff[:, None] * probe_entry_count.astype(jnp.float32)
    grad_key = (
        lax.all_to_all(
            grad_sent.reshape(group_size, slot_count, embed_width).astype(jnp.bfloat16),
            "narrow",
            split_axis=0,
            concat_axis=0,
            tiled=True,
        )
        .astype(jnp.float32)
        .reshape(pair_rows, embed_width)
    )
    grad_neg_mine = lax.psum_scatter(
        grad_neg.astype(jnp.bfloat16), "narrow", scatter_dimension=0, tiled=True
    ).astype(jnp.float32)
    grad_embed_b = jax.ops.segment_sum(
        grad_key, sent_ids, num_segments=points
    ) + jax.ops.segment_sum(grad_neg_mine, neg_ids, num_segments=points)
    wo_a, grad_norm_a = back_top(grad_embed_a, unit_a, scale_a, active_a, normed_a, w_out)
    wo_b, grad_norm_b = back_top(grad_embed_b, unit_b, scale_b, active_b, normed_b, w_out)
    sums = [
        jnp.sum(grad_norm_a, axis=0),
        jnp.sum(grad_norm_a * normed_a, axis=0),
        jnp.sum(grad_norm_b, axis=0),
        jnp.sum(grad_norm_b * normed_b, axis=0),
        jnp.full((zero.shape[1],), loss_local),
    ]
    back = small_sum(jnp.concatenate([jnp.stack(sums), zero]), 2)
    grad_sum_a, cross_sum_a, grad_sum_b, cross_sum_b = back[0], back[1], back[2], back[3]
    loss_total = back[4, 0]
    feat_grad_a, wh_a = back_bottom(
        rows_a, grad_norm_a, normed_a, inv_std_a, grad_sum_a, cross_sum_a, all_points, w_hidden
    )
    feat_grad_b, wh_b = back_bottom(
        rows_b, grad_norm_b, normed_b, inv_std_b, grad_sum_b, cross_sum_b, all_points, w_hidden
    )
    grad_wh, grad_wo = grad_sum(wh_a + wh_b, wo_a + wo_b, 3)
    loss = loss_total / pair_total
    return (
        loss,
        feat_grad_a.reshape(feat_a.shape),
        feat_grad_b.reshape(feat_b.shape),
        grad_wh,
        grad_wo,
    )


def solution(mesh):
    placed = (
        P("wide", "narrow", None, None),
        P("wide", "narrow", None, None),
        P(),
        P(),
        P("wide", "narrow", None, None),
        P("wide", "narrow", None, None),
        P("wide", "narrow", None),
        P("wide", "narrow", None),
    )
    return jax.shard_map(
        body,
        mesh=mesh,
        in_specs=placed,
        out_specs=(P(), P("wide", "narrow", None, None), P("wide", "narrow", None, None), P(), P()),
        check_vma=False,
    )
```

```python
import functools
import math

import jax
import jax.numpy as jnp
from jax import lax
from jax.experimental import pallas as pl
from jax.experimental.pallas import tpu as pltpu
from jax.sharding import PartitionSpec as P

MESH = pl.DeviceIdType.MESH
F32 = jnp.float32
BF16 = jnp.bfloat16
TEMPERATURE = 0.07
NT = (((1,), (1,)), ((), ()))
TN = (((0,), (0,)), ((), ()))


def dot(left, right, dims=None):
    if dims is None:
        return jnp.dot(left, right, preferred_element_type=F32)
    return lax.dot_general(left, right, dims, preferred_element_type=F32)


def one_hot(mask):
    return jnp.where(mask, 1.0, 0.0).astype(F32)


def fold(values):
    rows, width = values.shape
    return jnp.sum(values.reshape(rows // 8, 8, width), axis=0)


def remote(src, dst, sems, d, device):
    return pltpu.make_async_remote_copy(
        src_ref=src,
        dst_ref=dst,
        send_sem=sems.at[0, d],
        recv_sem=sems.at[1, d],
        device_id=device,
        device_id_type=MESH,
    )


def start_all(make, count):
    @pl.loop(1, count)
    def _(d):
        make(d).start()


def wait_all(make, count):
    @pl.loop(1, count)
    def _(d):
        make(d).wait()


def step_kernel(
    all_points,
    feat_a,
    feat_b,
    w_hidden,
    w_out,
    send_col,
    send_row,
    msg,
    neg_col,
    neg_row,
    loss_o,
    grad_feat_a,
    grad_feat_b,
    grad_wh_o,
    grad_wo_o,
    lin,
    normed,
    embed,
    scale,
    acc,
    stat,
    near,
    part,
    far,
    total,
    near2,
    part2,
    far2,
    total2,
    msg_in,
    dest_row,
    dest_col,
    negs,
    keys_out,
    keys_in,
    expo,
    exp_sum,
    num,
    spread,
    grad_rows,
    grad_out_slots,
    grad_in_slots,
    neg_out,
    neg_in,
    neg_mine,
    grad_norm,
    wo_acc,
    wh_acc,
    loss_acc,
    grads,
    half,
    own,
    piece,
    chunk,
    stack_in,
    merged,
    sem_msg,
    sem_near,
    sem_far,
    sem_near2,
    sem_far2,
    sem_neg,
    sem_key,
    sem_grad,
    sem_negback,
    sem_pair,
    sem_piece,
    sem_stack,
    sem_gather,
):
    w = lax.axis_index("wide")
    n = lax.axis_index("narrow")
    n_wide = far.shape[0]
    n_narrow = near.shape[0]
    n_z = stack_in.shape[0]
    points, _ = feat_a.shape
    hidden = w_hidden.shape[1]
    width = w_out.shape[1]
    cap = points // n_narrow
    neg_count = neg_col.shape[0]
    block = min(512, points)
    small = min(256, points)
    feats = (feat_a, feat_b)
    out_feats = (grad_feat_a, grad_feat_b)

    def peer(d):
        return (w, lax.rem(n + d, n_narrow))

    def across(d):
        return (lax.rem(w + d, n_wide), n)

    def rows_of(i, size):
        return pl.ds(pl.multiple_of(i * size, size), size)

    barrier = pltpu.get_barrier_semaphore()

    @pl.loop(1, n_narrow)
    def _(d):
        pl.semaphore_signal(barrier, inc=1, device_id=peer(d), device_id_type=MESH)

    @pl.loop(1, n_wide)
    def _(d):
        pl.semaphore_signal(barrier, inc=1, device_id=across(d), device_id_type=MESH)

    acc[...] = jnp.zeros_like(acc)
    for v in range(2):

        @pl.loop(0, points // block)
        def _(i):
            rows = rows_of(i, block)
            linear = dot(feats[v][rows, :], w_hidden[...])
            lin[v, rows, :] = linear
            acc[2 * v] += fold(linear)
            acc[2 * v + 1] += fold(linear * linear)

    stat[...] = jnp.zeros_like(stat)
    stat[0:4, :] = jnp.sum(acc[...], axis=1)
    stat[4:5, 0:cap] = jnp.sum(msg[:, 1, :].astype(F32), axis=0, keepdims=True)

    pl.semaphore_wait(barrier, n_narrow + n_wide - 2)

    def sum_all(near, part, far, total, sem_near, sem_far, between=None):
        def to_near(d):
            return remote(stat, near.at[n], sem_near, d, peer(d))

        def to_far(d):
            return remote(part, far.at[w], sem_far, d, across(d))

        start_all(to_near, n_narrow)
        near[n] = stat[...]
        if between is not None:
            between()
        wait_all(to_near, n_narrow)
        part[...] = jnp.sum(near[...], axis=0)
        start_all(to_far, n_wide)
        far[w] = part[...]
        wait_all(to_far, n_wide)
        total[...] = jnp.sum(far[...], axis=0)

    def to_msg(d):
        return remote(msg.at[lax.rem(n + d, n_narrow)], msg_in.at[n], sem_msg, d, peer(d))

    def send_msg():
        start_all(to_msg, n_narrow)
        msg_in[n] = msg[n]

    sum_all(near, part, far, total, sem_near, sem_far, send_msg)

    inv_count = 1.0 / all_points
    means, inverses = [], []
    for v in range(2):
        mean = total[2 * v : 2 * v + 1, :] * inv_count
        square = total[2 * v + 1 : 2 * v + 2, :] * inv_count
        means.append(mean)
        inverses.append(lax.rsqrt(square - mean * mean + 1e-5))

    def finish(v):
        @pl.loop(0, points // block)
        def _(i):
            rows = rows_of(i, block)
            value = ((lin[v, rows, :] - means[v]) * inverses[v]).astype(BF16)
            normed[v, rows, :] = value
            out = dot(jnp.maximum(value, 0), w_out[...])
            unit_scale = lax.rsqrt(jnp.sum(out * out, axis=1, keepdims=True) + 1e-6)
            embed[v, rows, :] = (out * unit_scale).astype(BF16)
            scale[v, rows, :] = unit_scale

    finish(1)
    lanes = lax.broadcasted_iota(jnp.int32, (neg_count, points), 1)
    my_negs = rows_of(n, neg_count)
    negs[my_negs, :] = dot(one_hot(neg_col[...] == lanes).astype(BF16), embed[1]).astype(BF16)

    def to_negs(d):
        return remote(negs.at[my_negs], negs.at[my_negs], sem_neg, d, peer(d))

    start_all(to_negs, n_narrow)

    batch = block // cap

    def to_key(d):
        return remote(
            keys_out.at[rows_of(lax.rem(n + d, n_narrow), cap)],
            keys_in.at[rows_of(n, cap)],
            sem_key,
            d,
            peer(d),
        )

    def gather(ids, table, i):
        lanes = lax.broadcasted_iota(jnp.int32, (cap, points), 1)
        picks = [
            one_hot(ids[rows_of(lax.rem(n + i * batch + k, n_narrow), cap), :] == lanes).astype(BF16)
            for k in range(batch)
        ]
        return dot(jnp.concatenate(picks, axis=0), table).astype(BF16)

    def permute_and_send(ids, table, out_ref, in_ref, make):
        @pl.loop(0, n_narrow // batch)
        def _(i):
            picked = gather(ids, table[...], i)
            for k in range(batch):
                d = i * batch + k
                out_ref[rows_of(lax.rem(n + d, n_narrow), cap), :] = picked[k * cap : (k + 1) * cap]

                @pl.when(d > 0)
                def _():
                    make(d).start()

        in_ref[rows_of(n, cap), :] = out_ref[rows_of(n, cap), :]

    permute_and_send(send_col, embed.at[1], keys_out, keys_in, to_key)

    finish(0)

    wait_all(to_msg, n_narrow)
    ids = msg_in[:, 0, :]
    slot = lax.broadcasted_iota(jnp.int32, ids.shape, 1)
    ids = jnp.where(slot < msg_in[:, 1, :], ids, ids + 2 * points)
    dest_row[...] = ids
    square_ids = jnp.concatenate(
        [ids.astype(F32), jnp.zeros((cap - n_narrow, cap), F32)], axis=0
    ).T.astype(jnp.int32)
    for s in range(n_narrow):
        dest_col[s * cap : (s + 1) * cap, :] = square_ids[:, s : s + 1]

    wait_all(to_negs, n_narrow)

    to_exp2 = math.log2(math.e) / TEMPERATURE

    @pl.loop(0, points // small)
    def _(i):
        rows = rows_of(i, small)
        score = dot(embed[0, rows, :], negs[...], NT)
        power = jnp.exp2(score * to_exp2)
        exp_sum[rows, :] = jnp.sum(power, axis=1, keepdims=True)
        power = power.astype(BF16)
        expo[rows, :] = power
        num[rows, :] = dot(power, negs[...])

    wait_all(to_key, n_narrow)

    pair_total = total[4:5, 0:1]
    weight = all_points / (pair_total * TEMPERATURE)
    loss_acc[...] = jnp.zeros_like(loss_acc)

    def rows_one_hot(row_ids, i, size, with_sum=False):
        place = lax.broadcasted_iota(jnp.int32, (size, cap), 0) + i * size
        picks = []
        hits = None
        for s in range(row_ids.shape[0]):
            hit = one_hot(row_ids[s : s + 1, :] == place)
            if with_sum:
                hits = hit if hits is None else hits + hit
            picks.append(hit.astype(BF16))
        picks = jnp.concatenate(picks, axis=1)
        return (picks, hits) if with_sum else picks

    @pl.loop(0, points // small)
    def _(i):
        rows = rows_of(i, small)
        picks, hits = rows_one_hot(dest_row, i, small, True)
        live = jnp.sum(hits, axis=1, keepdims=True)
        key = dot(picks, keys_in[...])
        query = embed[0, rows, :].astype(F32)
        positive = jnp.sum(query * key, axis=1, keepdims=True) * (1.0 / TEMPERATURE)
        exp_pos = jnp.exp(positive)
        denominator = exp_pos + exp_sum[rows, :]
        term = live * (jnp.log(denominator) - positive)
        loss_acc[...] += jnp.sum(term, axis=0, keepdims=True)
        share = live * weight / denominator
        pair_coeff = share * exp_pos - live * weight
        num[rows, :] = pair_coeff * key + share * num[rows, :]
        grad_rows[rows, :] = (pair_coeff * query).astype(BF16)
        spread[:, rows] = (share * query).T.astype(BF16)

    def to_slot(d):
        return remote(
            grad_out_slots.at[rows_of(lax.rem(n + d, n_narrow), cap)],
            grad_in_slots.at[rows_of(n, cap)],
            sem_grad,
            d,
            peer(d),
        )

    permute_and_send(dest_col, grad_rows, grad_out_slots, grad_in_slots, to_slot)

    def to_owner(d):
        return remote(
            neg_out.at[lax.rem(n + d, n_narrow)], neg_in.at[n], sem_negback, d, peer(d)
        )

    @pl.loop(0, n_narrow // batch)
    def _(i):
        for k in range(batch):
            d = i * batch + k
            owner = lax.rem(n + d, n_narrow)
            neg_out[owner] = dot(spread[...], expo[:, rows_of(owner, neg_count)]).T.astype(BF16)

            @pl.when(d > 0)
            def _():
                to_owner(d).start()

    neg_in[n] = neg_out[n]

    acc[...] = jnp.zeros_like(acc)
    wo_acc[...] = jnp.zeros_like(wo_acc)

    def back_top(v, grad_embed):
        @pl.loop(0, points // block)
        def _(i):
            rows = rows_of(i, block)
            grad = grad_embed(i, rows)
            unit = embed[v, rows, :].astype(F32)
            inner = jnp.sum(unit * grad, axis=1, keepdims=True)
            grad_out = (scale[v, rows, :] * (grad - unit * inner)).astype(BF16)
            value = normed[v, rows, :]
            wo_acc[...] += dot(grad_out, jnp.maximum(value, 0), TN)
            value = value.astype(F32)
            grad_act = jnp.where(value > 0, dot(grad_out, w_out[...], NT), 0.0)
            grad_norm[v, rows, :] = grad_act.astype(BF16)
            acc[2 * v] += fold(grad_act)
            acc[2 * v + 1] += fold(grad_act * value)

    back_top(0, lambda i, rows: num[rows, :])

    wait_all(to_slot, n_narrow)
    wait_all(to_owner, n_narrow)
    neg_mine[...] = jnp.sum(neg_in[...].astype(F32), axis=0).astype(BF16)

    def grad_b(i, rows):
        return dot(rows_one_hot(send_row, i, block), grad_in_slots[...]) + dot(
            rows_one_hot(neg_row, i, block), neg_mine[...]
        )

    back_top(1, grad_b)

    stat[0:4, :] = jnp.sum(acc[...], axis=1)
    stat[4:5, 0:cap] = loss_acc[0:1, :]
    sum_all(near2, part2, far2, total2, sem_near2, sem_far2)

    loss_o[...] = jnp.broadcast_to(total2[4:5, 0:cap] / pair_total, loss_o.shape)
    wh_acc[...] = jnp.zeros_like(wh_acc)
    for v in range(2):
        mean_grad = total2[2 * v : 2 * v + 1, :] * inv_count
        mean_cross = total2[2 * v + 1 : 2 * v + 2, :] * inv_count

        @pl.loop(0, points // block)
        def _(i):
            rows = rows_of(i, block)
            grad = grad_norm[v, rows, :].astype(F32)
            value = normed[v, rows, :].astype(F32)
            grad = (inverses[v] * (grad - mean_grad - value * mean_cross)).astype(BF16)
            grad_norm[v, rows, :] = grad
            wh_acc[...] += dot(feats[v][rows, :], grad, TN)

    depth = wh_acc.shape[0]
    parts = hidden // width
    for p in range(parts):
        grads[p * depth : (p + 1) * depth, :] = wh_acc[:, p * width : (p + 1) * width].astype(BF16)
    grads[parts * depth :, :] = wo_acc[...].T.astype(BF16)

    def feat_grad(v):
        @pl.loop(0, points // block)
        def _(i):
            rows = rows_of(i, block)
            out_feats[v][rows, :] = dot(grad_norm[v, rows, :], w_hidden[...], NT).astype(BF16)

    span, rows = half.shape[0], chunk.shape[0]
    z, c = w // 2, lax.rem(w, 2)
    partner = (2 * z + 1 - c, n)
    mine = pl.multiple_of(c * span, span)
    other = pl.multiple_of((1 - c) * span, span)
    swap = remote(grads.at[pl.ds(other, span)], half, sem_pair, 0, partner)
    swap.start()
    swap.wait()
    own[...] = (
        grads[pl.ds(mine, span), :].astype(F32) + half[...].astype(F32)
    ).astype(BF16)

    def to_piece(d):
        return remote(
            own.at[rows_of(lax.rem(n + d, n_narrow), rows)], piece.at[n], sem_piece, d, peer(d)
        )

    start_all(to_piece, n_narrow)
    piece[n] = own[rows_of(n, rows), :]
    feat_grad(0)
    wait_all(to_piece, n_narrow)
    chunk[...] = jnp.sum(piece[...].astype(F32), axis=0).astype(BF16)

    def to_stack(d):
        return remote(
            chunk, stack_in.at[z], sem_stack, d, (2 * lax.rem(z + d, n_z) + c, n)
        )

    start_all(to_stack, n_z)
    stack_in[z] = chunk[...]
    wait_all(to_stack, n_z)
    place = pl.ds(pl.multiple_of(mine + n * rows, rows), rows)
    merged[place, :] = jnp.sum(stack_in[...].astype(F32), axis=0).astype(BF16)

    def to_gather(d):
        return remote(merged.at[place], merged.at[place], sem_gather, d, peer(d))

    start_all(to_gather, n_narrow)
    feat_grad(1)
    wait_all(to_gather, n_narrow)
    swap = remote(merged.at[pl.ds(mine, span)], merged.at[pl.ds(mine, span)], sem_pair, 1, partner)
    swap.start()
    swap.wait()
    for p in range(parts):
        grad_wh_o[:, p * width : (p + 1) * width] = merged[
            p * depth : (p + 1) * depth, :
        ].astype(F32)
    grad_wo_o[...] = merged[parts * depth :, :].astype(F32)


def body(feat_a, feat_b, w_hidden, w_out, send_rows, dest_rows, counts, neg_rows):
    points, depth = feat_a.shape[2:]
    hidden, width = w_out.shape
    n_wide, n_narrow = lax.axis_size("wide"), lax.axis_size("narrow")
    n_z = n_wide // 2
    cap = send_rows.shape[3]
    neg_count = neg_rows.shape[2]
    total_negs = n_narrow * neg_count
    all_points = float(n_wide * n_narrow * points)
    send_row = send_rows.reshape(n_narrow, cap)
    dests = dest_rows.reshape(n_narrow, 1, cap)
    count = jnp.broadcast_to(counts.reshape(n_narrow, 1, 1), (n_narrow, 7, cap))
    msg = jnp.concatenate([dests, count], axis=1)
    stat = (8, hidden)
    grad_total = depth * hidden // width + hidden
    span = grad_total // 2
    rows = span // n_narrow
    vmem = pl.BlockSpec(memory_space=pltpu.VMEM)
    dma = pltpu.SemaphoreType.DMA
    out_shape = (
        jax.ShapeDtypeStruct((8, cap), F32),
        jax.ShapeDtypeStruct((points, depth), BF16),
        jax.ShapeDtypeStruct((points, depth), BF16),
        jax.ShapeDtypeStruct((depth, hidden), F32),
        jax.ShapeDtypeStruct((hidden, width), F32),
    )
    scratch = [
        pltpu.VMEM((2, points, hidden), F32),
        pltpu.VMEM((2, points, hidden), BF16),
        pltpu.VMEM((2, points, width), BF16),
        pltpu.VMEM((2, points, 1), F32),
        pltpu.VMEM((4, 8, hidden), F32),
        pltpu.VMEM(stat, F32),
        pltpu.VMEM((n_narrow,) + stat, F32),
        pltpu.VMEM(stat, F32),
        pltpu.VMEM((n_wide,) + stat, F32),
        pltpu.VMEM(stat, F32),
        pltpu.VMEM((n_narrow,) + stat, F32),
        pltpu.VMEM(stat, F32),
        pltpu.VMEM((n_wide,) + stat, F32),
        pltpu.VMEM(stat, F32),
        pltpu.VMEM((n_narrow, 8, cap), jnp.int32),
        pltpu.VMEM((n_narrow, cap), jnp.int32),
        pltpu.VMEM((points, 1), jnp.int32),
        pltpu.VMEM((total_negs, width), BF16),
        pltpu.VMEM((points, width), BF16),
        pltpu.VMEM((points, width), BF16),
        pltpu.VMEM((points, total_negs), BF16),
        pltpu.VMEM((points, 1), F32),
        pltpu.VMEM((points, width), F32),
        pltpu.VMEM((width, points), BF16),
        pltpu.VMEM((points, width), BF16),
        pltpu.VMEM((points, width), BF16),
        pltpu.VMEM((points, width), BF16),
        pltpu.VMEM((n_narrow, neg_count, width), BF16),
        pltpu.VMEM((n_narrow, neg_count, width), BF16),
        pltpu.VMEM((neg_count, width), BF16),
        pltpu.VMEM((2, points, hidden), BF16),
        pltpu.VMEM((width, hidden), F32),
        pltpu.VMEM((depth, hidden), F32),
        pltpu.VMEM((8, cap), F32),
        pltpu.VMEM((grad_total, width), BF16),
        pltpu.VMEM((span, width), BF16),
        pltpu.VMEM((span, width), BF16),
        pltpu.VMEM((n_narrow, rows, width), BF16),
        pltpu.VMEM((rows, width), BF16),
        pltpu.VMEM((n_z, rows, width), BF16),
        pltpu.VMEM((grad_total, width), BF16),
        dma((2, n_narrow)),
        dma((2, n_narrow)),
        dma((2, n_wide)),
        dma((2, n_narrow)),
        dma((2, n_wide)),
        dma((2, n_narrow)),
        dma((2, n_narrow)),
        dma((2, n_narrow)),
        dma((2, n_narrow)),
        dma((2, 2)),
        dma((2, n_narrow)),
        dma((2, n_z)),
        dma((2, n_narrow)),
    ]
    loss, grad_a, grad_b, grad_wh, grad_wo = pl.pallas_call(
        functools.partial(step_kernel, all_points),
        out_shape=out_shape,
        in_specs=[vmem] * 9,
        out_specs=(vmem,) * 5,
        scratch_shapes=scratch,
        compiler_params=pltpu.CompilerParams(
            collective_id=1, has_side_effects=True, vmem_limit_bytes=63 * 1024 * 1024
        ),
        name="step",
    )(
        feat_a.reshape(points, depth),
        feat_b.reshape(points, depth),
        w_hidden,
        w_out,
        send_row.reshape(points, 1),
        send_row,
        msg,
        neg_rows.reshape(neg_count, 1),
        neg_rows.reshape(1, neg_count),
    )
    return (
        loss[0, 0],
        grad_a.reshape(feat_a.shape),
        grad_b.reshape(feat_b.shape),
        grad_wh,
        grad_wo,
    )


def solution(mesh):
    placed = (
        P("wide", "narrow", None, None),
        P("wide", "narrow", None, None),
        P(),
        P(),
        P("wide", "narrow", None, None),
        P("wide", "narrow", None, None),
        P("wide", "narrow", None),
        P("wide", "narrow", None),
    )
    return jax.shard_map(
        body,
        mesh=mesh,
        in_specs=placed,
        out_specs=(P(), P("wide", "narrow", None, None), P("wide", "narrow", None, None), P(), P()),
        check_vma=False,
    )
```

```python
import functools
import math

import jax
import jax.numpy as jnp
from jax import lax
from jax.experimental import pallas as pl
from jax.experimental.pallas import tpu as pltpu
from jax.sharding import PartitionSpec as P

MESH = pl.DeviceIdType.MESH
F32 = jnp.float32
BF16 = jnp.bfloat16
TEMPERATURE = 0.07
NT = (((1,), (1,)), ((), ()))
TN = (((0,), (0,)), ((), ()))


def dot(left, right, dims=None):
    if dims is None:
        return jnp.dot(left, right, preferred_element_type=F32)
    return lax.dot_general(left, right, dims, preferred_element_type=F32)


def one_hot(mask):
    return jnp.where(mask, 1.0, 0.0).astype(F32)


def fold(values):
    rows, width = values.shape
    return jnp.sum(values.reshape(rows // 8, 8, width), axis=0)


def remote(src, dst, sems, d, device):
    return pltpu.make_async_remote_copy(
        src_ref=src,
        dst_ref=dst,
        send_sem=sems.at[0, d],
        recv_sem=sems.at[1, d],
        device_id=device,
        device_id_type=MESH,
    )


def start_all(make, count):
    @pl.loop(1, count)
    def _(d):
        make(d).start()


def wait_all(make, count):
    @pl.loop(1, count)
    def _(d):
        make(d).wait()


def wait_sent(make, count):
    @pl.loop(1, count)
    def _(d):
        make(d).wait_send()


def step_kernel(
    all_points,
    feat_a,
    feat_b,
    w_hidden,
    w_out,
    send_row,
    dest_own,
    counts,
    neg_row,
    loss_o,
    grad_feat_a,
    grad_feat_b,
    grads_o,
    feat,
    feat_slot,
    lin,
    normed,
    embed,
    scale,
    acc,
    feat_acc,
    stat,
    near,
    part,
    far,
    total,
    stat2,
    near2,
    part2,
    far2,
    total2,
    msg,
    msg_in,
    send_col,
    dest_row,
    dest_col,
    live_col,
    query,
    negs,
    keys_in,
    expo,
    exp_sum,
    num,
    spread,
    grad_query,
    grad_out_slots,
    grad_in_slots,
    neg_out,
    neg_in,
    neg_mine,
    grad_norm,
    wo_acc,
    wh_one,
    wh_two,
    loss_acc,
    grads,
    half,
    own,
    piece,
    chunk,
    stack_in,
    sem_in,
    sem_out,
    sem_msg,
    sem_near,
    sem_far,
    sem_near2,
    sem_far2,
    sem_neg,
    sem_key,
    sem_grad,
    sem_negback,
    sem_pair,
    sem_piece,
    sem_stack,
    sem_gather,
):
    w = lax.axis_index("wide")
    n = lax.axis_index("narrow")
    n_wide = far.shape[0]
    n_narrow = near.shape[0]
    n_z = stack_in.shape[0]
    points, depth = feat_a.shape
    hidden = w_hidden.shape[1]
    width = w_out.shape[1]
    cap = points // n_narrow
    neg_count = neg_row.shape[1]
    block = min(512, points)
    small = min(256, points)
    blocks = points // block
    split = hidden // 2

    def peer(d):
        return (w, lax.rem(n + d, n_narrow))

    def source(d):
        return lax.rem(n + n_narrow - d, n_narrow)

    def across(d):
        return (lax.rem(w + d, n_wide), n)

    def rows_of(i, size):
        return pl.ds(pl.multiple_of(i * size, size), size)

    barrier = pltpu.get_barrier_semaphore()

    @pl.loop(1, n_narrow)
    def _(d):
        pl.semaphore_signal(barrier, inc=1, device_id=peer(d), device_id_type=MESH)

    @pl.loop(1, n_wide)
    def _(d):
        pl.semaphore_signal(barrier, inc=1, device_id=across(d), device_id_type=MESH)

    def load(v, i):
        ref = (feat_a, feat_b)[v]
        rows = rows_of(i, block)
        return pltpu.make_async_copy(ref.at[rows], feat.at[v, rows], sem_in.at[v, i])

    for v in (1, 0):
        for i in range(blocks):
            load(v, i).start()

    acc[...] = jnp.zeros_like(acc)
    feat_acc[...] = jnp.zeros_like(feat_acc)
    for v in (1, 0):

        @pl.loop(0, blocks)
        def _(i):
            load(v, i).wait()
            rows = rows_of(i, block)
            points_in = feat[v, rows, :]
            linear = dot(points_in, w_hidden[...])
            acc[2 * v] += fold(linear)
            acc[2 * v + 1] += fold(linear * linear)
            feat_acc[v] += fold(points_in.astype(F32))

    def put_sums(stat, sums):
        for r in range(4):
            stat[2 * r : 2 * r + 1, 0:split] = sums[r : r + 1, 0:split]
            stat[2 * r + 1 : 2 * r + 2, 0:split] = sums[r : r + 1, split:]

    def get_sum(total, r):
        return jnp.concatenate(
            [total[2 * r : 2 * r + 1, 0:split], total[2 * r + 1 : 2 * r + 2, 0:split]], axis=1
        )

    put_sums(stat, jnp.sum(acc[...], axis=1))

    pl.semaphore_wait(barrier, n_narrow + n_wide - 2)

    def sum_all(stat, near, part, far, total, sem_near, sem_far, between=None, later=None):
        def to_near(d):
            return remote(stat, near.at[n], sem_near, d, peer(d))

        def to_far(d):
            return remote(part, far.at[w], sem_far, d, across(d))

        start_all(to_near, n_narrow)
        near[n] = stat[...]
        if between is not None:
            between()
        wait_all(to_near, n_narrow)
        part[...] = jnp.sum(near[...], axis=0)
        start_all(to_far, n_wide)
        far[w] = part[...]
        if later is not None:
            later()
        wait_all(to_far, n_wide)
        total[...] = jnp.sum(far[...], axis=0)

    def to_msg(d):
        return remote(msg.at[lax.rem(n + d, n_narrow)], msg_in.at[n], sem_msg, d, peer(d))

    def gather(ids, table, i):
        lanes = lax.broadcasted_iota(jnp.int32, (block, points), 1)
        return dot(one_hot(ids[rows_of(i, block), :] == lanes).astype(BF16), table)

    def columns(ids, ref):
        square = jnp.concatenate(
            [ids.astype(F32), jnp.zeros((cap - n_narrow, cap), F32)], axis=0
        ).T.astype(jnp.int32)
        for s in range(n_narrow):
            ref[s * cap : (s + 1) * cap, :] = square[:, s : s + 1]

    def spread_counts():
        across_lanes = lax.broadcasted_iota(jnp.int32, (n_narrow, n_narrow), 1)
        down = lax.broadcasted_iota(jnp.int32, (n_narrow, n_narrow), 0)
        here = jnp.broadcast_to(counts[...], (n_narrow, n_narrow)).astype(F32)
        return jnp.sum(jnp.where(across_lanes == down, here, 0.0), axis=1, keepdims=True)

    def slot_order():
        count = spread_counts().astype(jnp.int32)
        line = lax.broadcasted_iota(jnp.int32, (8, cap), 0)
        for s in range(n_narrow):
            msg[s] = jnp.where(line == 0, dest_own[s : s + 1, :], count[s : s + 1, :])
        start_all(to_msg, n_narrow)
        msg_in[n] = msg[n]
        columns(send_row[...], send_col)

        @pl.loop(0, blocks)
        def _(i):
            feat_slot[rows_of(i, block), :] = gather(send_col, feat[1], i).astype(BF16)

    def slot_linear():
        @pl.loop(0, blocks)
        def _(i):
            rows = rows_of(i, block)
            lin[rows, :] = dot(feat_slot[rows, :], w_hidden[...])

        wait_all(to_msg, n_narrow)
        ids = msg_in[:, 0, :]
        dest_row[...] = ids
        columns(ids, dest_col)
        line = lax.broadcasted_iota(jnp.int32, (cap, 1), 0)
        for s in range(n_narrow):
            live_col[s * cap : (s + 1) * cap, :] = one_hot(line < msg_in[s, 1:2, 0:1])

    sum_all(stat, near, part, far, total, sem_near, sem_far, slot_order, slot_linear)

    inv_count = 1.0 / all_points
    means, inverses = [], []
    for v in range(2):
        mean = get_sum(total, 2 * v) * inv_count
        square = get_sum(total, 2 * v + 1) * inv_count
        means.append(mean)
        inverses.append(lax.rsqrt(square - mean * mean + 1e-5))

    def finish(v):
        @pl.loop(0, blocks)
        def _(i):
            rows = rows_of(i, block)
            linear = lin[rows, :] if v else dot(feat[0, rows, :], w_hidden[...])
            value = ((linear - means[v]) * inverses[v]).astype(BF16)
            normed[v, rows, :] = value
            out = dot(jnp.maximum(value, 0), w_out[...])
            unit_scale = lax.rsqrt(jnp.sum(out * out, axis=1, keepdims=True) + 1e-6)
            embed[v, rows, :] = (out * unit_scale).astype(BF16)
            scale[v, rows, :] = unit_scale

    finish(1)
    neg_col = jnp.broadcast_to(neg_row[...].astype(F32), (cap, neg_count)).T.astype(jnp.int32)
    my_negs = rows_of(n, neg_count)
    picks = [
        one_hot(send_row[s : s + 1, :] == neg_col).astype(BF16) for s in range(n_narrow)
    ]
    negs[my_negs, :] = dot(jnp.concatenate(picks, axis=1), embed[1]).astype(BF16)

    def to_negs(d):
        return remote(negs.at[my_negs], negs.at[my_negs], sem_neg, d, peer(d))

    start_all(to_negs, n_narrow)

    def to_key(d):
        return remote(
            embed.at[1, rows_of(lax.rem(n + d, n_narrow), cap)],
            keys_in.at[rows_of(n, cap)],
            sem_key,
            d,
            peer(d),
        )

    start_all(to_key, n_narrow)
    keys_in[rows_of(n, cap), :] = embed[1, rows_of(n, cap), :]

    finish(0)

    @pl.loop(0, blocks)
    def _(i):
        query[rows_of(i, block), :] = gather(dest_col, embed[0], i).astype(BF16)

    wait_all(to_negs, n_narrow)

    to_exp2 = math.log2(math.e) / TEMPERATURE

    @pl.loop(0, points // small)
    def _(i):
        rows = rows_of(i, small)
        score = dot(query[rows, :], negs[...], NT)
        power = jnp.exp2(score * to_exp2)
        exp_sum[rows, :] = jnp.sum(power, axis=1, keepdims=True)
        power = power.astype(BF16)
        expo[rows, :] = power
        num[rows, :] = dot(power, negs[...])

    wh_two[...] = jnp.zeros_like(wh_two)
    wh_one[...] = jnp.zeros_like(wh_one)

    def view_rows(v, rows):
        return feat_slot[rows, :] if v else feat[0, rows, :]

    for v in range(2):

        @pl.loop(0, blocks)
        def _(i):
            rows = rows_of(i, block)
            wh_two[v] += dot(view_rows(v, rows), normed[v, rows, :], TN)

    loss_acc[...] = jnp.zeros_like(loss_acc)

    def to_slot(d):
        rows = rows_of(source(d), cap)
        return remote(
            grad_out_slots.at[rows],
            grad_in_slots.at[rows_of(n, cap)],
            sem_grad,
            d,
            (w, source(d)),
        )

    @pl.loop(0, n_narrow)
    def _(d):
        @pl.when(d > 0)
        def _():
            to_key(d).wait_recv()

        rows = rows_of(source(d), cap)
        live = live_col[rows, :]
        key = keys_in[rows, :].astype(F32)
        asked = query[rows, :].astype(F32)
        positive = jnp.sum(asked * key, axis=1, keepdims=True) * (1.0 / TEMPERATURE)
        exp_pos = jnp.exp(positive)
        denominator = exp_pos + exp_sum[rows, :]
        term = live * (jnp.log(denominator) - positive)
        loss_acc[...] += jnp.sum(term, axis=0, keepdims=True)
        weight = live * (1.0 / TEMPERATURE)
        share = weight / denominator
        pair_coeff = share * exp_pos - weight
        grad_out_slots[rows, :] = (pair_coeff * asked).astype(BF16)

        @pl.when(d > 0)
        def _():
            to_slot(d).start()

        grad_query[rows, :] = (pair_coeff * key + share * num[rows, :]).astype(BF16)
        spread[:, rows] = (share * asked).T.astype(BF16)

    grad_in_slots[rows_of(n, cap), :] = grad_out_slots[rows_of(n, cap), :]

    def to_owner(d):
        return remote(
            neg_out.at[rows_of(lax.rem(n + d, n_narrow), neg_count)],
            neg_in.at[n],
            sem_negback,
            d,
            peer(d),
        )

    batch = min(4, n_narrow)
    batches = n_narrow // batch

    @pl.loop(0, batches)
    def _(i):
        q = lax.rem(n // batch + i, batches)
        cols = rows_of(q, batch * neg_count)
        neg_out[cols, :] = dot(spread[...], expo[:, cols]).T.astype(BF16)
        for k in range(batch):
            d = lax.rem(q * batch + k - n + n_narrow, n_narrow)

            @pl.when(d > 0)
            def _():
                to_owner(d).start()

    neg_in[n] = neg_out[rows_of(n, neg_count), :]

    def rows_one_hot(row_ids, i, size):
        place = lax.broadcasted_iota(jnp.int32, (size, cap), 0) + i * size
        picks = [
            one_hot(row_ids[s : s + 1, :] == place).astype(BF16) for s in range(n_narrow)
        ]
        return jnp.concatenate(picks, axis=1)

    acc[...] = jnp.zeros_like(acc)
    wo_acc[...] = jnp.zeros_like(wo_acc)

    def back_top(v, grad_embed):
        @pl.loop(0, blocks)
        def _(i):
            rows = rows_of(i, block)
            grad = grad_embed(i, rows)
            unit = embed[v, rows, :].astype(F32)
            inner = jnp.sum(unit * grad, axis=1, keepdims=True)
            grad_out = (scale[v, rows, :] * (grad - unit * inner)).astype(BF16)
            value = normed[v, rows, :]
            wo_acc[...] += dot(grad_out, jnp.maximum(value, 0), TN)
            value = value.astype(F32)
            grad_act = jnp.where(value > 0, dot(grad_out, w_out[...], NT), 0.0)
            acc[2 * v] += fold(grad_act)
            acc[2 * v + 1] += fold(grad_act * value)
            grad_norm[v, rows, :] = grad_act.astype(BF16)

    def first_product(v):
        @pl.loop(0, blocks)
        def _(i):
            rows = rows_of(i, block)
            wh_one[v] += dot(view_rows(v, rows), grad_norm[v, rows, :], TN)

    back_top(0, lambda i, rows: dot(rows_one_hot(dest_row, i, block), grad_query[...]))
    first_product(0)

    wait_sent(to_key, n_narrow)
    wait_all(to_slot, n_narrow)
    wait_all(to_owner, n_narrow)
    neg_mine[...] = jnp.sum(neg_in[...].astype(F32), axis=0).astype(BF16)

    def grad_b(i, rows):
        mask = one_hot(send_col[rows, :] == neg_row[...]).astype(BF16)
        return grad_in_slots[rows, :].astype(F32) + dot(mask, neg_mine[...])

    back_top(1, grad_b)

    put_sums(stat2, jnp.sum(acc[...], axis=1))
    stat2[0:1, split:] = loss_acc[0:1, :]
    stat2[1:8, split:] = jnp.broadcast_to(
        jnp.sum(spread_counts(), axis=0, keepdims=True), (7, cap)
    )
    sum_all(
        stat2,
        near2,
        part2,
        far2,
        total2,
        sem_near2,
        sem_far2,
        lambda: first_product(1),
    )

    pair_total = total2[1:2, split : split + 1]
    grad_weight = all_points / pair_total
    loss_o[...] = jnp.broadcast_to(total2[0:1, split:] / pair_total, loss_o.shape)
    mean_grads = [get_sum(total2, 2 * v) * inv_count for v in range(2)]
    mean_crosses = [get_sum(total2, 2 * v + 1) * inv_count for v in range(2)]
    scales = [inverses[v] * grad_weight for v in range(2)]
    parts = hidden // width
    totals = [jnp.sum(feat_acc[v], axis=0, keepdims=True) for v in range(2)]
    downs = [jnp.broadcast_to(row, (8, depth)).T[:, 0:1] for row in totals]
    for p in range(parts):
        cols = slice(p * width, (p + 1) * width)
        value = sum(
            scales[v][:, cols]
            * (
                wh_one[v, :, cols]
                - downs[v] * mean_grads[v][:, cols]
                - wh_two[v, :, cols] * mean_crosses[v][:, cols]
            )
            for v in range(2)
        )
        grads[p * depth : (p + 1) * depth, :] = value.astype(BF16)
    grads[parts * depth :, :] = (wo_acc[...].T * grad_weight).astype(BF16)

    def store(v, i):
        ref = (grad_feat_a, grad_feat_b)[v]
        rows = rows_of(i, block)
        return pltpu.make_async_copy(normed.at[v, rows], ref.at[rows], sem_out.at[v, i])

    def feat_grad(v):
        @pl.loop(0, blocks)
        def _(i):
            rows = rows_of(i, block)
            grad = grad_norm[v, rows, :].astype(F32)
            value = normed[v, rows, :].astype(F32)
            grad = scales[v] * (grad - mean_grads[v] - value * mean_crosses[v])
            out = dot(grad.astype(BF16), w_hidden[...], NT).astype(BF16)
            if v:
                feat_slot[rows, :] = out
            else:
                normed[v, rows, :] = out
                store(v, i).start()

    def row_order():
        @pl.loop(0, blocks)
        def _(i):
            picks = rows_one_hot(send_row, i, block)
            normed[1, rows_of(i, block), :] = dot(picks, feat_slot[...]).astype(BF16)
            store(1, i).start()

    span, rows = half.shape[0], chunk.shape[0]
    z, c = w // 2, lax.rem(w, 2)
    partner = (2 * z + 1 - c, n)
    mine = pl.multiple_of(c * span, span)
    other = pl.multiple_of((1 - c) * span, span)
    swap = remote(grads.at[pl.ds(other, span)], half, sem_pair, 0, partner)
    swap.start()
    swap.wait()
    own[...] = (
        grads[pl.ds(mine, span), :].astype(F32) + half[...].astype(F32)
    ).astype(BF16)

    def to_piece(d):
        return remote(
            own.at[rows_of(lax.rem(n + d, n_narrow), rows)], piece.at[n], sem_piece, d, peer(d)
        )

    start_all(to_piece, n_narrow)
    piece[n] = own[rows_of(n, rows), :]
    feat_grad(0)
    wait_all(to_piece, n_narrow)
    chunk[...] = jnp.sum(piece[...].astype(F32), axis=0).astype(BF16)

    def to_stack(d):
        return remote(
            chunk, stack_in.at[z], sem_stack, d, (2 * lax.rem(z + d, n_z) + c, n)
        )

    start_all(to_stack, n_z)
    stack_in[z] = chunk[...]
    feat_grad(1)
    wait_all(to_stack, n_z)
    place = pl.ds(pl.multiple_of(mine + n * rows, rows), rows)
    grads_o[place, :] = jnp.sum(stack_in[...].astype(F32), axis=0).astype(BF16)

    def to_gather(d):
        return remote(grads_o.at[place], grads_o.at[place], sem_gather, d, peer(d))

    start_all(to_gather, n_narrow)
    row_order()
    wait_all(to_gather, n_narrow)
    swap = remote(
        grads_o.at[pl.ds(mine, span)], grads_o.at[pl.ds(mine, span)], sem_pair, 1, partner
    )
    swap.start()
    for v in range(2):
        for i in range(blocks):
            store(v, i).wait()
    swap.wait()


def deliver_kernel(loss, grad_a, grad_b, grads, loss_o, out_a, out_b, out_wh, out_wo, sems):
    pieces = sems.shape[1]
    rows = grad_a.shape[0] // pieces
    copies = [
        pltpu.make_async_copy(
            src.at[pl.ds(i * rows, rows)], dst.at[pl.ds(i * rows, rows)], sems.at[v, i]
        )
        for v, (src, dst) in enumerate(((grad_a, out_a), (grad_b, out_b)))
        for i in range(pieces)
    ]
    for copy in copies:
        copy.start()
    depth, hidden = out_wh.shape
    width = out_wo.shape[1]
    for p in range(hidden // width):
        out_wh[:, p * width : (p + 1) * width] = grads[p * depth : (p + 1) * depth, :].astype(F32)
    out_wo[...] = grads[hidden // width * depth :, :].astype(F32)
    loss_o[...] = loss[0:1, 0:1]
    for copy in copies:
        copy.wait()


def body(feat_a, feat_b, w_hidden, w_out, send_rows, dest_rows, counts, neg_rows):
    points, depth = feat_a.shape[2:]
    hidden, width = w_out.shape
    n_wide, n_narrow = lax.axis_size("wide"), lax.axis_size("narrow")
    n_z = n_wide // 2
    cap = send_rows.shape[3]
    neg_count = neg_rows.shape[2]
    total_negs = n_narrow * neg_count
    all_points = float(n_wide * n_narrow * points)
    blocks = points // min(512, points)
    stat = (8, hidden // 2)
    stat2 = (8, hidden // 2 + cap)
    grad_total = depth * hidden // width + hidden
    span = grad_total // 2
    rows = span // n_narrow
    vmem = pl.BlockSpec(memory_space=pltpu.VMEM)
    anywhere = pl.BlockSpec(memory_space=pl.ANY)
    dma = pltpu.SemaphoreType.DMA
    out_shape = (
        jax.ShapeDtypeStruct((8, cap), F32),
        jax.ShapeDtypeStruct((points, depth), BF16),
        jax.ShapeDtypeStruct((points, depth), BF16),
        jax.ShapeDtypeStruct((grad_total, width), BF16),
    )
    scratch = [
        pltpu.VMEM((2, points, depth), BF16),
        pltpu.VMEM((points, depth), BF16),
        pltpu.VMEM((points, hidden), F32),
        pltpu.VMEM((2, points, hidden), BF16),
        pltpu.VMEM((2, points, width), BF16),
        pltpu.VMEM((2, points, 1), F32),
        pltpu.VMEM((4, 8, hidden), F32),
        pltpu.VMEM((2, 8, depth), F32),
        pltpu.VMEM(stat, F32),
        pltpu.VMEM((n_narrow,) + stat, F32),
        pltpu.VMEM(stat, F32),
        pltpu.VMEM((n_wide,) + stat, F32),
        pltpu.VMEM(stat, F32),
        pltpu.VMEM(stat2, F32),
        pltpu.VMEM((n_narrow,) + stat2, F32),
        pltpu.VMEM(stat2, F32),
        pltpu.VMEM((n_wide,) + stat2, F32),
        pltpu.VMEM(stat2, F32),
        pltpu.VMEM((n_narrow, 8, cap), jnp.int32),
        pltpu.VMEM((n_narrow, 8, cap), jnp.int32),
        pltpu.VMEM((points, 1), jnp.int32),
        pltpu.VMEM((n_narrow, cap), jnp.int32),
        pltpu.VMEM((points, 1), jnp.int32),
        pltpu.VMEM((points, 1), F32),
        pltpu.VMEM((points, width), BF16),
        pltpu.VMEM((total_negs, width), BF16),
        pltpu.VMEM((points, width), BF16),
        pltpu.VMEM((points, total_negs), BF16),
        pltpu.VMEM((points, 1), F32),
        pltpu.VMEM((points, width), F32),
        pltpu.VMEM((width, points), BF16),
        pltpu.VMEM((points, width), BF16),
        pltpu.VMEM((points, width), BF16),
        pltpu.VMEM((points, width), BF16),
        pltpu.VMEM((total_negs, width), BF16),
        pltpu.VMEM((n_narrow, neg_count, width), BF16),
        pltpu.VMEM((neg_count, width), BF16),
        pltpu.VMEM((2, points, hidden), BF16),
        pltpu.VMEM((width, hidden), F32),
        pltpu.VMEM((2, depth, hidden), F32),
        pltpu.VMEM((2, depth, hidden), F32),
        pltpu.VMEM((8, cap), F32),
        pltpu.VMEM((grad_total, width), BF16),
        pltpu.VMEM((span, width), BF16),
        pltpu.VMEM((span, width), BF16),
        pltpu.VMEM((n_narrow, rows, width), BF16),
        pltpu.VMEM((rows, width), BF16),
        pltpu.VMEM((n_z, rows, width), BF16),
        dma((2, blocks)),
        dma((2, blocks)),
        dma((2, n_narrow)),
        dma((2, n_narrow)),
        dma((2, n_wide)),
        dma((2, n_narrow)),
        dma((2, n_wide)),
        dma((2, n_narrow)),
        dma((2, n_narrow)),
        dma((2, n_narrow)),
        dma((2, n_narrow)),
        dma((2, 2)),
        dma((2, n_narrow)),
        dma((2, n_z)),
        dma((2, n_narrow)),
    ]
    loss, grad_a, grad_b, grads = pl.pallas_call(
        functools.partial(step_kernel, all_points),
        out_shape=out_shape,
        in_specs=[anywhere] * 2 + [vmem] * 6,
        out_specs=(vmem, anywhere, anywhere, vmem),
        scratch_shapes=scratch,
        compiler_params=pltpu.CompilerParams(
            collective_id=1, has_side_effects=True, vmem_limit_bytes=63 * 1024 * 1024
        ),
        name="step",
    )(
        feat_a.reshape(points, depth),
        feat_b.reshape(points, depth),
        w_hidden,
        w_out,
        send_rows.reshape(n_narrow, cap),
        dest_rows.reshape(n_narrow, cap),
        counts.reshape(1, n_narrow),
        neg_rows.reshape(1, neg_count),
    )
    loss, grad_a, grad_b, grad_wh, grad_wo = pl.pallas_call(
        deliver_kernel,
        out_shape=(
            jax.ShapeDtypeStruct((1, 1), F32),
            jax.ShapeDtypeStruct((points, depth), BF16),
            jax.ShapeDtypeStruct((points, depth), BF16),
            jax.ShapeDtypeStruct((depth, hidden), F32),
            jax.ShapeDtypeStruct((hidden, width), F32),
        ),
        in_specs=[vmem, anywhere, anywhere, vmem],
        out_specs=(vmem, anywhere, anywhere, vmem, vmem),
        scratch_shapes=[dma((2, 4))],
        compiler_params=pltpu.CompilerParams(vmem_limit_bytes=16 * 1024 * 1024),
        name="deliver",
    )(loss, grad_a, grad_b, grads)
    return (
        loss.reshape(()),
        grad_a.reshape(feat_a.shape),
        grad_b.reshape(feat_b.shape),
        grad_wh,
        grad_wo,
    )


def solution(mesh):
    placed = (
        P("wide", "narrow", None, None),
        P("wide", "narrow", None, None),
        P(),
        P(),
        P("wide", "narrow", None, None),
        P("wide", "narrow", None, None),
        P("wide", "narrow", None),
        P("wide", "narrow", None),
    )
    return jax.shard_map(
        body,
        mesh=mesh,
        in_specs=placed,
        out_specs=(P(), P("wide", "narrow", None, None), P("wide", "narrow", None, None), P(), P()),
        check_vma=False,
    )
```

```python
import functools
import math

import jax
import jax.numpy as jnp
from jax import lax
from jax.experimental import pallas as pl
from jax.experimental.pallas import tpu as pltpu
from jax.sharding import PartitionSpec as P

MESH = pl.DeviceIdType.MESH
F32 = jnp.float32
BF16 = jnp.bfloat16
TEMPERATURE = 0.07
NT = (((1,), (1,)), ((), ()))
TN = (((0,), (0,)), ((), ()))


def dot(left, right, dims=None):
    if dims is None:
        return jnp.dot(left, right, preferred_element_type=F32)
    return lax.dot_general(left, right, dims, preferred_element_type=F32)


def one_hot(mask):
    return jnp.where(mask, 1.0, 0.0).astype(F32)


def fold(values):
    rows, width = values.shape
    return jnp.sum(values.reshape(rows // 8, 8, width), axis=0)


def remote(src, dst, sems, d, device):
    return pltpu.make_async_remote_copy(
        src_ref=src,
        dst_ref=dst,
        send_sem=sems.at[0, d],
        recv_sem=sems.at[1, d],
        device_id=device,
        device_id_type=MESH,
    )


def start_all(make, count):
    @pl.loop(1, count)
    def _(d):
        make(d).start()


def wait_all(make, count):
    @pl.loop(1, count)
    def _(d):
        make(d).wait()


def wait_sent(make, count):
    @pl.loop(1, count)
    def _(d):
        make(d).wait_send()


def step_kernel(
    all_points,
    feat_a,
    feat_b,
    w_hidden,
    w_out,
    send_row,
    dest_own,
    counts,
    neg_row,
    loss_o,
    grad_feat_a,
    grad_feat_b,
    grads_o,
    feat,
    feat_slot,
    lin,
    normed,
    embed,
    scale,
    acc,
    feat_acc,
    stat,
    near,
    part,
    far,
    total,
    stat2,
    near2,
    part2,
    far2,
    total2,
    msg,
    msg_in,
    send_col,
    dest_row,
    dest_col,
    live_col,
    query,
    negs,
    keys_in,
    expo,
    exp_sum,
    num,
    spread,
    grad_query,
    grad_out_slots,
    grad_in_slots,
    neg_out,
    low_in,
    high_in,
    low_mid,
    high_mid,
    low_end,
    high_end,
    neg_mine,
    grad_norm,
    wo_acc,
    wh_one,
    wh_two,
    loss_acc,
    grads,
    half,
    own,
    piece,
    chunk,
    stack_in,
    sem_in,
    sem_out,
    sem_msg,
    sem_near,
    sem_far,
    sem_near2,
    sem_far2,
    sem_neg,
    sem_key,
    sem_grad,
    sem_negback,
    sem_pair,
    sem_piece,
    sem_stack,
    sem_gather,
):
    w = lax.axis_index("wide")
    n = lax.axis_index("narrow")
    n_wide = far.shape[0]
    n_narrow = near.shape[0]
    n_z = stack_in.shape[0]
    points, depth = feat_a.shape
    hidden = w_hidden.shape[1]
    width = w_out.shape[1]
    cap = points // n_narrow
    neg_count = neg_row.shape[1]
    block = min(512, points)
    small = min(256, points)
    blocks = points // block
    split = hidden // 2
    side = negs.shape[0]
    upper = neg_count // 2
    row, col = n // side, lax.rem(n, side)
    halves = (slice(0, upper), slice(upper, neg_count))

    def peer(d):
        return (w, lax.rem(n + d, n_narrow))

    def along_row(d):
        return (w, row * side + lax.rem(col + d, side))

    def along_col(d):
        return (w, lax.rem(row + d, side) * side + col)

    def source(d):
        return lax.rem(n + n_narrow - d, n_narrow)

    def across(d):
        return (lax.rem(w + d, n_wide), n)

    def rows_of(i, size):
        return pl.ds(pl.multiple_of(i * size, size), size)

    barrier = pltpu.get_barrier_semaphore()

    @pl.loop(1, n_narrow)
    def _(d):
        pl.semaphore_signal(barrier, inc=1, device_id=peer(d), device_id_type=MESH)

    @pl.loop(1, n_wide)
    def _(d):
        pl.semaphore_signal(barrier, inc=1, device_id=across(d), device_id_type=MESH)

    def load(v, i):
        ref = (feat_a, feat_b)[v]
        rows = rows_of(i, block)
        return pltpu.make_async_copy(ref.at[rows], feat.at[v, rows], sem_in.at[v, i])

    for v in (1, 0):
        for i in range(blocks):
            load(v, i).start()

    acc[...] = jnp.zeros_like(acc)
    feat_acc[...] = jnp.zeros_like(feat_acc)
    for v in (1, 0):

        @pl.loop(0, blocks)
        def _(i):
            load(v, i).wait()
            rows = rows_of(i, block)
            points_in = feat[v, rows, :]
            linear = dot(points_in, w_hidden[...])
            acc[2 * v] += fold(linear)
            acc[2 * v + 1] += fold(linear * linear)
            feat_acc[v] += fold(points_in.astype(F32))

    def put_sums(stat, sums):
        for r in range(4):
            stat[2 * r : 2 * r + 1, 0:split] = sums[r : r + 1, 0:split]
            stat[2 * r + 1 : 2 * r + 2, 0:split] = sums[r : r + 1, split:]

    def get_sum(total, r):
        return jnp.concatenate(
            [total[2 * r : 2 * r + 1, 0:split], total[2 * r + 1 : 2 * r + 2, 0:split]], axis=1
        )

    put_sums(stat, jnp.sum(acc[...], axis=1))

    pl.semaphore_wait(barrier, n_narrow + n_wide - 2)

    def sum_all(stat, near, part, far, total, sem_near, sem_far, between=None, later=None):
        def to_near(d):
            return remote(stat, near.at[n], sem_near, d, peer(d))

        def to_far(d):
            return remote(part, far.at[w], sem_far, d, across(d))

        start_all(to_near, n_narrow)
        near[n] = stat[...]
        if between is not None:
            between()
        wait_all(to_near, n_narrow)
        part[...] = jnp.sum(near[...], axis=0)
        start_all(to_far, n_wide)
        far[w] = part[...]
        if later is not None:
            later()
        wait_all(to_far, n_wide)
        total[...] = jnp.sum(far[...], axis=0)

    def to_msg(d):
        return remote(msg.at[lax.rem(n + d, n_narrow)], msg_in.at[n], sem_msg, d, peer(d))

    def gather(ids, table, i):
        lanes = lax.broadcasted_iota(jnp.int32, (block, points), 1)
        return dot(one_hot(ids[rows_of(i, block), :] == lanes).astype(BF16), table)

    def columns(ids, ref):
        square = jnp.concatenate(
            [ids.astype(F32), jnp.zeros((cap - n_narrow, cap), F32)], axis=0
        ).T.astype(jnp.int32)
        for s in range(n_narrow):
            ref[s * cap : (s + 1) * cap, :] = square[:, s : s + 1]

    def spread_counts():
        across_lanes = lax.broadcasted_iota(jnp.int32, (n_narrow, n_narrow), 1)
        down = lax.broadcasted_iota(jnp.int32, (n_narrow, n_narrow), 0)
        here = jnp.broadcast_to(counts[...], (n_narrow, n_narrow)).astype(F32)
        return jnp.sum(jnp.where(across_lanes == down, here, 0.0), axis=1, keepdims=True)

    def slot_order():
        count = spread_counts().astype(jnp.int32)
        line = lax.broadcasted_iota(jnp.int32, (8, cap), 0)
        for s in range(n_narrow):
            msg[s] = jnp.where(line == 0, dest_own[s : s + 1, :], count[s : s + 1, :])
        start_all(to_msg, n_narrow)
        msg_in[n] = msg[n]
        columns(send_row[...], send_col)

        @pl.loop(0, blocks)
        def _(i):
            feat_slot[rows_of(i, block), :] = gather(send_col, feat[1], i).astype(BF16)

    def slot_linear():
        @pl.loop(0, blocks)
        def _(i):
            rows = rows_of(i, block)
            lin[rows, :] = dot(feat_slot[rows, :], w_hidden[...])

        wait_all(to_msg, n_narrow)
        ids = msg_in[:, 0, :]
        dest_row[...] = ids
        columns(ids, dest_col)
        line = lax.broadcasted_iota(jnp.int32, (cap, 1), 0)
        for s in range(n_narrow):
            live_col[s * cap : (s + 1) * cap, :] = one_hot(line < msg_in[s, 1:2, 0:1])

    sum_all(stat, near, part, far, total, sem_near, sem_far, slot_order, slot_linear)

    inv_count = 1.0 / all_points
    means, inverses = [], []
    for v in range(2):
        mean = get_sum(total, 2 * v) * inv_count
        square = get_sum(total, 2 * v + 1) * inv_count
        means.append(mean)
        inverses.append(lax.rsqrt(square - mean * mean + 1e-5))

    def finish(v):
        @pl.loop(0, blocks)
        def _(i):
            rows = rows_of(i, block)
            linear = lin[rows, :] if v else dot(feat[0, rows, :], w_hidden[...])
            value = ((linear - means[v]) * inverses[v]).astype(BF16)
            normed[v, rows, :] = value
            out = dot(jnp.maximum(value, 0), w_out[...])
            unit_scale = lax.rsqrt(jnp.sum(out * out, axis=1, keepdims=True) + 1e-6)
            embed[v, rows, :] = (out * unit_scale).astype(BF16)
            scale[v, rows, :] = unit_scale

    finish(1)
    neg_col = jnp.broadcast_to(neg_row[...].astype(F32), (cap, neg_count)).T.astype(jnp.int32)
    picks = [
        one_hot(send_row[s : s + 1, :] == neg_col).astype(BF16) for s in range(n_narrow)
    ]
    negs[row, col] = dot(jnp.concatenate(picks, axis=1), embed[1]).astype(BF16)

    def neg_first(d):
        low, high = negs.at[row, col, halves[0]], negs.at[row, col, halves[1]]
        return (
            remote(low, low, sem_neg, d, along_row(d)),
            remote(high, high, sem_neg, side + d, along_col(d)),
        )

    def neg_second(d):
        low, high = negs.at[row, :, halves[0]], negs.at[:, col, halves[1]]
        return (
            remote(low, low, sem_neg, 2 * side + d, along_col(d)),
            remote(high, high, sem_neg, 3 * side + d, along_row(d)),
        )

    def start_both(make):
        for d in range(1, side):
            for copy in make(d):
                copy.start()

    def wait_both(make):
        for d in range(1, side):
            for copy in make(d):
                copy.wait()

    start_both(neg_first)

    def to_key(d):
        return remote(
            embed.at[1, rows_of(lax.rem(n + d, n_narrow), cap)],
            keys_in.at[rows_of(n, cap)],
            sem_key,
            d,
            peer(d),
        )

    start_all(to_key, n_narrow)
    keys_in[rows_of(n, cap), :] = embed[1, rows_of(n, cap), :]

    finish(0)

    wait_both(neg_first)
    start_both(neg_second)

    @pl.loop(0, blocks)
    def _(i):
        query[rows_of(i, block), :] = gather(dest_col, embed[0], i).astype(BF16)

    wait_both(neg_second)
    total_negs = n_narrow * neg_count

    to_exp2 = math.log2(math.e) / TEMPERATURE

    @pl.loop(0, points // small)
    def _(i):
        rows = rows_of(i, small)
        table = negs[...].reshape(total_negs, width)
        score = dot(query[rows, :], table, NT)
        power = jnp.exp2(score * to_exp2)
        exp_sum[rows, :] = jnp.sum(power, axis=1, keepdims=True)
        power = power.astype(BF16)
        expo[rows, :] = power
        num[rows, :] = dot(power, table)

    wh_two[...] = jnp.zeros_like(wh_two)
    wh_one[...] = jnp.zeros_like(wh_one)

    def view_rows(v, rows):
        return feat_slot[rows, :] if v else feat[0, rows, :]

    for v in range(2):

        @pl.loop(0, blocks)
        def _(i):
            rows = rows_of(i, block)
            wh_two[v] += dot(view_rows(v, rows), normed[v, rows, :], TN)

    loss_acc[...] = jnp.zeros_like(loss_acc)

    def to_slot(d):
        rows = rows_of(source(d), cap)
        return remote(
            grad_out_slots.at[rows],
            grad_in_slots.at[rows_of(n, cap)],
            sem_grad,
            d,
            (w, source(d)),
        )

    def answer(d):
        rows = rows_of(source(d), cap)
        live = live_col[rows, :]
        key = keys_in[rows, :].astype(F32)
        asked = query[rows, :].astype(F32)
        positive = jnp.sum(asked * key, axis=1, keepdims=True) * (1.0 / TEMPERATURE)
        exp_pos = jnp.exp(positive)
        denominator = exp_pos + exp_sum[rows, :]
        term = live * (jnp.log(denominator) - positive)
        weight = live * (1.0 / TEMPERATURE)
        share = weight / denominator
        pair_coeff = share * exp_pos - weight
        grad_out_slots[rows, :] = (pair_coeff * asked).astype(BF16)
        grad_query[rows, :] = (pair_coeff * key + share * num[rows, :]).astype(BF16)
        spread[:, rows] = (share * asked).T.astype(BF16)
        return jnp.sum(term, axis=0, keepdims=True)

    pair = 2

    @pl.loop(0, n_narrow // pair)
    def _(i):
        for k in range(pair):
            d = i * pair + k

            @pl.when(d > 0)
            def _():
                to_key(d).wait_recv()

        loss_acc[...] += sum(answer(i * pair + k) for k in range(pair))
        for k in range(pair):
            d = i * pair + k

            @pl.when(d > 0)
            def _():
                to_slot(d).start()

    grad_in_slots[rows_of(n, cap), :] = grad_out_slots[rows_of(n, cap), :]

    def to_owner_row(q):
        d = lax.rem(q - row + side, side)
        return remote(
            neg_out.at[q, :, halves[0]], low_in.at[row], sem_negback, d, (w, q * side + col)
        )

    def to_owner_col(d):
        q = lax.rem(col + d, side)
        return remote(
            neg_out.at[:, q, halves[1]], high_in.at[col], sem_negback, side + d, along_row(d)
        )

    def to_owner_second(d):
        return (
            remote(
                low_mid.at[lax.rem(col + d, side)],
                low_end.at[col],
                sem_negback,
                2 * side + d,
                along_row(d),
            ),
            remote(
                high_mid.at[lax.rem(row + d, side)],
                high_end.at[row],
                sem_negback,
                3 * side + d,
                along_col(d),
            ),
        )

    @pl.loop(1, side + 1)
    def _(i):
        q = lax.rem(row + i, side)
        cols = rows_of(q, side * neg_count)
        neg_out[q] = (
            dot(spread[...], expo[:, cols]).T.astype(BF16).reshape(side, neg_count, width)
        )

        @pl.when(i < side)
        def _():
            to_owner_row(q).start()

    start_all(to_owner_col, side)
    low_in[row] = neg_out[row, :, halves[0]]
    high_in[col] = neg_out[:, col, halves[1]]

    def pass_on():
        @pl.loop(1, side)
        def _(i):
            to_owner_row(lax.rem(row + i, side)).wait()

        wait_all(to_owner_col, side)
        low_mid[...] = jnp.sum(low_in[...].astype(F32), axis=0).astype(BF16)
        high_mid[...] = jnp.sum(high_in[...].astype(F32), axis=0).astype(BF16)
        start_both(to_owner_second)
        low_end[col] = low_mid[col]
        high_end[row] = high_mid[row]

    def rows_one_hot(row_ids, i, size):
        place = lax.broadcasted_iota(jnp.int32, (size, cap), 0) + i * size
        picks = [
            one_hot(row_ids[s : s + 1, :] == place).astype(BF16) for s in range(n_narrow)
        ]
        return jnp.concatenate(picks, axis=1)

    acc[...] = jnp.zeros_like(acc)
    wo_acc[...] = jnp.zeros_like(wo_acc)

    def back_top(v, grad_embed):
        @pl.loop(0, blocks)
        def _(i):
            rows = rows_of(i, block)
            grad = grad_embed(i, rows)
            unit = embed[v, rows, :].astype(F32)
            inner = jnp.sum(unit * grad, axis=1, keepdims=True)
            grad_out = (scale[v, rows, :] * (grad - unit * inner)).astype(BF16)
            value = normed[v, rows, :]
            wo_acc[...] += dot(grad_out, jnp.maximum(value, 0), TN)
            value = value.astype(F32)
            grad_act = jnp.where(value > 0, dot(grad_out, w_out[...], NT), 0.0)
            acc[2 * v] += fold(grad_act)
            acc[2 * v + 1] += fold(grad_act * value)
            grad_norm[v, rows, :] = grad_act.astype(BF16)

    def first_product(v):
        @pl.loop(0, blocks)
        def _(i):
            rows = rows_of(i, block)
            wh_one[v] += dot(view_rows(v, rows), grad_norm[v, rows, :], TN)

    back_top(0, lambda i, rows: dot(rows_one_hot(dest_row, i, block), grad_query[...]))
    pass_on()
    first_product(0)

    wait_sent(to_key, n_narrow)
    wait_all(to_slot, n_narrow)
    wait_both(to_owner_second)
    neg_mine[halves[0], :] = jnp.sum(low_end[...].astype(F32), axis=0).astype(BF16)
    neg_mine[halves[1], :] = jnp.sum(high_end[...].astype(F32), axis=0).astype(BF16)

    def grad_b(i, rows):
        mask = one_hot(send_col[rows, :] == neg_row[...]).astype(BF16)
        return grad_in_slots[rows, :].astype(F32) + dot(mask, neg_mine[...])

    back_top(1, grad_b)

    put_sums(stat2, jnp.sum(acc[...], axis=1))
    stat2[0:1, split:] = loss_acc[0:1, :]
    stat2[1:8, split:] = jnp.broadcast_to(
        jnp.sum(spread_counts(), axis=0, keepdims=True), (7, cap)
    )
    sum_all(
        stat2,
        near2,
        part2,
        far2,
        total2,
        sem_near2,
        sem_far2,
        lambda: first_product(1),
    )

    pair_total = total2[1:2, split : split + 1]
    grad_weight = all_points / pair_total
    loss_o[...] = jnp.broadcast_to(total2[0:1, split:] / pair_total, loss_o.shape)
    mean_grads = [get_sum(total2, 2 * v) * inv_count for v in range(2)]
    mean_crosses = [get_sum(total2, 2 * v + 1) * inv_count for v in range(2)]
    scales = [inverses[v] * grad_weight for v in range(2)]
    parts = hidden // width
    totals = [jnp.sum(feat_acc[v], axis=0, keepdims=True) for v in range(2)]
    downs = [jnp.broadcast_to(row, (8, depth)).T[:, 0:1] for row in totals]
    for p in range(parts):
        cols = slice(p * width, (p + 1) * width)
        value = sum(
            scales[v][:, cols]
            * (
                wh_one[v, :, cols]
                - downs[v] * mean_grads[v][:, cols]
                - wh_two[v, :, cols] * mean_crosses[v][:, cols]
            )
            for v in range(2)
        )
        grads[p * depth : (p + 1) * depth, :] = value.astype(BF16)
    grads[parts * depth :, :] = (wo_acc[...].T * grad_weight).astype(BF16)

    def store(v, i):
        ref = (grad_feat_a, grad_feat_b)[v]
        rows = rows_of(i, block)
        return pltpu.make_async_copy(normed.at[v, rows], ref.at[rows], sem_out.at[v, i])

    def feat_grad(v):
        @pl.loop(0, blocks)
        def _(i):
            rows = rows_of(i, block)
            grad = grad_norm[v, rows, :].astype(F32)
            value = normed[v, rows, :].astype(F32)
            grad = scales[v] * (grad - mean_grads[v] - value * mean_crosses[v])
            out = dot(grad.astype(BF16), w_hidden[...], NT).astype(BF16)
            if v:
                feat_slot[rows, :] = out
            else:
                normed[v, rows, :] = out
                store(v, i).start()

    def row_order():
        @pl.loop(0, blocks)
        def _(i):
            picks = rows_one_hot(send_row, i, block)
            normed[1, rows_of(i, block), :] = dot(picks, feat_slot[...]).astype(BF16)
            store(1, i).start()

    span, rows = half.shape[0], chunk.shape[0]
    z, c = w // 2, lax.rem(w, 2)
    partner = (2 * z + 1 - c, n)
    mine = pl.multiple_of(c * span, span)
    other = pl.multiple_of((1 - c) * span, span)
    swap = remote(grads.at[pl.ds(other, span)], half, sem_pair, 0, partner)
    swap.start()
    swap.wait()
    own[...] = (
        grads[pl.ds(mine, span), :].astype(F32) + half[...].astype(F32)
    ).astype(BF16)

    def to_piece(d):
        return remote(
            own.at[rows_of(lax.rem(n + d, n_narrow), rows)], piece.at[n], sem_piece, d, peer(d)
        )

    start_all(to_piece, n_narrow)
    piece[n] = own[rows_of(n, rows), :]
    feat_grad(0)
    wait_all(to_piece, n_narrow)
    chunk[...] = jnp.sum(piece[...].astype(F32), axis=0).astype(BF16)

    def to_stack(d):
        return remote(
            chunk, stack_in.at[z], sem_stack, d, (2 * lax.rem(z + d, n_z) + c, n)
        )

    start_all(to_stack, n_z)
    stack_in[z] = chunk[...]
    feat_grad(1)
    wait_all(to_stack, n_z)
    place = pl.ds(pl.multiple_of(mine + n * rows, rows), rows)
    grads_o[place, :] = jnp.sum(stack_in[...].astype(F32), axis=0).astype(BF16)

    def to_gather(d):
        return remote(grads_o.at[place], grads_o.at[place], sem_gather, d, peer(d))

    start_all(to_gather, n_narrow)
    row_order()
    wait_all(to_gather, n_narrow)
    swap = remote(
        grads_o.at[pl.ds(mine, span)], grads_o.at[pl.ds(mine, span)], sem_pair, 1, partner
    )
    swap.start()
    for v in range(2):
        for i in range(blocks):
            store(v, i).wait()
    swap.wait()


def deliver_kernel(loss, grad_a, grad_b, grads, loss_o, out_a, out_b, out_wh, out_wo, sems):
    pieces = sems.shape[1]
    rows = grad_a.shape[0] // pieces
    copies = [
        pltpu.make_async_copy(
            src.at[pl.ds(i * rows, rows)], dst.at[pl.ds(i * rows, rows)], sems.at[v, i]
        )
        for v, (src, dst) in enumerate(((grad_a, out_a), (grad_b, out_b)))
        for i in range(pieces)
    ]
    for copy in copies:
        copy.start()
    depth, hidden = out_wh.shape
    width = out_wo.shape[1]
    for p in range(hidden // width):
        out_wh[:, p * width : (p + 1) * width] = grads[p * depth : (p + 1) * depth, :].astype(F32)
    out_wo[...] = grads[hidden // width * depth :, :].astype(F32)
    loss_o[...] = loss[0:1, 0:1]
    for copy in copies:
        copy.wait()


def body(feat_a, feat_b, w_hidden, w_out, send_rows, dest_rows, counts, neg_rows):
    points, depth = feat_a.shape[2:]
    hidden, width = w_out.shape
    n_wide, n_narrow = lax.axis_size("wide"), lax.axis_size("narrow")
    n_z = n_wide // 2
    side = math.isqrt(n_narrow)
    cap = send_rows.shape[3]
    neg_count = neg_rows.shape[2]
    total_negs = n_narrow * neg_count
    all_points = float(n_wide * n_narrow * points)
    blocks = points // min(512, points)
    stat = (8, hidden // 2)
    stat2 = (8, hidden // 2 + cap)
    grad_total = depth * hidden // width + hidden
    span = grad_total // 2
    rows = span // n_narrow
    vmem = pl.BlockSpec(memory_space=pltpu.VMEM)
    anywhere = pl.BlockSpec(memory_space=pl.ANY)
    dma = pltpu.SemaphoreType.DMA
    out_shape = (
        jax.ShapeDtypeStruct((8, cap), F32),
        jax.ShapeDtypeStruct((points, depth), BF16),
        jax.ShapeDtypeStruct((points, depth), BF16),
        jax.ShapeDtypeStruct((grad_total, width), BF16),
    )
    scratch = [
        pltpu.VMEM((2, points, depth), BF16),
        pltpu.VMEM((points, depth), BF16),
        pltpu.VMEM((points, hidden), F32),
        pltpu.VMEM((2, points, hidden), BF16),
        pltpu.VMEM((2, points, width), BF16),
        pltpu.VMEM((2, points, 1), F32),
        pltpu.VMEM((4, 8, hidden), F32),
        pltpu.VMEM((2, 8, depth), F32),
        pltpu.VMEM(stat, F32),
        pltpu.VMEM((n_narrow,) + stat, F32),
        pltpu.VMEM(stat, F32),
        pltpu.VMEM((n_wide,) + stat, F32),
        pltpu.VMEM(stat, F32),
        pltpu.VMEM(stat2, F32),
        pltpu.VMEM((n_narrow,) + stat2, F32),
        pltpu.VMEM(stat2, F32),
        pltpu.VMEM((n_wide,) + stat2, F32),
        pltpu.VMEM(stat2, F32),
        pltpu.VMEM((n_narrow, 8, cap), jnp.int32),
        pltpu.VMEM((n_narrow, 8, cap), jnp.int32),
        pltpu.VMEM((points, 1), jnp.int32),
        pltpu.VMEM((n_narrow, cap), jnp.int32),
        pltpu.VMEM((points, 1), jnp.int32),
        pltpu.VMEM((points, 1), F32),
        pltpu.VMEM((points, width), BF16),
        pltpu.VMEM((side, side, neg_count, width), BF16),
        pltpu.VMEM((points, width), BF16),
        pltpu.VMEM((points, total_negs), BF16),
        pltpu.VMEM((points, 1), F32),
        pltpu.VMEM((points, width), F32),
        pltpu.VMEM((width, points), BF16),
        pltpu.VMEM((points, width), BF16),
        pltpu.VMEM((points, width), BF16),
        pltpu.VMEM((points, width), BF16),
        pltpu.VMEM((side, side, neg_count, width), BF16),
        pltpu.VMEM((side, side, neg_count // 2, width), BF16),
        pltpu.VMEM((side, side, neg_count // 2, width), BF16),
        pltpu.VMEM((side, neg_count // 2, width), BF16),
        pltpu.VMEM((side, neg_count // 2, width), BF16),
        pltpu.VMEM((side, neg_count // 2, width), BF16),
        pltpu.VMEM((side, neg_count // 2, width), BF16),
        pltpu.VMEM((neg_count, width), BF16),
        pltpu.VMEM((2, points, hidden), BF16),
        pltpu.VMEM((width, hidden), F32),
        pltpu.VMEM((2, depth, hidden), F32),
        pltpu.VMEM((2, depth, hidden), F32),
        pltpu.VMEM((8, cap), F32),
        pltpu.VMEM((grad_total, width), BF16),
        pltpu.VMEM((span, width), BF16),
        pltpu.VMEM((span, width), BF16),
        pltpu.VMEM((n_narrow, rows, width), BF16),
        pltpu.VMEM((rows, width), BF16),
        pltpu.VMEM((n_z, rows, width), BF16),
        dma((2, blocks)),
        dma((2, blocks)),
        dma((2, n_narrow)),
        dma((2, n_narrow)),
        dma((2, n_wide)),
        dma((2, n_narrow)),
        dma((2, n_wide)),
        dma((2, 4 * side)),
        dma((2, n_narrow)),
        dma((2, n_narrow)),
        dma((2, 4 * side)),
        dma((2, 2)),
        dma((2, n_narrow)),
        dma((2, n_z)),
        dma((2, n_narrow)),
    ]
    loss, grad_a, grad_b, grads = pl.pallas_call(
        functools.partial(step_kernel, all_points),
        out_shape=out_shape,
        in_specs=[anywhere] * 2 + [vmem] * 6,
        out_specs=(vmem, anywhere, anywhere, vmem),
        scratch_shapes=scratch,
        compiler_params=pltpu.CompilerParams(
            collective_id=1, has_side_effects=True, vmem_limit_bytes=63 * 1024 * 1024
        ),
        name="step",
    )(
        feat_a.reshape(points, depth),
        feat_b.reshape(points, depth),
        w_hidden,
        w_out,
        send_rows.reshape(n_narrow, cap),
        dest_rows.reshape(n_narrow, cap),
        counts.reshape(1, n_narrow),
        neg_rows.reshape(1, neg_count),
    )
    loss, grad_a, grad_b, grad_wh, grad_wo = pl.pallas_call(
        deliver_kernel,
        out_shape=(
            jax.ShapeDtypeStruct((1, 1), F32),
            jax.ShapeDtypeStruct((points, depth), BF16),
            jax.ShapeDtypeStruct((points, depth), BF16),
            jax.ShapeDtypeStruct((depth, hidden), F32),
            jax.ShapeDtypeStruct((hidden, width), F32),
        ),
        in_specs=[vmem, anywhere, anywhere, vmem],
        out_specs=(vmem, anywhere, anywhere, vmem, vmem),
        scratch_shapes=[dma((2, 4))],
        compiler_params=pltpu.CompilerParams(vmem_limit_bytes=63 * 1024 * 1024),
        name="deliver",
    )(loss, grad_a, grad_b, grads)
    return (
        loss.reshape(()),
        grad_a.reshape(feat_a.shape),
        grad_b.reshape(feat_b.shape),
        grad_wh,
        grad_wo,
    )


def solution(mesh):
    placed = (
        P("wide", "narrow", None, None),
        P("wide", "narrow", None, None),
        P(),
        P(),
        P("wide", "narrow", None, None),
        P("wide", "narrow", None, None),
        P("wide", "narrow", None),
        P("wide", "narrow", None),
    )
    return jax.shard_map(
        body,
        mesh=mesh,
        in_specs=placed,
        out_specs=(P(), P("wide", "narrow", None, None), P("wide", "narrow", None, None), P(), P()),
        check_vma=False,
    )
```

```python
import functools
import math

import jax
import jax.numpy as jnp
from jax import lax
from jax.experimental import pallas as pl
from jax.experimental.pallas import tpu as pltpu
from jax.sharding import PartitionSpec as P

MESH = pl.DeviceIdType.MESH
F32 = jnp.float32
BF16 = jnp.bfloat16
TEMPERATURE = 0.07
NT = (((1,), (1,)), ((), ()))
TN = (((0,), (0,)), ((), ()))


def dot(left, right, dims=None):
    if dims is None:
        return jnp.dot(left, right, preferred_element_type=F32)
    return lax.dot_general(left, right, dims, preferred_element_type=F32)


def one_hot(mask):
    return jnp.where(mask, 1.0, 0.0).astype(F32)


def fold(values):
    rows, width = values.shape
    return jnp.sum(values.reshape(rows // 8, 8, width), axis=0)


def remote(src, dst, sems, d, device):
    return pltpu.make_async_remote_copy(
        src_ref=src,
        dst_ref=dst,
        send_sem=sems.at[0, d],
        recv_sem=sems.at[1, d],
        device_id=device,
        device_id_type=MESH,
    )


def start_all(make, count):
    @pl.loop(1, count)
    def _(d):
        make(d).start()


def wait_all(make, count):
    @pl.loop(1, count)
    def _(d):
        make(d).wait()


def wait_sent(make, count):
    @pl.loop(1, count)
    def _(d):
        make(d).wait_send()


def step_kernel(
    all_points,
    feat_a,
    feat_b,
    w_hidden,
    w_out,
    send_row,
    dest_own,
    counts,
    neg_row,
    loss_o,
    grad_feat_a,
    grad_feat_b,
    grads_o,
    feat,
    feat_slot,
    lin,
    normed,
    embed,
    scale,
    acc,
    feat_acc,
    stat,
    near,
    part,
    far,
    total,
    stat2,
    near2,
    part2,
    far2,
    total2,
    msg,
    msg_in,
    send_col,
    dest_row,
    dest_col,
    live_col,
    query,
    negs,
    keys_in,
    expo,
    exp_sum,
    num,
    spread,
    grad_query,
    grad_out_slots,
    grad_in_slots,
    neg_out,
    low_in,
    high_in,
    low_mid,
    high_mid,
    low_end,
    high_end,
    neg_mine,
    grad_norm,
    wo_acc,
    wh_one,
    wh_two,
    loss_acc,
    grads,
    half,
    own,
    piece,
    chunk,
    stack_in,
    sem_in,
    sem_out,
    sem_msg,
    sem_near,
    sem_far,
    sem_near2,
    sem_far2,
    sem_neg,
    sem_key,
    sem_grad,
    sem_negback,
    sem_pair,
    sem_piece,
    sem_stack,
    sem_gather,
):
    w = lax.axis_index("wide")
    n = lax.axis_index("narrow")
    n_wide = far.shape[0]
    n_narrow = near.shape[0]
    n_z = stack_in.shape[0]
    points, depth = feat_a.shape
    hidden = w_hidden.shape[1]
    width = w_out.shape[1]
    cap = points // n_narrow
    neg_count = neg_row.shape[1]
    block = min(512, points)
    small = min(256, points)
    blocks = points // block
    split = hidden // 2
    side = negs.shape[0]
    upper = neg_count // 2
    row, col = n // side, lax.rem(n, side)
    halves = (slice(0, upper), slice(upper, neg_count))

    def peer(d):
        return (w, lax.rem(n + d, n_narrow))

    def along_row(d):
        return (w, row * side + lax.rem(col + d, side))

    def along_col(d):
        return (w, lax.rem(row + d, side) * side + col)

    def source(d):
        return lax.rem(n + n_narrow - d, n_narrow)

    def across(d):
        return (lax.rem(w + d, n_wide), n)

    def rows_of(i, size):
        return pl.ds(pl.multiple_of(i * size, size), size)

    barrier = pltpu.get_barrier_semaphore()

    @pl.loop(1, n_narrow)
    def _(d):
        pl.semaphore_signal(barrier, inc=1, device_id=peer(d), device_id_type=MESH)

    @pl.loop(1, n_wide)
    def _(d):
        pl.semaphore_signal(barrier, inc=1, device_id=across(d), device_id_type=MESH)

    def load(v, i):
        ref = (feat_a, feat_b)[v]
        rows = rows_of(i, block)
        return pltpu.make_async_copy(ref.at[rows], feat.at[v, rows], sem_in.at[v, i])

    for v in (1, 0):
        for i in range(blocks):
            load(v, i).start()

    acc[...] = jnp.zeros_like(acc)
    feat_acc[...] = jnp.zeros_like(feat_acc)
    for v in (1, 0):

        @pl.loop(0, blocks)
        def _(i):
            load(v, i).wait()
            rows = rows_of(i, block)
            points_in = feat[v, rows, :]
            linear = dot(points_in, w_hidden[...])
            acc[2 * v] += fold(linear)
            acc[2 * v + 1] += fold(linear * linear)
            feat_acc[v] += fold(points_in.astype(F32))

    def put_sums(stat, sums):
        for r in range(4):
            stat[2 * r : 2 * r + 1, 0:split] = sums[r : r + 1, 0:split]
            stat[2 * r + 1 : 2 * r + 2, 0:split] = sums[r : r + 1, split:]

    def get_sum(total, r):
        return jnp.concatenate(
            [total[2 * r : 2 * r + 1, 0:split], total[2 * r + 1 : 2 * r + 2, 0:split]], axis=1
        )

    put_sums(stat, jnp.sum(acc[...], axis=1))

    pl.semaphore_wait(barrier, n_narrow + n_wide - 2)

    def sum_all(stat, near, part, far, total, sem_near, sem_far, between=None, later=None):
        def to_near(d):
            return remote(stat, near.at[n], sem_near, d, peer(d))

        def to_far(d):
            return remote(part, far.at[w], sem_far, d, across(d))

        start_all(to_near, n_narrow)
        near[n] = stat[...]
        if between is not None:
            between()
        wait_all(to_near, n_narrow)
        part[...] = jnp.sum(near[...], axis=0)
        start_all(to_far, n_wide)
        far[w] = part[...]
        if later is not None:
            later()
        wait_all(to_far, n_wide)
        total[...] = jnp.sum(far[...], axis=0)

    def to_msg(d):
        return remote(msg.at[lax.rem(n + d, n_narrow)], msg_in.at[n], sem_msg, d, peer(d))

    def gather(ids, table, i):
        lanes = lax.broadcasted_iota(jnp.int32, (block, points), 1)
        return dot(one_hot(ids[rows_of(i, block), :] == lanes).astype(BF16), table)

    def columns(ids, ref):
        square = jnp.concatenate(
            [ids.astype(F32), jnp.zeros((cap - n_narrow, cap), F32)], axis=0
        ).T.astype(jnp.int32)
        for s in range(n_narrow):
            ref[s * cap : (s + 1) * cap, :] = square[:, s : s + 1]

    def spread_counts():
        across_lanes = lax.broadcasted_iota(jnp.int32, (n_narrow, n_narrow), 1)
        down = lax.broadcasted_iota(jnp.int32, (n_narrow, n_narrow), 0)
        here = jnp.broadcast_to(counts[...], (n_narrow, n_narrow)).astype(F32)
        return jnp.sum(jnp.where(across_lanes == down, here, 0.0), axis=1, keepdims=True)

    def slot_order():
        count = spread_counts().astype(jnp.int32)
        line = lax.broadcasted_iota(jnp.int32, (8, cap), 0)
        for s in range(n_narrow):
            msg[s] = jnp.where(line == 0, dest_own[s : s + 1, :], count[s : s + 1, :])
        start_all(to_msg, n_narrow)
        msg_in[n] = msg[n]
        columns(send_row[...], send_col)

        @pl.loop(0, blocks)
        def _(i):
            feat_slot[rows_of(i, block), :] = gather(send_col, feat[1], i).astype(BF16)

    def slot_linear():
        @pl.loop(0, blocks)
        def _(i):
            rows = rows_of(i, block)
            lin[rows, :] = dot(feat_slot[rows, :], w_hidden[...])

        wait_all(to_msg, n_narrow)
        ids = msg_in[:, 0, :]
        dest_row[...] = ids
        columns(ids, dest_col)
        line = lax.broadcasted_iota(jnp.int32, (cap, 1), 0)
        for s in range(n_narrow):
            live_col[s * cap : (s + 1) * cap, :] = one_hot(line < msg_in[s, 1:2, 0:1])

    sum_all(stat, near, part, far, total, sem_near, sem_far, slot_order, slot_linear)

    inv_count = 1.0 / all_points
    means, inverses = [], []
    for v in range(2):
        mean = get_sum(total, 2 * v) * inv_count
        square = get_sum(total, 2 * v + 1) * inv_count
        means.append(mean)
        inverses.append(lax.rsqrt(square - mean * mean + 1e-5))

    def finish(v):
        @pl.loop(0, blocks)
        def _(i):
            rows = rows_of(i, block)
            linear = lin[rows, :] if v else dot(feat[0, rows, :], w_hidden[...])
            value = ((linear - means[v]) * inverses[v]).astype(BF16)
            normed[v, rows, :] = value
            out = dot(jnp.maximum(value, 0), w_out[...])
            unit_scale = lax.rsqrt(jnp.sum(out * out, axis=1, keepdims=True) + 1e-6)
            embed[v, rows, :] = (out * unit_scale).astype(BF16)
            scale[v, rows, :] = unit_scale

    finish(1)
    neg_col = jnp.broadcast_to(neg_row[...].astype(F32), (cap, neg_count)).T.astype(jnp.int32)
    picks = [
        one_hot(send_row[s : s + 1, :] == neg_col).astype(BF16) for s in range(n_narrow)
    ]
    negs[row, col] = dot(jnp.concatenate(picks, axis=1), embed[1]).astype(BF16)

    def neg_first(d):
        low, high = negs.at[row, col, halves[0]], negs.at[row, col, halves[1]]
        return (
            remote(low, low, sem_neg, d, along_row(d)),
            remote(high, high, sem_neg, side + d, along_col(d)),
        )

    def neg_second(d):
        low, high = negs.at[row, :, halves[0]], negs.at[:, col, halves[1]]
        return (
            remote(low, low, sem_neg, 2 * side + d, along_col(d)),
            remote(high, high, sem_neg, 3 * side + d, along_row(d)),
        )

    def start_both(make):
        for d in range(1, side):
            for copy in make(d):
                copy.start()

    def wait_both(make):
        for d in range(1, side):
            for copy in make(d):
                copy.wait()

    start_both(neg_first)

    def to_key(d):
        return remote(
            embed.at[1, rows_of(lax.rem(n + d, n_narrow), cap)],
            keys_in.at[rows_of(n, cap)],
            sem_key,
            d,
            peer(d),
        )

    finish(0)

    wait_both(neg_first)
    start_both(neg_second)
    start_all(to_key, n_narrow)
    keys_in[rows_of(n, cap), :] = embed[1, rows_of(n, cap), :]

    @pl.loop(0, blocks)
    def _(i):
        query[rows_of(i, block), :] = gather(dest_col, embed[0], i).astype(BF16)

    wh_two[...] = jnp.zeros_like(wh_two)
    wh_one[...] = jnp.zeros_like(wh_one)

    def view_rows(v, rows):
        return feat_slot[rows, :] if v else feat[0, rows, :]

    for v in range(2):

        @pl.loop(0, blocks)
        def _(i):
            rows = rows_of(i, block)
            wh_two[v] += dot(view_rows(v, rows), normed[v, rows, :], TN)

    wait_both(neg_second)
    total_negs = n_narrow * neg_count

    to_exp2 = math.log2(math.e) / TEMPERATURE

    @pl.loop(0, points // small)
    def _(i):
        rows = rows_of(i, small)
        table = negs[...].reshape(total_negs, width)
        score = dot(query[rows, :], table, NT)
        power = jnp.exp2(score * to_exp2)
        exp_sum[rows, :] = jnp.sum(power, axis=1, keepdims=True)
        power = power.astype(BF16)
        expo[rows, :] = power
        num[rows, :] = dot(power, table)

    loss_acc[...] = jnp.zeros_like(loss_acc)

    def to_slot(d):
        rows = rows_of(source(d), cap)
        return remote(
            grad_out_slots.at[rows],
            grad_in_slots.at[rows_of(n, cap)],
            sem_grad,
            d,
            (w, source(d)),
        )

    def answer(d):
        rows = rows_of(source(d), cap)
        live = live_col[rows, :]
        key = keys_in[rows, :].astype(F32)
        asked = query[rows, :].astype(F32)
        positive = jnp.sum(asked * key, axis=1, keepdims=True) * (1.0 / TEMPERATURE)
        exp_pos = jnp.exp(positive)
        denominator = exp_pos + exp_sum[rows, :]
        term = live * (jnp.log(denominator) - positive)
        weight = live * (1.0 / TEMPERATURE)
        share = weight / denominator
        pair_coeff = share * exp_pos - weight
        grad_out_slots[rows, :] = (pair_coeff * asked).astype(BF16)
        grad_query[rows, :] = (pair_coeff * key + share * num[rows, :]).astype(BF16)
        spread[:, rows] = (share * asked).T.astype(BF16)
        return jnp.sum(term, axis=0, keepdims=True)

    pair = 2

    @pl.loop(0, n_narrow // pair)
    def _(i):
        for k in range(pair):
            d = i * pair + k

            @pl.when(d > 0)
            def _():
                to_key(d).wait_recv()

        loss_acc[...] += sum(answer(i * pair + k) for k in range(pair))
        for k in range(pair):
            d = i * pair + k

            @pl.when(d > 0)
            def _():
                to_slot(d).start()

    grad_in_slots[rows_of(n, cap), :] = grad_out_slots[rows_of(n, cap), :]

    def to_owner_row(q):
        d = lax.rem(q - row + side, side)
        return remote(
            neg_out.at[q, :, halves[0]], low_in.at[row], sem_negback, d, (w, q * side + col)
        )

    def to_owner_col(d):
        q = lax.rem(col + d, side)
        return remote(
            neg_out.at[:, q, halves[1]], high_in.at[col], sem_negback, side + d, along_row(d)
        )

    def to_owner_second(d):
        return (
            remote(
                low_mid.at[lax.rem(col + d, side)],
                low_end.at[col],
                sem_negback,
                2 * side + d,
                along_row(d),
            ),
            remote(
                high_mid.at[lax.rem(row + d, side)],
                high_end.at[row],
                sem_negback,
                3 * side + d,
                along_col(d),
            ),
        )

    @pl.loop(1, side + 1)
    def _(i):
        q = lax.rem(row + i, side)
        cols = rows_of(q, side * neg_count)
        neg_out[q] = (
            dot(spread[...], expo[:, cols]).T.astype(BF16).reshape(side, neg_count, width)
        )

        @pl.when(i < side)
        def _():
            to_owner_row(q).start()

    start_all(to_owner_col, side)
    low_in[row] = neg_out[row, :, halves[0]]
    high_in[col] = neg_out[:, col, halves[1]]

    def pass_on():
        @pl.loop(1, side)
        def _(i):
            to_owner_row(lax.rem(row + i, side)).wait()

        wait_all(to_owner_col, side)
        low_mid[...] = jnp.sum(low_in[...].astype(F32), axis=0).astype(BF16)
        high_mid[...] = jnp.sum(high_in[...].astype(F32), axis=0).astype(BF16)
        start_both(to_owner_second)
        low_end[col] = low_mid[col]
        high_end[row] = high_mid[row]

    def rows_one_hot(row_ids, i, size):
        place = lax.broadcasted_iota(jnp.int32, (size, cap), 0) + i * size
        picks = [
            one_hot(row_ids[s : s + 1, :] == place).astype(BF16) for s in range(n_narrow)
        ]
        return jnp.concatenate(picks, axis=1)

    acc[...] = jnp.zeros_like(acc)
    wo_acc[...] = jnp.zeros_like(wo_acc)

    def back_top(v, grad_embed):
        @pl.loop(0, blocks)
        def _(i):
            rows = rows_of(i, block)
            grad = grad_embed(i, rows)
            unit = embed[v, rows, :].astype(F32)
            inner = jnp.sum(unit * grad, axis=1, keepdims=True)
            grad_out = (scale[v, rows, :] * (grad - unit * inner)).astype(BF16)
            value = normed[v, rows, :]
            wo_acc[...] += dot(grad_out, jnp.maximum(value, 0), TN)
            value = value.astype(F32)
            grad_act = jnp.where(value > 0, dot(grad_out, w_out[...], NT), 0.0)
            acc[2 * v] += fold(grad_act)
            acc[2 * v + 1] += fold(grad_act * value)
            grad_norm[v, rows, :] = grad_act.astype(BF16)

    def first_product(v):
        @pl.loop(0, blocks)
        def _(i):
            rows = rows_of(i, block)
            wh_one[v] += dot(view_rows(v, rows), grad_norm[v, rows, :], TN)

    back_top(0, lambda i, rows: dot(rows_one_hot(dest_row, i, block), grad_query[...]))
    pass_on()
    first_product(0)

    wait_sent(to_key, n_narrow)
    wait_all(to_slot, n_narrow)
    wait_both(to_owner_second)
    neg_mine[halves[0], :] = jnp.sum(low_end[...].astype(F32), axis=0).astype(BF16)
    neg_mine[halves[1], :] = jnp.sum(high_end[...].astype(F32), axis=0).astype(BF16)

    def grad_b(i, rows):
        mask = one_hot(send_col[rows, :] == neg_row[...]).astype(BF16)
        return grad_in_slots[rows, :].astype(F32) + dot(mask, neg_mine[...])

    back_top(1, grad_b)

    put_sums(stat2, jnp.sum(acc[...], axis=1))
    stat2[0:1, split:] = loss_acc[0:1, :]
    stat2[1:8, split:] = jnp.broadcast_to(
        jnp.sum(spread_counts(), axis=0, keepdims=True), (7, cap)
    )
    sum_all(
        stat2,
        near2,
        part2,
        far2,
        total2,
        sem_near2,
        sem_far2,
        lambda: first_product(1),
    )

    pair_total = total2[1:2, split : split + 1]
    grad_weight = all_points / pair_total
    loss_o[...] = jnp.broadcast_to(total2[0:1, split:] / pair_total, loss_o.shape)
    mean_grads = [get_sum(total2, 2 * v) * inv_count for v in range(2)]
    mean_crosses = [get_sum(total2, 2 * v + 1) * inv_count for v in range(2)]
    scales = [inverses[v] * grad_weight for v in range(2)]
    parts = hidden // width
    totals = [jnp.sum(feat_acc[v], axis=0, keepdims=True) for v in range(2)]
    downs = [jnp.broadcast_to(row, (8, depth)).T[:, 0:1] for row in totals]
    for p in range(parts):
        cols = slice(p * width, (p + 1) * width)
        value = sum(
            scales[v][:, cols]
            * (
                wh_one[v, :, cols]
                - downs[v] * mean_grads[v][:, cols]
                - wh_two[v, :, cols] * mean_crosses[v][:, cols]
            )
            for v in range(2)
        )
        grads[p * depth : (p + 1) * depth, :] = value.astype(BF16)
    grads[parts * depth :, :] = (wo_acc[...].T * grad_weight).astype(BF16)

    def store(v, i):
        ref = (grad_feat_a, grad_feat_b)[v]
        rows = rows_of(i, block)
        return pltpu.make_async_copy(normed.at[v, rows], ref.at[rows], sem_out.at[v, i])

    def feat_grad(v):
        @pl.loop(0, blocks)
        def _(i):
            rows = rows_of(i, block)
            grad = grad_norm[v, rows, :].astype(F32)
            value = normed[v, rows, :].astype(F32)
            grad = scales[v] * (grad - mean_grads[v] - value * mean_crosses[v])
            out = dot(grad.astype(BF16), w_hidden[...], NT).astype(BF16)
            if v:
                feat_slot[rows, :] = out
            else:
                normed[v, rows, :] = out
                store(v, i).start()

    def row_order():
        @pl.loop(0, blocks)
        def _(i):
            picks = rows_one_hot(send_row, i, block)
            normed[1, rows_of(i, block), :] = dot(picks, feat_slot[...]).astype(BF16)
            store(1, i).start()

    span, rows = half.shape[0], chunk.shape[0]
    z, c = w // 2, lax.rem(w, 2)
    partner = (2 * z + 1 - c, n)
    mine = pl.multiple_of(c * span, span)
    other = pl.multiple_of((1 - c) * span, span)
    swap = remote(grads.at[pl.ds(other, span)], half, sem_pair, 0, partner)
    swap.start()
    swap.wait()
    own[...] = (
        grads[pl.ds(mine, span), :].astype(F32) + half[...].astype(F32)
    ).astype(BF16)

    def to_piece(d):
        return remote(
            own.at[rows_of(lax.rem(n + d, n_narrow), rows)], piece.at[n], sem_piece, d, peer(d)
        )

    start_all(to_piece, n_narrow)
    piece[n] = own[rows_of(n, rows), :]
    feat_grad(0)
    wait_all(to_piece, n_narrow)
    chunk[...] = jnp.sum(piece[...].astype(F32), axis=0).astype(BF16)

    def to_stack(d):
        return remote(
            chunk, stack_in.at[z], sem_stack, d, (2 * lax.rem(z + d, n_z) + c, n)
        )

    start_all(to_stack, n_z)
    stack_in[z] = chunk[...]
    feat_grad(1)
    wait_all(to_stack, n_z)
    place = pl.ds(pl.multiple_of(mine + n * rows, rows), rows)
    grads_o[place, :] = jnp.sum(stack_in[...].astype(F32), axis=0).astype(BF16)

    def to_gather(d):
        return remote(grads_o.at[place], grads_o.at[place], sem_gather, d, peer(d))

    start_all(to_gather, n_narrow)
    row_order()
    wait_all(to_gather, n_narrow)
    swap = remote(
        grads_o.at[pl.ds(mine, span)], grads_o.at[pl.ds(mine, span)], sem_pair, 1, partner
    )
    swap.start()
    for v in range(2):
        for i in range(blocks):
            store(v, i).wait()
    swap.wait()


def deliver_kernel(
    loss, grad_a, grad_b, grads, loss_o, out_a, out_b, out_wh, out_wo, held, read_sem, write_sem
):
    pieces = read_sem.shape[1]
    rows = grad_a.shape[0] // pieces
    reads, writes = [], []
    for v, (src, dst) in enumerate(((grad_a, out_a), (grad_b, out_b))):
        for i in range(pieces):
            part = pl.ds(i * rows, rows)
            middle = held.at[v, part]
            reads.append(pltpu.make_async_copy(src.at[part], middle, read_sem.at[v, i]))
            writes.append(pltpu.make_async_copy(middle, dst.at[part], write_sem.at[v, i]))
    for copy in reads:
        copy.start()
    for arrived, copy in zip(reads, writes):
        arrived.wait()
        copy.start()
    depth, hidden = out_wh.shape
    width = out_wo.shape[1]
    for p in range(hidden // width):
        out_wh[:, p * width : (p + 1) * width] = grads[p * depth : (p + 1) * depth, :].astype(F32)
    out_wo[...] = grads[hidden // width * depth :, :].astype(F32)
    loss_o[...] = loss[0:1, 0:1]
    for copy in writes:
        copy.wait()

def body(feat_a, feat_b, w_hidden, w_out, send_rows, dest_rows, counts, neg_rows):
    points, depth = feat_a.shape[2:]
    hidden, width = w_out.shape
    n_wide, n_narrow = lax.axis_size("wide"), lax.axis_size("narrow")
    n_z = n_wide // 2
    side = math.isqrt(n_narrow)
    cap = send_rows.shape[3]
    neg_count = neg_rows.shape[2]
    total_negs = n_narrow * neg_count
    all_points = float(n_wide * n_narrow * points)
    blocks = points // min(512, points)
    stat = (8, hidden // 2)
    stat2 = (8, hidden // 2 + cap)
    grad_total = depth * hidden // width + hidden
    span = grad_total // 2
    rows = span // n_narrow
    vmem = pl.BlockSpec(memory_space=pltpu.VMEM)
    anywhere = pl.BlockSpec(memory_space=pl.ANY)
    dma = pltpu.SemaphoreType.DMA
    out_shape = (
        jax.ShapeDtypeStruct((8, cap), F32),
        jax.ShapeDtypeStruct((points, depth), BF16),
        jax.ShapeDtypeStruct((points, depth), BF16),
        jax.ShapeDtypeStruct((grad_total, width), BF16),
    )
    scratch = [
        pltpu.VMEM((2, points, depth), BF16),
        pltpu.VMEM((points, depth), BF16),
        pltpu.VMEM((points, hidden), F32),
        pltpu.VMEM((2, points, hidden), BF16),
        pltpu.VMEM((2, points, width), BF16),
        pltpu.VMEM((2, points, 1), F32),
        pltpu.VMEM((4, 8, hidden), F32),
        pltpu.VMEM((2, 8, depth), F32),
        pltpu.VMEM(stat, F32),
        pltpu.VMEM((n_narrow,) + stat, F32),
        pltpu.VMEM(stat, F32),
        pltpu.VMEM((n_wide,) + stat, F32),
        pltpu.VMEM(stat, F32),
        pltpu.VMEM(stat2, F32),
        pltpu.VMEM((n_narrow,) + stat2, F32),
        pltpu.VMEM(stat2, F32),
        pltpu.VMEM((n_wide,) + stat2, F32),
        pltpu.VMEM(stat2, F32),
        pltpu.VMEM((n_narrow, 8, cap), jnp.int32),
        pltpu.VMEM((n_narrow, 8, cap), jnp.int32),
        pltpu.VMEM((points, 1), jnp.int32),
        pltpu.VMEM((n_narrow, cap), jnp.int32),
        pltpu.VMEM((points, 1), jnp.int32),
        pltpu.VMEM((points, 1), F32),
        pltpu.VMEM((points, width), BF16),
        pltpu.VMEM((side, side, neg_count, width), BF16),
        pltpu.VMEM((points, width), BF16),
        pltpu.VMEM((points, total_negs), BF16),
        pltpu.VMEM((points, 1), F32),
        pltpu.VMEM((points, width), F32),
        pltpu.VMEM((width, points), BF16),
        pltpu.VMEM((points, width), BF16),
        pltpu.VMEM((points, width), BF16),
        pltpu.VMEM((points, width), BF16),
        pltpu.VMEM((side, side, neg_count, width), BF16),
        pltpu.VMEM((side, side, neg_count // 2, width), BF16),
        pltpu.VMEM((side, side, neg_count // 2, width), BF16),
        pltpu.VMEM((side, neg_count // 2, width), BF16),
        pltpu.VMEM((side, neg_count // 2, width), BF16),
        pltpu.VMEM((side, neg_count // 2, width), BF16),
        pltpu.VMEM((side, neg_count // 2, width), BF16),
        pltpu.VMEM((neg_count, width), BF16),
        pltpu.VMEM((2, points, hidden), BF16),
        pltpu.VMEM((width, hidden), F32),
        pltpu.VMEM((2, depth, hidden), F32),
        pltpu.VMEM((2, depth, hidden), F32),
        pltpu.VMEM((8, cap), F32),
        pltpu.VMEM((grad_total, width), BF16),
        pltpu.VMEM((span, width), BF16),
        pltpu.VMEM((span, width), BF16),
        pltpu.VMEM((n_narrow, rows, width), BF16),
        pltpu.VMEM((rows, width), BF16),
        pltpu.VMEM((n_z, rows, width), BF16),
        dma((2, blocks)),
        dma((2, blocks)),
        dma((2, n_narrow)),
        dma((2, n_narrow)),
        dma((2, n_wide)),
        dma((2, n_narrow)),
        dma((2, n_wide)),
        dma((2, 4 * side)),
        dma((2, n_narrow)),
        dma((2, n_narrow)),
        dma((2, 4 * side)),
        dma((2, 2)),
        dma((2, n_narrow)),
        dma((2, n_z)),
        dma((2, n_narrow)),
    ]
    loss, grad_a, grad_b, grads = pl.pallas_call(
        functools.partial(step_kernel, all_points),
        out_shape=out_shape,
        in_specs=[anywhere] * 2 + [vmem] * 6,
        out_specs=(vmem, anywhere, anywhere, vmem),
        scratch_shapes=scratch,
        compiler_params=pltpu.CompilerParams(
            collective_id=1, has_side_effects=True, vmem_limit_bytes=63 * 1024 * 1024
        ),
        name="step",
    )(
        feat_a.reshape(points, depth),
        feat_b.reshape(points, depth),
        w_hidden,
        w_out,
        send_rows.reshape(n_narrow, cap),
        dest_rows.reshape(n_narrow, cap),
        counts.reshape(1, n_narrow),
        neg_rows.reshape(1, neg_count),
    )
    loss, grad_a, grad_b, grad_wh, grad_wo = pl.pallas_call(
        deliver_kernel,
        out_shape=(
            jax.ShapeDtypeStruct((1, 1), F32),
            jax.ShapeDtypeStruct((points, depth), BF16),
            jax.ShapeDtypeStruct((points, depth), BF16),
            jax.ShapeDtypeStruct((depth, hidden), F32),
            jax.ShapeDtypeStruct((hidden, width), F32),
        ),
        in_specs=[vmem, anywhere, anywhere, vmem],
        out_specs=(vmem, anywhere, anywhere, vmem, vmem),
        scratch_shapes=[pltpu.VMEM((2, points, depth), BF16), dma((2, 4)), dma((2, 4))],
        compiler_params=pltpu.CompilerParams(vmem_limit_bytes=63 * 1024 * 1024),
        name="deliver",
    )(loss, grad_a, grad_b, grads)
    return (
        loss.reshape(()),
        grad_a.reshape(feat_a.shape),
        grad_b.reshape(feat_b.shape),
        grad_wh,
        grad_wo,
    )


def solution(mesh):
    placed = (
        P("wide", "narrow", None, None),
        P("wide", "narrow", None, None),
        P(),
        P(),
        P("wide", "narrow", None, None),
        P("wide", "narrow", None, None),
        P("wide", "narrow", None),
        P("wide", "narrow", None),
    )
    return jax.shard_map(
        body,
        mesh=mesh,
        in_specs=placed,
        out_specs=(P(), P("wide", "narrow", None, None), P("wide", "narrow", None, None), P(), P()),
        check_vma=False,
    )
```

```python
import functools
import math

import jax
import jax.numpy as jnp
from jax import lax
from jax.experimental import pallas as pl
from jax.experimental.pallas import tpu as pltpu
from jax.sharding import PartitionSpec as P

MESH = pl.DeviceIdType.MESH
F32 = jnp.float32
BF16 = jnp.bfloat16
TEMPERATURE = 0.07
NT = (((1,), (1,)), ((), ()))
TN = (((0,), (0,)), ((), ()))


def dot(left, right, dims=None):
    if dims is None:
        return jnp.dot(left, right, preferred_element_type=F32)
    return lax.dot_general(left, right, dims, preferred_element_type=F32)


def one_hot(mask):
    return jnp.where(mask, 1.0, 0.0).astype(F32)


def fold(values):
    rows, width = values.shape
    return jnp.sum(values.reshape(rows // 8, 8, width), axis=0)


def remote(src, dst, sems, d, device):
    return pltpu.make_async_remote_copy(
        src_ref=src,
        dst_ref=dst,
        send_sem=sems.at[0, d],
        recv_sem=sems.at[1, d],
        device_id=device,
        device_id_type=MESH,
    )


def start_all(make, count):
    for d in range(1, count):
        make(d).start()


def wait_all(make, count):
    for d in range(1, count):
        make(d).wait()


def wait_sent(make, count):
    for d in range(1, count):
        make(d).wait_send()


def step_kernel(
    all_points,
    feat_a,
    feat_b,
    w_hidden,
    w_out,
    send_row,
    dest_own,
    counts,
    neg_row,
    loss_o,
    grad_feat_a,
    grad_feat_b,
    grads_o,
    feat,
    feat_slot,
    lin,
    normed,
    embed,
    scale,
    acc,
    feat_acc,
    stat,
    near,
    part,
    far,
    total,
    stat2,
    near2,
    part2,
    far2,
    total2,
    msg,
    msg_in,
    send_col,
    dest_row,
    dest_col,
    live_col,
    query,
    negs,
    keys_in,
    expo,
    exp_sum,
    num,
    spread,
    grad_query,
    grad_out_slots,
    grad_in_slots,
    neg_out,
    low_in,
    high_in,
    low_mid,
    high_mid,
    low_end,
    high_end,
    neg_mine,
    grad_norm,
    wo_acc,
    wh_one,
    wh_two,
    loss_acc,
    grads,
    half,
    own,
    piece,
    chunk,
    stack_in,
    half_wo,
    own_wo,
    piece_wo,
    chunk_wo,
    stack_wo,
    sem_in,
    sem_out,
    sem_msg,
    sem_near,
    sem_far,
    sem_near2,
    sem_far2,
    sem_neg,
    sem_key,
    sem_grad,
    sem_negback,
    sem_pair,
    sem_piece,
    sem_stack,
    sem_gather,
):
    w = lax.axis_index("wide")
    n = lax.axis_index("narrow")
    n_wide = far.shape[0]
    n_narrow = near.shape[0]
    n_z = stack_in.shape[0]
    points, depth = feat_a.shape
    hidden = w_hidden.shape[1]
    width = w_out.shape[1]
    cap = points // n_narrow
    neg_count = neg_row.shape[1]
    block = min(512, points)
    small = min(256, points)
    blocks = points // block
    split = hidden // 2
    parts = hidden // width
    wh_first, wo_first = 0, parts * depth
    sets = (
        (half, own, piece, chunk, stack_in),
        (half_wo, own_wo, piece_wo, chunk_wo, stack_wo),
    )
    side = negs.shape[0]
    upper = neg_count // 2
    row, col = n // side, lax.rem(n, side)
    halves = (slice(0, upper), slice(upper, neg_count))

    def peer(d):
        return (w, lax.rem(n + d, n_narrow))

    def along_row(d):
        return (w, row * side + lax.rem(col + d, side))

    def along_col(d):
        return (w, lax.rem(row + d, side) * side + col)

    def source(d):
        return lax.rem(n + n_narrow - d, n_narrow)

    def across(d):
        return (lax.rem(w + d, n_wide), n)

    def rows_of(i, size):
        return pl.ds(pl.multiple_of(i * size, size), size)

    barrier = pltpu.get_barrier_semaphore()

    for d in range(1, n_narrow):
        pl.semaphore_signal(barrier, inc=1, device_id=peer(d), device_id_type=MESH)
    for d in range(1, n_wide):
        pl.semaphore_signal(barrier, inc=1, device_id=across(d), device_id_type=MESH)

    def load(v, i):
        ref = (feat_a, feat_b)[v]
        rows = rows_of(i, block)
        return pltpu.make_async_copy(ref.at[rows], feat.at[v, rows], sem_in.at[v, i])

    for v in (1, 0):
        for i in range(blocks):
            load(v, i).start()

    acc[...] = jnp.zeros_like(acc)
    feat_acc[...] = jnp.zeros_like(feat_acc)
    for v in (1, 0):

        @pl.loop(0, blocks)
        def _(i):
            load(v, i).wait()
            rows = rows_of(i, block)
            points_in = feat[v, rows, :]
            linear = dot(points_in, w_hidden[...])
            acc[2 * v] += fold(linear)
            acc[2 * v + 1] += fold(linear * linear)
            feat_acc[v] += fold(points_in.astype(F32))

    def put_sums(stat, sums):
        for r in range(4):
            stat[2 * r : 2 * r + 1, 0:split] = sums[r : r + 1, 0:split]
            stat[2 * r + 1 : 2 * r + 2, 0:split] = sums[r : r + 1, split:]

    def get_sum(total, r):
        return jnp.concatenate(
            [total[2 * r : 2 * r + 1, 0:split], total[2 * r + 1 : 2 * r + 2, 0:split]], axis=1
        )

    put_sums(stat, jnp.sum(acc[...], axis=1))

    pl.semaphore_wait(barrier, n_narrow + n_wide - 2)

    def sum_all(stat, near, part, far, total, sem_near, sem_far, between=None, later=None):
        def to_near(d):
            return remote(stat, near.at[n], sem_near, d, peer(d))

        def to_far(d):
            return remote(part, far.at[w], sem_far, d, across(d))

        start_all(to_near, n_narrow)
        near[n] = stat[...]
        if between is not None:
            between()
        wait_all(to_near, n_narrow)
        part[...] = jnp.sum(near[...], axis=0)
        start_all(to_far, n_wide)
        far[w] = part[...]
        if later is not None:
            later()
        wait_all(to_far, n_wide)
        total[...] = jnp.sum(far[...], axis=0)

    def to_msg(d):
        return remote(msg.at[lax.rem(n + d, n_narrow)], msg_in.at[n], sem_msg, d, peer(d))

    def gather(ids, table, i):
        lanes = lax.broadcasted_iota(jnp.int32, (block, points), 1)
        return dot(one_hot(ids[rows_of(i, block), :] == lanes).astype(BF16), table)

    def columns(ids, ref):
        square = jnp.concatenate(
            [ids.astype(F32), jnp.zeros((cap - n_narrow, cap), F32)], axis=0
        ).T.astype(jnp.int32)
        for s in range(n_narrow):
            ref[s * cap : (s + 1) * cap, :] = square[:, s : s + 1]

    def spread_counts():
        across_lanes = lax.broadcasted_iota(jnp.int32, (n_narrow, n_narrow), 1)
        down = lax.broadcasted_iota(jnp.int32, (n_narrow, n_narrow), 0)
        here = jnp.broadcast_to(counts[...], (n_narrow, n_narrow)).astype(F32)
        return jnp.sum(jnp.where(across_lanes == down, here, 0.0), axis=1, keepdims=True)

    def slot_order():
        count = spread_counts().astype(jnp.int32)
        line = lax.broadcasted_iota(jnp.int32, (8, cap), 0)
        for s in range(n_narrow):
            msg[s] = jnp.where(line == 0, dest_own[s : s + 1, :], count[s : s + 1, :])
        start_all(to_msg, n_narrow)
        msg_in[n] = msg[n]
        columns(send_row[...], send_col)
        to_slots(0, blocks - 1)

    def to_slots(low, high):
        @pl.loop(low, high)
        def _(i):
            feat_slot[rows_of(i, block), :] = gather(send_col, feat[1], i).astype(BF16)

    def slot_linear():
        to_slots(blocks - 1, blocks)

        @pl.loop(0, blocks)
        def _(i):
            rows = rows_of(i, block)
            lin[rows, :] = dot(feat_slot[rows, :], w_hidden[...])

        wait_all(to_msg, n_narrow)
        ids = msg_in[:, 0, :]
        dest_row[...] = ids
        columns(ids, dest_col)
        line = lax.broadcasted_iota(jnp.int32, (cap, 1), 0)
        for s in range(n_narrow):
            live_col[s * cap : (s + 1) * cap, :] = one_hot(line < msg_in[s, 1:2, 0:1])

    sum_all(stat, near, part, far, total, sem_near, sem_far, slot_order, slot_linear)

    inv_count = 1.0 / all_points
    means, inverses = [], []
    for v in range(2):
        mean = get_sum(total, 2 * v) * inv_count
        square = get_sum(total, 2 * v + 1) * inv_count
        means.append(mean)
        inverses.append(lax.rsqrt(square - mean * mean + 1e-5))

    def finish(v):
        @pl.loop(0, blocks)
        def _(i):
            rows = rows_of(i, block)
            linear = lin[rows, :] if v else dot(feat[0, rows, :], w_hidden[...])
            value = ((linear - means[v]) * inverses[v]).astype(BF16)
            normed[v, rows, :] = value
            out = dot(jnp.maximum(value, 0), w_out[...])
            unit_scale = lax.rsqrt(jnp.sum(out * out, axis=1, keepdims=True) + 1e-6)
            embed[v, rows, :] = (out * unit_scale).astype(BF16)
            scale[v, rows, :] = unit_scale

    finish(1)
    neg_col = jnp.broadcast_to(neg_row[...].astype(F32), (cap, neg_count)).T.astype(jnp.int32)
    picks = [
        one_hot(send_row[s : s + 1, :] == neg_col).astype(BF16) for s in range(n_narrow)
    ]
    negs[row, col] = dot(jnp.concatenate(picks, axis=1), embed[1]).astype(BF16)

    def neg_first(d):
        low, high = negs.at[row, col, halves[0]], negs.at[row, col, halves[1]]
        return (
            remote(low, low, sem_neg, d, along_row(d)),
            remote(high, high, sem_neg, side + d, along_col(d)),
        )

    def neg_second(d):
        low, high = negs.at[row, :, halves[0]], negs.at[:, col, halves[1]]
        return (
            remote(low, low, sem_neg, 2 * side + d, along_col(d)),
            remote(high, high, sem_neg, 3 * side + d, along_row(d)),
        )

    def start_both(make):
        for d in range(1, side):
            for copy in make(d):
                copy.start()

    def wait_both(make):
        for d in range(1, side):
            for copy in make(d):
                copy.wait()

    start_both(neg_first)

    def to_key(d):
        return remote(
            embed.at[1, rows_of(lax.rem(n + d, n_narrow), cap)],
            keys_in.at[rows_of(n, cap)],
            sem_key,
            d,
            peer(d),
        )

    finish(0)

    wait_both(neg_first)
    start_both(neg_second)
    start_all(to_key, n_narrow)
    keys_in[rows_of(n, cap), :] = embed[1, rows_of(n, cap), :]

    @pl.loop(0, blocks)
    def _(i):
        query[rows_of(i, block), :] = gather(dest_col, embed[0], i).astype(BF16)

    wh_two[...] = jnp.zeros_like(wh_two)
    wh_one[...] = jnp.zeros_like(wh_one)

    def view_rows(v, rows):
        return feat_slot[rows, :] if v else feat[0, rows, :]

    for v in range(2):

        @pl.loop(0, blocks)
        def _(i):
            rows = rows_of(i, block)
            wh_two[v] += dot(view_rows(v, rows), normed[v, rows, :], TN)

    wait_both(neg_second)
    total_negs = n_narrow * neg_count

    to_exp2 = math.log2(math.e) / TEMPERATURE

    @pl.loop(0, points // small)
    def _(i):
        rows = rows_of(i, small)
        table = negs[...].reshape(total_negs, width)
        score = dot(query[rows, :], table, NT)
        power = jnp.exp2(score * to_exp2)
        exp_sum[rows, :] = jnp.sum(power, axis=1, keepdims=True)
        power = power.astype(BF16)
        expo[rows, :] = power
        num[rows, :] = dot(power, table)

    loss_acc[...] = jnp.zeros_like(loss_acc)

    def to_slot(d):
        rows = rows_of(source(d), cap)
        return remote(
            grad_out_slots.at[rows],
            grad_in_slots.at[rows_of(n, cap)],
            sem_grad,
            d,
            (w, source(d)),
        )

    def answer(d):
        rows = rows_of(source(d), cap)
        live = live_col[rows, :]
        key = keys_in[rows, :].astype(F32)
        asked = query[rows, :].astype(F32)
        positive = jnp.sum(asked * key, axis=1, keepdims=True) * (1.0 / TEMPERATURE)
        exp_pos = jnp.exp(positive)
        denominator = exp_pos + exp_sum[rows, :]
        term = live * (jnp.log(denominator) - positive)
        weight = live * (1.0 / TEMPERATURE)
        share = weight / denominator
        pair_coeff = share * exp_pos - weight
        grad_out_slots[rows, :] = (pair_coeff * asked).astype(BF16)
        grad_query[rows, :] = (pair_coeff * key + share * num[rows, :]).astype(BF16)
        spread[:, rows] = (share * asked).T.astype(BF16)
        return jnp.sum(term, axis=0, keepdims=True)

    pair = 2

    @pl.loop(0, n_narrow // pair)
    def _(i):
        for k in range(pair):
            d = i * pair + k

            @pl.when(d > 0)
            def _():
                to_key(d).wait_recv()

        loss_acc[...] += sum(answer(i * pair + k) for k in range(pair))
        for k in range(pair):
            d = i * pair + k

            @pl.when(d > 0)
            def _():
                to_slot(d).start()

    grad_in_slots[rows_of(n, cap), :] = grad_out_slots[rows_of(n, cap), :]

    def to_owner_row(q):
        d = lax.rem(q - row + side, side)
        return remote(
            neg_out.at[q, :, halves[0]], low_in.at[row], sem_negback, d, (w, q * side + col)
        )

    def to_owner_col(d):
        q = lax.rem(col + d, side)
        return remote(
            neg_out.at[:, q, halves[1]], high_in.at[col], sem_negback, side + d, along_row(d)
        )

    def to_owner_second(d):
        return (
            remote(
                low_mid.at[lax.rem(col + d, side)],
                low_end.at[col],
                sem_negback,
                2 * side + d,
                along_row(d),
            ),
            remote(
                high_mid.at[lax.rem(row + d, side)],
                high_end.at[row],
                sem_negback,
                3 * side + d,
                along_col(d),
            ),
        )

    @pl.loop(1, side + 1)
    def _(i):
        q = lax.rem(row + i, side)
        cols = rows_of(q, side * neg_count)
        neg_out[q] = (
            dot(spread[...], expo[:, cols]).T.astype(BF16).reshape(side, neg_count, width)
        )

        @pl.when(i < side)
        def _():
            to_owner_row(q).start()

    start_all(to_owner_col, side)
    low_in[row] = neg_out[row, :, halves[0]]
    high_in[col] = neg_out[:, col, halves[1]]

    def pass_on():
        @pl.loop(1, side)
        def _(i):
            to_owner_row(lax.rem(row + i, side)).wait()

        wait_all(to_owner_col, side)
        low_mid[...] = jnp.sum(low_in[...].astype(F32), axis=0).astype(BF16)
        high_mid[...] = jnp.sum(high_in[...].astype(F32), axis=0).astype(BF16)
        start_both(to_owner_second)
        low_end[col] = low_mid[col]
        high_end[row] = high_mid[row]

    def rows_one_hot(row_ids, i, size):
        place = lax.broadcasted_iota(jnp.int32, (size, cap), 0) + i * size
        picks = [
            one_hot(row_ids[s : s + 1, :] == place).astype(BF16) for s in range(n_narrow)
        ]
        return jnp.concatenate(picks, axis=1)

    acc[...] = jnp.zeros_like(acc)
    wo_acc[...] = jnp.zeros_like(wo_acc)

    def back_top(v, grad_embed):
        @pl.loop(0, blocks)
        def _(i):
            rows = rows_of(i, block)
            grad = grad_embed(i, rows)
            unit = embed[v, rows, :].astype(F32)
            inner = jnp.sum(unit * grad, axis=1, keepdims=True)
            grad_out = (scale[v, rows, :] * (grad - unit * inner)).astype(BF16)
            value = normed[v, rows, :]
            wo_acc[...] += dot(grad_out, jnp.maximum(value, 0), TN)
            value = value.astype(F32)
            grad_act = jnp.where(value > 0, dot(grad_out, w_out[...], NT), 0.0)
            acc[2 * v] += fold(grad_act)
            acc[2 * v + 1] += fold(grad_act * value)
            grad_norm[v, rows, :] = grad_act.astype(BF16)

    def first_product(v):
        @pl.loop(0, blocks)
        def _(i):
            rows = rows_of(i, block)
            wh_one[v] += dot(view_rows(v, rows), grad_norm[v, rows, :], TN)

    back_top(0, lambda i, rows: dot(rows_one_hot(dest_row, i, block), grad_query[...]))
    pass_on()
    first_product(0)

    wait_sent(to_key, n_narrow)
    wait_all(to_slot, n_narrow)
    wait_both(to_owner_second)
    neg_mine[halves[0], :] = jnp.sum(low_end[...].astype(F32), axis=0).astype(BF16)
    neg_mine[halves[1], :] = jnp.sum(high_end[...].astype(F32), axis=0).astype(BF16)

    def grad_b(i, rows):
        mask = one_hot(send_col[rows, :] == neg_row[...]).astype(BF16)
        return grad_in_slots[rows, :].astype(F32) + dot(mask, neg_mine[...])

    back_top(1, grad_b)

    z, c = w // 2, lax.rem(w, 2)
    partner = (2 * z + 1 - c, n)

    def sum_stages(k, first):
        half, own, piece, chunk, stack_in = sets[k]
        span, rows = half.shape[0], chunk.shape[0]
        mine = pl.multiple_of(first + c * span, 16)
        other = pl.multiple_of(first + (1 - c) * span, 16)
        place = pl.ds(pl.multiple_of(mine + n * rows, 16), rows)

        def swap():
            return remote(grads.at[pl.ds(other, span)], half, sem_pair.at[k], 0, partner)

        def to_piece(d):
            return remote(
                own.at[rows_of(lax.rem(n + d, n_narrow), rows)],
                piece.at[n],
                sem_piece.at[k],
                d,
                peer(d),
            )

        def start_piece():
            own[...] = (
                grads[pl.ds(mine, span), :].astype(F32) + half[...].astype(F32)
            ).astype(BF16)
            start_all(to_piece, n_narrow)
            piece[n] = own[rows_of(n, rows), :]

        def to_stack(d):
            return remote(
                chunk,
                stack_in.at[z],
                sem_stack.at[k],
                d,
                (2 * lax.rem(z + d, n_z) + c, n),
            )

        def start_stack():
            wait_all(to_piece, n_narrow)
            chunk[...] = jnp.sum(piece[...].astype(F32), axis=0).astype(BF16)
            start_all(to_stack, n_z)
            stack_in[z] = chunk[...]

        def to_gather(d):
            return remote(grads_o.at[place], grads_o.at[place], sem_gather.at[k], d, peer(d))

        def start_gather():
            wait_all(to_stack, n_z)
            grads_o[place, :] = jnp.sum(stack_in[...].astype(F32), axis=0).astype(BF16)
            start_all(to_gather, n_narrow)

        def last():
            part = grads_o.at[pl.ds(mine, span)]
            return remote(part, part, sem_pair.at[k], 1, partner)

        def start_last():
            wait_all(to_gather, n_narrow)
            last().start()

        def finish_last():
            last().wait()

        return swap, start_piece, start_stack, start_gather, start_last, finish_last

    grads[wo_first:, :] = wo_acc[...].T.astype(BF16)
    send_wo = sum_stages(1, wo_first)
    send_wo[0]().start()

    def wo_piece():
        send_wo[0]().wait()
        send_wo[1]()
        first_product(1)

    put_sums(stat2, jnp.sum(acc[...], axis=1))
    stat2[0:1, split:] = loss_acc[0:1, :]
    stat2[1:8, split:] = jnp.broadcast_to(
        jnp.sum(spread_counts(), axis=0, keepdims=True), (7, cap)
    )
    sum_all(
        stat2,
        near2,
        part2,
        far2,
        total2,
        sem_near2,
        sem_far2,
        wo_piece,
        send_wo[2],
    )

    pair_total = total2[1:2, split : split + 1]
    grad_weight = all_points / pair_total
    loss_o[0:1, :] = total2[0:1, split:] / pair_total
    mean_grads = [get_sum(total2, 2 * v) * inv_count for v in range(2)]
    mean_crosses = [get_sum(total2, 2 * v + 1) * inv_count for v in range(2)]
    scales = [inverses[v] * grad_weight for v in range(2)]
    loss_o[1:2, :] = jnp.broadcast_to(grad_weight, (1, cap))
    totals = [jnp.sum(feat_acc[v], axis=0, keepdims=True) for v in range(2)]
    downs = [jnp.broadcast_to(row, (8, depth)).T[:, 0:1] for row in totals]
    for p in range(parts):
        cols = slice(p * width, (p + 1) * width)
        value = sum(
            scales[v][:, cols]
            * (
                wh_one[v, :, cols]
                - downs[v] * mean_grads[v][:, cols]
                - wh_two[v, :, cols] * mean_crosses[v][:, cols]
            )
            for v in range(2)
        )
        grads[p * depth : (p + 1) * depth, :] = value.astype(BF16)

    def store(v, i):
        ref = (grad_feat_a, grad_feat_b)[v]
        rows = rows_of(i, block)
        return pltpu.make_async_copy(normed.at[v, rows], ref.at[rows], sem_out.at[v, i])

    def feat_grad(v):
        @pl.loop(0, blocks)
        def _(i):
            rows = rows_of(i, block)
            grad = grad_norm[v, rows, :].astype(F32)
            value = normed[v, rows, :].astype(F32)
            grad = scales[v] * (grad - mean_grads[v] - value * mean_crosses[v])
            out = dot(grad.astype(BF16), w_hidden[...], NT).astype(BF16)
            if v:
                feat_slot[rows, :] = out
            else:
                normed[v, rows, :] = out
                store(v, i).start()

    def row_order():
        @pl.loop(0, blocks)
        def _(i):
            picks = rows_one_hot(send_row, i, block)
            normed[1, rows_of(i, block), :] = dot(picks, feat_slot[...]).astype(BF16)
            store(1, i).start()

    send_wh = sum_stages(0, wh_first)
    swap = send_wh[0]()
    swap.start()
    swap.wait()
    send_wh[1]()
    feat_grad(0)
    send_wh[2]()
    feat_grad(1)
    send_wo[3]()
    send_wh[3]()
    row_order()
    send_wo[4]()
    send_wh[4]()
    for v in range(2):
        for i in range(blocks):
            store(v, i).wait()
    send_wo[5]()
    send_wh[5]()


def deliver_kernel(
    loss, grad_a, grad_b, grads, loss_o, out_a, out_b, out_wh, out_wo, held, read_sem, write_sem
):
    pieces = read_sem.shape[1]
    rows = grad_a.shape[0] // pieces
    reads, writes = [], []
    for v, (src, dst) in enumerate(((grad_a, out_a), (grad_b, out_b))):
        for i in range(pieces):
            part = pl.ds(i * rows, rows)
            middle = held.at[v, part]
            reads.append(pltpu.make_async_copy(src.at[part], middle, read_sem.at[v, i]))
            writes.append(pltpu.make_async_copy(middle, dst.at[part], write_sem.at[v, i]))
    for copy in reads:
        copy.start()
    for arrived, copy in zip(reads, writes):
        arrived.wait()
        copy.start()
    depth, hidden = out_wh.shape
    width = out_wo.shape[1]
    for p in range(hidden // width):
        out_wh[:, p * width : (p + 1) * width] = grads[p * depth : (p + 1) * depth, :].astype(F32)
    out_wo[...] = grads[hidden // width * depth :, :].astype(F32) * loss[1:2, 0:1]
    loss_o[...] = loss[0:1, 0:1]
    for copy in writes:
        copy.wait()

def body(feat_a, feat_b, w_hidden, w_out, send_rows, dest_rows, counts, neg_rows):
    points, depth = feat_a.shape[2:]
    hidden, width = w_out.shape
    n_wide, n_narrow = lax.axis_size("wide"), lax.axis_size("narrow")
    n_z = n_wide // 2
    side = math.isqrt(n_narrow)
    cap = send_rows.shape[3]
    neg_count = neg_rows.shape[2]
    total_negs = n_narrow * neg_count
    all_points = float(n_wide * n_narrow * points)
    blocks = points // min(512, points)
    stat = (8, hidden // 2)
    stat2 = (8, hidden // 2 + cap)
    grad_total = depth * hidden // width + hidden
    wh_rows = depth * hidden // width

    def sum_scratch(total):
        span = total // 2
        rows = span // n_narrow
        return (
            pltpu.VMEM((span, width), BF16),
            pltpu.VMEM((span, width), BF16),
            pltpu.VMEM((n_narrow, rows, width), BF16),
            pltpu.VMEM((rows, width), BF16),
            pltpu.VMEM((n_z, rows, width), BF16),
        )

    vmem = pl.BlockSpec(memory_space=pltpu.VMEM)
    anywhere = pl.BlockSpec(memory_space=pl.ANY)
    dma = pltpu.SemaphoreType.DMA
    out_shape = (
        jax.ShapeDtypeStruct((8, cap), F32),
        jax.ShapeDtypeStruct((points, depth), BF16),
        jax.ShapeDtypeStruct((points, depth), BF16),
        jax.ShapeDtypeStruct((grad_total, width), BF16),
    )
    scratch = [
        pltpu.VMEM((2, points, depth), BF16),
        pltpu.VMEM((points, depth), BF16),
        pltpu.VMEM((points, hidden), F32),
        pltpu.VMEM((2, points, hidden), BF16),
        pltpu.VMEM((2, points, width), BF16),
        pltpu.VMEM((2, points, 1), F32),
        pltpu.VMEM((4, 8, hidden), F32),
        pltpu.VMEM((2, 8, depth), F32),
        pltpu.VMEM(stat, F32),
        pltpu.VMEM((n_narrow,) + stat, F32),
        pltpu.VMEM(stat, F32),
        pltpu.VMEM((n_wide,) + stat, F32),
        pltpu.VMEM(stat, F32),
        pltpu.VMEM(stat2, F32),
        pltpu.VMEM((n_narrow,) + stat2, F32),
        pltpu.VMEM(stat2, F32),
        pltpu.VMEM((n_wide,) + stat2, F32),
        pltpu.VMEM(stat2, F32),
        pltpu.VMEM((n_narrow, 8, cap), jnp.int32),
        pltpu.VMEM((n_narrow, 8, cap), jnp.int32),
        pltpu.VMEM((points, 1), jnp.int32),
        pltpu.VMEM((n_narrow, cap), jnp.int32),
        pltpu.VMEM((points, 1), jnp.int32),
        pltpu.VMEM((points, 1), F32),
        pltpu.VMEM((points, width), BF16),
        pltpu.VMEM((side, side, neg_count, width), BF16),
        pltpu.VMEM((points, width), BF16),
        pltpu.VMEM((points, total_negs), BF16),
        pltpu.VMEM((points, 1), F32),
        pltpu.VMEM((points, width), F32),
        pltpu.VMEM((width, points), BF16),
        pltpu.VMEM((points, width), BF16),
        pltpu.VMEM((points, width), BF16),
        pltpu.VMEM((points, width), BF16),
        pltpu.VMEM((side, side, neg_count, width), BF16),
        pltpu.VMEM((side, side, neg_count // 2, width), BF16),
        pltpu.VMEM((side, side, neg_count // 2, width), BF16),
        pltpu.VMEM((side, neg_count // 2, width), BF16),
        pltpu.VMEM((side, neg_count // 2, width), BF16),
        pltpu.VMEM((side, neg_count // 2, width), BF16),
        pltpu.VMEM((side, neg_count // 2, width), BF16),
        pltpu.VMEM((neg_count, width), BF16),
        pltpu.VMEM((2, points, hidden), BF16),
        pltpu.VMEM((width, hidden), F32),
        pltpu.VMEM((2, depth, hidden), F32),
        pltpu.VMEM((2, depth, hidden), F32),
        pltpu.VMEM((8, cap), F32),
        pltpu.VMEM((grad_total, width), BF16),
        *sum_scratch(wh_rows),
        *sum_scratch(hidden),
        dma((2, blocks)),
        dma((2, blocks)),
        dma((2, n_narrow)),
        dma((2, n_narrow)),
        dma((2, n_wide)),
        dma((2, n_narrow)),
        dma((2, n_wide)),
        dma((2, 4 * side)),
        dma((2, n_narrow)),
        dma((2, n_narrow)),
        dma((2, 4 * side)),
        dma((2, 2, 2)),
        dma((2, 2, n_narrow)),
        dma((2, 2, n_z)),
        dma((2, 2, n_narrow)),
    ]
    loss, grad_a, grad_b, grads = pl.pallas_call(
        functools.partial(step_kernel, all_points),
        out_shape=out_shape,
        in_specs=[anywhere] * 2 + [vmem] * 6,
        out_specs=(vmem, anywhere, anywhere, vmem),
        scratch_shapes=scratch,
        compiler_params=pltpu.CompilerParams(
            collective_id=1, has_side_effects=True, vmem_limit_bytes=63 * 1024 * 1024
        ),
        name="step",
    )(
        feat_a.reshape(points, depth),
        feat_b.reshape(points, depth),
        w_hidden,
        w_out,
        send_rows.reshape(n_narrow, cap),
        dest_rows.reshape(n_narrow, cap),
        counts.reshape(1, n_narrow),
        neg_rows.reshape(1, neg_count),
    )
    loss, grad_a, grad_b, grad_wh, grad_wo = pl.pallas_call(
        deliver_kernel,
        out_shape=(
            jax.ShapeDtypeStruct((1, 1), F32),
            jax.ShapeDtypeStruct((points, depth), BF16),
            jax.ShapeDtypeStruct((points, depth), BF16),
            jax.ShapeDtypeStruct((depth, hidden), F32),
            jax.ShapeDtypeStruct((hidden, width), F32),
        ),
        in_specs=[vmem, anywhere, anywhere, vmem],
        out_specs=(vmem, anywhere, anywhere, vmem, vmem),
        scratch_shapes=[pltpu.VMEM((2, points, depth), BF16), dma((2, 4)), dma((2, 4))],
        compiler_params=pltpu.CompilerParams(vmem_limit_bytes=63 * 1024 * 1024),
        name="deliver",
    )(loss, grad_a, grad_b, grads)
    return (
        loss.reshape(()),
        grad_a.reshape(feat_a.shape),
        grad_b.reshape(feat_b.shape),
        grad_wh,
        grad_wo,
    )


def solution(mesh):
    placed = (
        P("wide", "narrow", None, None),
        P("wide", "narrow", None, None),
        P(),
        P(),
        P("wide", "narrow", None, None),
        P("wide", "narrow", None, None),
        P("wide", "narrow", None),
        P("wide", "narrow", None),
    )
    return jax.shard_map(
        body,
        mesh=mesh,
        in_specs=placed,
        out_specs=(P(), P("wide", "narrow", None, None), P("wide", "narrow", None, None), P(), P()),
        check_vma=False,
    )
```

```python
import functools
import math

import jax
import jax.numpy as jnp
from jax import lax
from jax.experimental import pallas as pl
from jax.experimental.pallas import tpu as pltpu
from jax.sharding import PartitionSpec as P

MESH = pl.DeviceIdType.MESH
F32 = jnp.float32
BF16 = jnp.bfloat16
TEMPERATURE = 0.07
NT = (((1,), (1,)), ((), ()))
TN = (((0,), (0,)), ((), ()))


def dot(left, right, dims=None):
    if dims is None:
        return jnp.dot(left, right, preferred_element_type=F32)
    return lax.dot_general(left, right, dims, preferred_element_type=F32)


def one_hot(mask):
    return jnp.where(mask, 1.0, 0.0).astype(F32)


def fold(values):
    rows, width = values.shape
    return jnp.sum(values.reshape(rows // 8, 8, width), axis=0)


def remote(src, dst, sems, d, device):
    return pltpu.make_async_remote_copy(
        src_ref=src,
        dst_ref=dst,
        send_sem=sems.at[0, d],
        recv_sem=sems.at[1, d],
        device_id=device,
        device_id_type=MESH,
    )


def start_all(make, count):
    for d in range(1, count):
        make(d).start()


def wait_all(make, count):
    for d in range(1, count):
        make(d).wait()


def wait_sent(make, count):
    for d in range(1, count):
        make(d).wait_send()


def step_kernel(
    all_points,
    feat_a,
    feat_b,
    w_hidden_in,
    w_out_in,
    send_in,
    dest_in,
    counts_in,
    neg_in,
    loss_out,
    grad_feat_a,
    grad_feat_b,
    grads_out,
    w_hidden,
    w_out,
    send_row,
    dest_own,
    counts,
    neg_row,
    loss_o,
    grads_o,
    feat,
    feat_slot,
    lin,
    normed,
    embed,
    scale,
    acc,
    feat_acc,
    stat,
    near,
    part,
    far,
    total,
    stat2,
    near2,
    part2,
    far2,
    total2,
    msg,
    msg_in,
    send_col,
    dest_row,
    dest_col,
    live_col,
    query,
    negs,
    keys_in,
    expo,
    exp_sum,
    num,
    spread,
    grad_query,
    grad_out_slots,
    grad_in_slots,
    neg_out,
    low_in,
    high_in,
    low_mid,
    high_mid,
    low_end,
    high_end,
    neg_mine,
    grad_norm,
    wo_acc,
    wh_one,
    wh_two,
    loss_acc,
    grads,
    half,
    own,
    piece,
    chunk,
    stack_in,
    half_wo,
    own_wo,
    piece_wo,
    chunk_wo,
    stack_wo,
    sem_small,
    sem_result,
    sem_in,
    sem_out,
    sem_msg,
    sem_near,
    sem_far,
    sem_near2,
    sem_far2,
    sem_neg,
    sem_key,
    sem_grad,
    sem_negback,
    sem_pair,
    sem_piece,
    sem_stack,
    sem_gather,
):
    w = lax.axis_index("wide")
    n = lax.axis_index("narrow")
    n_wide = far.shape[0]
    n_narrow = near.shape[0]
    n_z = stack_in.shape[0]
    points, depth = feat_a.shape
    hidden = w_hidden.shape[1]
    width = w_out.shape[1]
    cap = points // n_narrow
    neg_count = neg_row.shape[1]
    block = min(512, points)
    small = min(256, points)
    blocks = points // block
    split = hidden // 2
    parts = hidden // width
    wh_first, wo_first = 0, parts * depth
    sets = (
        (half, own, piece, chunk, stack_in),
        (half_wo, own_wo, piece_wo, chunk_wo, stack_wo),
    )
    side = negs.shape[0]
    upper = neg_count // 2
    row, col = n // side, lax.rem(n, side)
    halves = (slice(0, upper), slice(upper, neg_count))

    def peer(d):
        return (w, lax.rem(n + d, n_narrow))

    def along_row(d):
        return (w, row * side + lax.rem(col + d, side))

    def along_col(d):
        return (w, lax.rem(row + d, side) * side + col)

    def source(d):
        return lax.rem(n + n_narrow - d, n_narrow)

    def across(d):
        return (lax.rem(w + d, n_wide), n)

    def rows_of(i, size):
        return pl.ds(pl.multiple_of(i * size, size), size)

    barrier = pltpu.get_barrier_semaphore()

    for d in range(1, n_narrow):
        pl.semaphore_signal(barrier, inc=1, device_id=peer(d), device_id_type=MESH)
    for d in range(1, n_wide):
        pl.semaphore_signal(barrier, inc=1, device_id=across(d), device_id_type=MESH)

    small_loads = [
        pltpu.make_async_copy(src, dst, sem_small.at[k])
        for k, (src, dst) in enumerate(
            (
                (w_hidden_in, w_hidden),
                (w_out_in, w_out),
                (send_in, send_row),
                (dest_in, dest_own),
                (counts_in, counts),
                (neg_in, neg_row),
            )
        )
    ]
    small_loads[0].start()

    def load(v, i):
        ref = (feat_a, feat_b)[v]
        rows = rows_of(i, block)
        return pltpu.make_async_copy(ref.at[rows], feat.at[v, rows], sem_in.at[v, i])

    for v in (1, 0):
        for i in range(blocks):
            load(v, i).start()
    for copy in small_loads[1:]:
        copy.start()
    small_loads[0].wait()

    acc[...] = jnp.zeros_like(acc)
    feat_acc[...] = jnp.zeros_like(feat_acc)
    for v in (1, 0):

        @pl.loop(0, blocks)
        def _(i):
            load(v, i).wait()
            rows = rows_of(i, block)
            points_in = feat[v, rows, :]
            linear = dot(points_in, w_hidden[...])
            acc[2 * v] += fold(linear)
            acc[2 * v + 1] += fold(linear * linear)
            feat_acc[v] += fold(points_in.astype(F32))

    def put_sums(stat, sums):
        for r in range(4):
            stat[2 * r : 2 * r + 1, 0:split] = sums[r : r + 1, 0:split]
            stat[2 * r + 1 : 2 * r + 2, 0:split] = sums[r : r + 1, split:]

    def get_sum(total, r):
        return jnp.concatenate(
            [total[2 * r : 2 * r + 1, 0:split], total[2 * r + 1 : 2 * r + 2, 0:split]], axis=1
        )

    for copy in small_loads[1:]:
        copy.wait()
    put_sums(stat, jnp.sum(acc[...], axis=1))

    pl.semaphore_wait(barrier, n_narrow + n_wide - 2)

    def sum_all(stat, near, part, far, total, sem_near, sem_far, between=None, later=None):
        def to_near(d):
            return remote(stat, near.at[n], sem_near, d, peer(d))

        def to_far(d):
            return remote(part, far.at[w], sem_far, d, across(d))

        start_all(to_near, n_narrow)
        near[n] = stat[...]
        if between is not None:
            between()
        wait_all(to_near, n_narrow)
        part[...] = jnp.sum(near[...], axis=0)
        start_all(to_far, n_wide)
        far[w] = part[...]
        if later is not None:
            later()
        wait_all(to_far, n_wide)
        total[...] = jnp.sum(far[...], axis=0)

    def to_msg(d):
        return remote(msg.at[lax.rem(n + d, n_narrow)], msg_in.at[n], sem_msg, d, peer(d))

    def gather(ids, table, i):
        lanes = lax.broadcasted_iota(jnp.int32, (block, points), 1)
        return dot(one_hot(ids[rows_of(i, block), :] == lanes).astype(BF16), table)

    def columns(ids, ref):
        square = jnp.concatenate(
            [ids.astype(F32), jnp.zeros((cap - n_narrow, cap), F32)], axis=0
        ).T.astype(jnp.int32)
        for s in range(n_narrow):
            ref[s * cap : (s + 1) * cap, :] = square[:, s : s + 1]

    def spread_counts():
        across_lanes = lax.broadcasted_iota(jnp.int32, (n_narrow, n_narrow), 1)
        down = lax.broadcasted_iota(jnp.int32, (n_narrow, n_narrow), 0)
        here = jnp.broadcast_to(counts[...], (n_narrow, n_narrow)).astype(F32)
        return jnp.sum(jnp.where(across_lanes == down, here, 0.0), axis=1, keepdims=True)

    def slot_order():
        count = spread_counts().astype(jnp.int32)
        line = lax.broadcasted_iota(jnp.int32, (8, cap), 0)
        for s in range(n_narrow):
            msg[s] = jnp.where(line == 0, dest_own[s : s + 1, :], count[s : s + 1, :])
        start_all(to_msg, n_narrow)
        msg_in[n] = msg[n]
        columns(send_row[...], send_col)
        to_slots(0, blocks - 1)

    def to_slots(low, high):
        @pl.loop(low, high)
        def _(i):
            feat_slot[rows_of(i, block), :] = gather(send_col, feat[1], i).astype(BF16)

    def slot_linear():
        to_slots(blocks - 1, blocks)

        @pl.loop(0, blocks)
        def _(i):
            rows = rows_of(i, block)
            lin[rows, :] = dot(feat_slot[rows, :], w_hidden[...])

        wait_all(to_msg, n_narrow)
        ids = msg_in[:, 0, :]
        dest_row[...] = ids
        columns(ids, dest_col)
        line = lax.broadcasted_iota(jnp.int32, (cap, 1), 0)
        for s in range(n_narrow):
            live_col[s * cap : (s + 1) * cap, :] = one_hot(line < msg_in[s, 1:2, 0:1])

    sum_all(stat, near, part, far, total, sem_near, sem_far, slot_order, slot_linear)

    inv_count = 1.0 / all_points
    means, inverses = [], []
    for v in range(2):
        mean = get_sum(total, 2 * v) * inv_count
        square = get_sum(total, 2 * v + 1) * inv_count
        means.append(mean)
        inverses.append(lax.rsqrt(square - mean * mean + 1e-5))

    def finish(v):
        @pl.loop(0, blocks)
        def _(i):
            rows = rows_of(i, block)
            linear = lin[rows, :] if v else dot(feat[0, rows, :], w_hidden[...])
            value = ((linear - means[v]) * inverses[v]).astype(BF16)
            normed[v, rows, :] = value
            out = dot(jnp.maximum(value, 0), w_out[...])
            unit_scale = lax.rsqrt(jnp.sum(out * out, axis=1, keepdims=True) + 1e-6)
            embed[v, rows, :] = (out * unit_scale).astype(BF16)
            scale[v, rows, :] = unit_scale

    finish(1)
    neg_col = jnp.broadcast_to(neg_row[...].astype(F32), (cap, neg_count)).T.astype(jnp.int32)
    picks = [
        one_hot(send_row[s : s + 1, :] == neg_col).astype(BF16) for s in range(n_narrow)
    ]
    negs[row, col] = dot(jnp.concatenate(picks, axis=1), embed[1]).astype(BF16)

    def neg_first(d):
        low, high = negs.at[row, col, halves[0]], negs.at[row, col, halves[1]]
        return (
            remote(low, low, sem_neg, d, along_row(d)),
            remote(high, high, sem_neg, side + d, along_col(d)),
        )

    def neg_second(d):
        low, high = negs.at[row, :, halves[0]], negs.at[:, col, halves[1]]
        return (
            remote(low, low, sem_neg, 2 * side + d, along_col(d)),
            remote(high, high, sem_neg, 3 * side + d, along_row(d)),
        )

    def start_both(make):
        for d in range(1, side):
            for copy in make(d):
                copy.start()

    def wait_both(make):
        for d in range(1, side):
            for copy in make(d):
                copy.wait()

    start_both(neg_first)

    def to_key(d):
        return remote(
            embed.at[1, rows_of(lax.rem(n + d, n_narrow), cap)],
            keys_in.at[rows_of(n, cap)],
            sem_key,
            d,
            peer(d),
        )

    finish(0)

    wait_both(neg_first)
    start_both(neg_second)
    start_all(to_key, n_narrow)
    keys_in[rows_of(n, cap), :] = embed[1, rows_of(n, cap), :]

    @pl.loop(0, blocks)
    def _(i):
        query[rows_of(i, block), :] = gather(dest_col, embed[0], i).astype(BF16)

    wh_two[...] = jnp.zeros_like(wh_two)
    wh_one[...] = jnp.zeros_like(wh_one)

    def view_rows(v, rows):
        return feat_slot[rows, :] if v else feat[0, rows, :]

    for v in range(2):

        @pl.loop(0, blocks)
        def _(i):
            rows = rows_of(i, block)
            wh_two[v] += dot(view_rows(v, rows), normed[v, rows, :], TN)

    wait_both(neg_second)
    total_negs = n_narrow * neg_count

    to_exp2 = math.log2(math.e) / TEMPERATURE

    @pl.loop(0, points // small)
    def _(i):
        rows = rows_of(i, small)
        table = negs[...].reshape(total_negs, width)
        score = dot(query[rows, :], table, NT)
        power = jnp.exp2(score * to_exp2)
        exp_sum[rows, :] = jnp.sum(power, axis=1, keepdims=True)
        power = power.astype(BF16)
        expo[rows, :] = power
        num[rows, :] = dot(power, table)

    loss_acc[...] = jnp.zeros_like(loss_acc)

    def to_slot(d):
        rows = rows_of(source(d), cap)
        return remote(
            grad_out_slots.at[rows],
            grad_in_slots.at[rows_of(n, cap)],
            sem_grad,
            d,
            (w, source(d)),
        )

    def answer(d):
        rows = rows_of(source(d), cap)
        live = live_col[rows, :]
        key = keys_in[rows, :].astype(F32)
        asked = query[rows, :].astype(F32)
        positive = jnp.sum(asked * key, axis=1, keepdims=True) * (1.0 / TEMPERATURE)
        exp_pos = jnp.exp(positive)
        denominator = exp_pos + exp_sum[rows, :]
        term = live * (jnp.log(denominator) - positive)
        weight = live * (1.0 / TEMPERATURE)
        share = weight / denominator
        pair_coeff = share * exp_pos - weight
        grad_out_slots[rows, :] = (pair_coeff * asked).astype(BF16)
        grad_query[rows, :] = (pair_coeff * key + share * num[rows, :]).astype(BF16)
        spread[:, rows] = (share * asked).T.astype(BF16)
        return jnp.sum(term, axis=0, keepdims=True)

    pair = 2

    @pl.loop(0, n_narrow // pair)
    def _(i):
        for k in range(pair):
            d = i * pair + k

            @pl.when(d > 0)
            def _():
                to_key(d).wait_recv()

        loss_acc[...] += sum(answer(i * pair + k) for k in range(pair))
        for k in range(pair):
            d = i * pair + k

            @pl.when(d > 0)
            def _():
                to_slot(d).start()

    grad_in_slots[rows_of(n, cap), :] = grad_out_slots[rows_of(n, cap), :]

    def to_owner_row(q):
        d = lax.rem(q - row + side, side)
        return remote(
            neg_out.at[q, :, halves[0]], low_in.at[row], sem_negback, d, (w, q * side + col)
        )

    def to_owner_col(d):
        q = lax.rem(col + d, side)
        return remote(
            neg_out.at[:, q, halves[1]], high_in.at[col], sem_negback, side + d, along_row(d)
        )

    def to_owner_second(d):
        return (
            remote(
                low_mid.at[lax.rem(col + d, side)],
                low_end.at[col],
                sem_negback,
                2 * side + d,
                along_row(d),
            ),
            remote(
                high_mid.at[lax.rem(row + d, side)],
                high_end.at[row],
                sem_negback,
                3 * side + d,
                along_col(d),
            ),
        )

    @pl.loop(1, side + 1)
    def _(i):
        q = lax.rem(row + i, side)
        cols = rows_of(q, side * neg_count)
        neg_out[q] = (
            dot(spread[...], expo[:, cols]).T.astype(BF16).reshape(side, neg_count, width)
        )

        @pl.when(i < side)
        def _():
            to_owner_row(q).start()

    start_all(to_owner_col, side)
    low_in[row] = neg_out[row, :, halves[0]]
    high_in[col] = neg_out[:, col, halves[1]]

    def pass_on():
        @pl.loop(1, side)
        def _(i):
            to_owner_row(lax.rem(row + i, side)).wait()

        wait_all(to_owner_col, side)
        low_mid[...] = jnp.sum(low_in[...].astype(F32), axis=0).astype(BF16)
        high_mid[...] = jnp.sum(high_in[...].astype(F32), axis=0).astype(BF16)
        start_both(to_owner_second)
        low_end[col] = low_mid[col]
        high_end[row] = high_mid[row]

    def rows_one_hot(row_ids, i, size):
        place = lax.broadcasted_iota(jnp.int32, (size, cap), 0) + i * size
        picks = [
            one_hot(row_ids[s : s + 1, :] == place).astype(BF16) for s in range(n_narrow)
        ]
        return jnp.concatenate(picks, axis=1)

    acc[...] = jnp.zeros_like(acc)
    wo_acc[...] = jnp.zeros_like(wo_acc)

    def back_top(v, grad_embed):
        @pl.loop(0, blocks)
        def _(i):
            rows = rows_of(i, block)
            grad = grad_embed(i, rows)
            unit = embed[v, rows, :].astype(F32)
            inner = jnp.sum(unit * grad, axis=1, keepdims=True)
            grad_out = (scale[v, rows, :] * (grad - unit * inner)).astype(BF16)
            value = normed[v, rows, :]
            wo_acc[...] += dot(grad_out, jnp.maximum(value, 0), TN)
            value = value.astype(F32)
            grad_act = jnp.where(value > 0, dot(grad_out, w_out[...], NT), 0.0)
            acc[2 * v] += fold(grad_act)
            acc[2 * v + 1] += fold(grad_act * value)
            grad_norm[v, rows, :] = grad_act.astype(BF16)

    def first_product(v):
        @pl.loop(0, blocks)
        def _(i):
            rows = rows_of(i, block)
            wh_one[v] += dot(view_rows(v, rows), grad_norm[v, rows, :], TN)

    back_top(0, lambda i, rows: dot(rows_one_hot(dest_row, i, block), grad_query[...]))
    pass_on()
    first_product(0)

    wait_sent(to_key, n_narrow)
    wait_all(to_slot, n_narrow)
    wait_both(to_owner_second)
    neg_mine[halves[0], :] = jnp.sum(low_end[...].astype(F32), axis=0).astype(BF16)
    neg_mine[halves[1], :] = jnp.sum(high_end[...].astype(F32), axis=0).astype(BF16)

    def grad_b(i, rows):
        mask = one_hot(send_col[rows, :] == neg_row[...]).astype(BF16)
        return grad_in_slots[rows, :].astype(F32) + dot(mask, neg_mine[...])

    back_top(1, grad_b)

    z, c = w // 2, lax.rem(w, 2)
    partner = (2 * z + 1 - c, n)

    def sum_stages(k, first):
        half, own, piece, chunk, stack_in = sets[k]
        span, rows = half.shape[0], chunk.shape[0]
        mine = pl.multiple_of(first + c * span, 16)
        other = pl.multiple_of(first + (1 - c) * span, 16)
        place = pl.ds(pl.multiple_of(mine + n * rows, 16), rows)

        def swap():
            return remote(grads.at[pl.ds(other, span)], half, sem_pair.at[k], 0, partner)

        def to_piece(d):
            return remote(
                own.at[rows_of(lax.rem(n + d, n_narrow), rows)],
                piece.at[n],
                sem_piece.at[k],
                d,
                peer(d),
            )

        def start_piece():
            own[...] = (
                grads[pl.ds(mine, span), :].astype(F32) + half[...].astype(F32)
            ).astype(BF16)
            start_all(to_piece, n_narrow)
            piece[n] = own[rows_of(n, rows), :]

        def to_stack(d):
            return remote(
                chunk,
                stack_in.at[z],
                sem_stack.at[k],
                d,
                (2 * lax.rem(z + d, n_z) + c, n),
            )

        def start_stack():
            wait_all(to_piece, n_narrow)
            chunk[...] = jnp.sum(piece[...].astype(F32), axis=0).astype(BF16)
            start_all(to_stack, n_z)
            stack_in[z] = chunk[...]

        def to_gather(d):
            return remote(grads_o.at[place], grads_o.at[place], sem_gather.at[k], d, peer(d))

        def start_gather():
            wait_all(to_stack, n_z)
            grads_o[place, :] = jnp.sum(stack_in[...].astype(F32), axis=0).astype(BF16)
            start_all(to_gather, n_narrow)

        def last():
            part = grads_o.at[pl.ds(mine, span)]
            return remote(part, part, sem_pair.at[k], 1, partner)

        def write(k2, first):
            part = pl.ds(first, span)
            return pltpu.make_async_copy(
                grads_o.at[part], grads_out.at[part], sem_result.at[2 * k + k2]
            )

        def start_last():
            wait_all(to_gather, n_narrow)
            last().start()
            write(0, mine).start()

        def finish_last():
            last().wait()
            write(1, other).start()

        def end():
            write(0, mine).wait()
            write(1, other).wait()

        return swap, start_piece, start_stack, start_gather, start_last, finish_last, end

    grads[wo_first:, :] = wo_acc[...].T.astype(BF16)
    send_wo = sum_stages(1, wo_first)
    send_wo[0]().start()

    def wo_piece():
        send_wo[0]().wait()
        send_wo[1]()
        first_product(1)

    put_sums(stat2, jnp.sum(acc[...], axis=1))
    stat2[0:1, split:] = loss_acc[0:1, :]
    stat2[1:8, split:] = jnp.broadcast_to(
        jnp.sum(spread_counts(), axis=0, keepdims=True), (7, cap)
    )
    sum_all(
        stat2,
        near2,
        part2,
        far2,
        total2,
        sem_near2,
        sem_far2,
        wo_piece,
        send_wo[2],
    )

    pair_total = total2[1:2, split : split + 1]
    grad_weight = all_points / pair_total
    loss_o[0:1, :] = total2[0:1, split:] / pair_total
    mean_grads = [get_sum(total2, 2 * v) * inv_count for v in range(2)]
    mean_crosses = [get_sum(total2, 2 * v + 1) * inv_count for v in range(2)]
    scales = [inverses[v] * grad_weight for v in range(2)]
    loss_o[1:8, :] = jnp.broadcast_to(grad_weight, (7, cap))
    loss_write = pltpu.make_async_copy(loss_o, loss_out, sem_result.at[4])
    loss_write.start()
    totals = [jnp.sum(feat_acc[v], axis=0, keepdims=True) for v in range(2)]
    downs = [jnp.broadcast_to(row, (8, depth)).T[:, 0:1] for row in totals]
    for p in range(parts):
        cols = slice(p * width, (p + 1) * width)
        value = sum(
            scales[v][:, cols]
            * (
                wh_one[v, :, cols]
                - downs[v] * mean_grads[v][:, cols]
                - wh_two[v, :, cols] * mean_crosses[v][:, cols]
            )
            for v in range(2)
        )
        grads[p * depth : (p + 1) * depth, :] = value.astype(BF16)

    def store(v, i):
        ref = (grad_feat_a, grad_feat_b)[v]
        rows = rows_of(i, block)
        return pltpu.make_async_copy(normed.at[v, rows], ref.at[rows], sem_out.at[v, i])

    def feat_grad(v):
        @pl.loop(0, blocks)
        def _(i):
            rows = rows_of(i, block)
            grad = grad_norm[v, rows, :].astype(F32)
            value = normed[v, rows, :].astype(F32)
            grad = scales[v] * (grad - mean_grads[v] - value * mean_crosses[v])
            out = dot(grad.astype(BF16), w_hidden[...], NT).astype(BF16)
            if v:
                feat_slot[rows, :] = out
            else:
                normed[v, rows, :] = out
                store(v, i).start()

    def row_order():
        @pl.loop(0, blocks)
        def _(i):
            picks = rows_one_hot(send_row, i, block)
            normed[1, rows_of(i, block), :] = dot(picks, feat_slot[...]).astype(BF16)
            store(1, i).start()

    send_wh = sum_stages(0, wh_first)
    swap = send_wh[0]()
    swap.start()
    swap.wait()
    send_wh[1]()
    feat_grad(0)
    send_wh[2]()
    feat_grad(1)
    send_wo[3]()
    send_wh[3]()
    row_order()
    send_wo[4]()
    send_wh[4]()
    send_wo[5]()
    send_wh[5]()
    for v in range(2):
        for i in range(blocks):
            store(v, i).wait()
    send_wo[6]()
    send_wh[6]()
    loss_write.wait()


def deliver_kernel(
    loss_in,
    grad_a,
    grad_b,
    grads_in,
    loss_o,
    out_a,
    out_b,
    out_wh,
    out_wo,
    loss,
    grads,
    wh,
    wo,
    held,
    sem,
    read_sem,
    write_sem,
):
    pieces = read_sem.shape[1]
    rows = grad_a.shape[0] // pieces
    reads, writes = [], []
    for v, (src, dst) in enumerate(((grad_a, out_a), (grad_b, out_b))):
        for i in range(pieces):
            part = pl.ds(i * rows, rows)
            middle = held.at[v, part]
            reads.append(pltpu.make_async_copy(src.at[part], middle, read_sem.at[v, i]))
            writes.append(pltpu.make_async_copy(middle, dst.at[part], write_sem.at[v, i]))
    first = [
        pltpu.make_async_copy(grads_in, grads, sem.at[0]),
        pltpu.make_async_copy(loss_in, loss, sem.at[1]),
    ]
    for copy in first + reads:
        copy.start()
    for copy in first:
        copy.wait()
    depth, hidden = wh.shape
    width = wo.shape[1]
    for p in range(hidden // width):
        wh[:, p * width : (p + 1) * width] = grads[p * depth : (p + 1) * depth, :].astype(F32)
    writes.append(pltpu.make_async_copy(wh, out_wh, sem.at[2]))
    writes[-1].start()
    wo[...] = grads[hidden // width * depth :, :].astype(F32) * loss[1:2, 0:1]
    writes.append(pltpu.make_async_copy(wo, out_wo, sem.at[3]))
    writes[-1].start()
    for arrived, copy in zip(reads, writes):
        arrived.wait()
        copy.start()
    loss_o[...] = loss[0:1, 0:1]
    for copy in writes:
        copy.wait()

def body(feat_a, feat_b, w_hidden, w_out, send_rows, dest_rows, counts, neg_rows):
    points, depth = feat_a.shape[2:]
    hidden, width = w_out.shape
    n_wide, n_narrow = lax.axis_size("wide"), lax.axis_size("narrow")
    n_z = n_wide // 2
    side = math.isqrt(n_narrow)
    cap = send_rows.shape[3]
    neg_count = neg_rows.shape[2]
    total_negs = n_narrow * neg_count
    all_points = float(n_wide * n_narrow * points)
    blocks = points // min(512, points)
    stat = (8, hidden // 2)
    stat2 = (8, hidden // 2 + cap)
    grad_total = depth * hidden // width + hidden
    wh_rows = depth * hidden // width

    def sum_scratch(total):
        span = total // 2
        rows = span // n_narrow
        return (
            pltpu.VMEM((span, width), BF16),
            pltpu.VMEM((span, width), BF16),
            pltpu.VMEM((n_narrow, rows, width), BF16),
            pltpu.VMEM((rows, width), BF16),
            pltpu.VMEM((n_z, rows, width), BF16),
        )

    vmem = pl.BlockSpec(memory_space=pltpu.VMEM)
    anywhere = pl.BlockSpec(memory_space=pl.ANY)
    dma = pltpu.SemaphoreType.DMA
    out_shape = (
        jax.ShapeDtypeStruct((8, cap), F32),
        jax.ShapeDtypeStruct((points, depth), BF16),
        jax.ShapeDtypeStruct((points, depth), BF16),
        jax.ShapeDtypeStruct((grad_total, width), BF16),
    )
    scratch = [
        pltpu.VMEM((depth, hidden), BF16),
        pltpu.VMEM((hidden, width), BF16),
        pltpu.VMEM((n_narrow, cap), jnp.int32),
        pltpu.VMEM((n_narrow, cap), jnp.int32),
        pltpu.VMEM((1, n_narrow), jnp.int32),
        pltpu.VMEM((1, neg_count), jnp.int32),
        pltpu.VMEM((8, cap), F32),
        pltpu.VMEM((grad_total, width), BF16),
        pltpu.VMEM((2, points, depth), BF16),
        pltpu.VMEM((points, depth), BF16),
        pltpu.VMEM((points, hidden), F32),
        pltpu.VMEM((2, points, hidden), BF16),
        pltpu.VMEM((2, points, width), BF16),
        pltpu.VMEM((2, points, 1), F32),
        pltpu.VMEM((4, 8, hidden), F32),
        pltpu.VMEM((2, 8, depth), F32),
        pltpu.VMEM(stat, F32),
        pltpu.VMEM((n_narrow,) + stat, F32),
        pltpu.VMEM(stat, F32),
        pltpu.VMEM((n_wide,) + stat, F32),
        pltpu.VMEM(stat, F32),
        pltpu.VMEM(stat2, F32),
        pltpu.VMEM((n_narrow,) + stat2, F32),
        pltpu.VMEM(stat2, F32),
        pltpu.VMEM((n_wide,) + stat2, F32),
        pltpu.VMEM(stat2, F32),
        pltpu.VMEM((n_narrow, 8, cap), jnp.int32),
        pltpu.VMEM((n_narrow, 8, cap), jnp.int32),
        pltpu.VMEM((points, 1), jnp.int32),
        pltpu.VMEM((n_narrow, cap), jnp.int32),
        pltpu.VMEM((points, 1), jnp.int32),
        pltpu.VMEM((points, 1), F32),
        pltpu.VMEM((points, width), BF16),
        pltpu.VMEM((side, side, neg_count, width), BF16),
        pltpu.VMEM((points, width), BF16),
        pltpu.VMEM((points, total_negs), BF16),
        pltpu.VMEM((points, 1), F32),
        pltpu.VMEM((points, width), F32),
        pltpu.VMEM((width, points), BF16),
        pltpu.VMEM((points, width), BF16),
        pltpu.VMEM((points, width), BF16),
        pltpu.VMEM((points, width), BF16),
        pltpu.VMEM((side, side, neg_count, width), BF16),
        pltpu.VMEM((side, side, neg_count // 2, width), BF16),
        pltpu.VMEM((side, side, neg_count // 2, width), BF16),
        pltpu.VMEM((side, neg_count // 2, width), BF16),
        pltpu.VMEM((side, neg_count // 2, width), BF16),
        pltpu.VMEM((side, neg_count // 2, width), BF16),
        pltpu.VMEM((side, neg_count // 2, width), BF16),
        pltpu.VMEM((neg_count, width), BF16),
        pltpu.VMEM((2, points, hidden), BF16),
        pltpu.VMEM((width, hidden), F32),
        pltpu.VMEM((2, depth, hidden), F32),
        pltpu.VMEM((2, depth, hidden), F32),
        pltpu.VMEM((8, cap), F32),
        pltpu.VMEM((grad_total, width), BF16),
        *sum_scratch(wh_rows),
        *sum_scratch(hidden),
        dma((6,)),
        dma((5,)),
        dma((2, blocks)),
        dma((2, blocks)),
        dma((2, n_narrow)),
        dma((2, n_narrow)),
        dma((2, n_wide)),
        dma((2, n_narrow)),
        dma((2, n_wide)),
        dma((2, 4 * side)),
        dma((2, n_narrow)),
        dma((2, n_narrow)),
        dma((2, 4 * side)),
        dma((2, 2, 2)),
        dma((2, 2, n_narrow)),
        dma((2, 2, n_z)),
        dma((2, 2, n_narrow)),
    ]
    loss, grad_a, grad_b, grads = pl.pallas_call(
        functools.partial(step_kernel, all_points),
        out_shape=out_shape,
        in_specs=[anywhere] * 8,
        out_specs=(anywhere,) * 4,
        scratch_shapes=scratch,
        compiler_params=pltpu.CompilerParams(
            collective_id=1, has_side_effects=True, vmem_limit_bytes=63 * 1024 * 1024
        ),
        name="step",
    )(
        feat_a.reshape(points, depth),
        feat_b.reshape(points, depth),
        w_hidden,
        w_out,
        send_rows.reshape(n_narrow, cap),
        dest_rows.reshape(n_narrow, cap),
        counts.reshape(1, n_narrow),
        neg_rows.reshape(1, neg_count),
    )
    loss, grad_a, grad_b, grad_wh, grad_wo = pl.pallas_call(
        deliver_kernel,
        out_shape=(
            jax.ShapeDtypeStruct((1, 1), F32),
            jax.ShapeDtypeStruct((points, depth), BF16),
            jax.ShapeDtypeStruct((points, depth), BF16),
            jax.ShapeDtypeStruct((depth, hidden), F32),
            jax.ShapeDtypeStruct((hidden, width), F32),
        ),
        in_specs=[anywhere] * 4,
        out_specs=(vmem,) + (anywhere,) * 4,
        scratch_shapes=[
            pltpu.VMEM((8, cap), F32),
            pltpu.VMEM((grad_total, width), BF16),
            pltpu.VMEM((depth, hidden), F32),
            pltpu.VMEM((hidden, width), F32),
            pltpu.VMEM((2, points, depth), BF16),
            dma((4,)),
            dma((2, 4)),
            dma((2, 4)),
        ],
        compiler_params=pltpu.CompilerParams(vmem_limit_bytes=63 * 1024 * 1024),
        name="deliver",
    )(loss, grad_a, grad_b, grads)
    return (
        loss.reshape(()),
        grad_a.reshape(feat_a.shape),
        grad_b.reshape(feat_b.shape),
        grad_wh,
        grad_wo,
    )


def solution(mesh):
    placed = (
        P("wide", "narrow", None, None),
        P("wide", "narrow", None, None),
        P(),
        P(),
        P("wide", "narrow", None, None),
        P("wide", "narrow", None, None),
        P("wide", "narrow", None),
        P("wide", "narrow", None),
    )
    return jax.shard_map(
        body,
        mesh=mesh,
        in_specs=placed,
        out_specs=(P(), P("wide", "narrow", None, None), P("wide", "narrow", None, None), P(), P()),
        check_vma=False,
    )
```

```python
import functools
import math

import jax
import jax.numpy as jnp
from jax import lax
from jax.experimental import pallas as pl
from jax.experimental.pallas import tpu as pltpu
from jax.sharding import PartitionSpec as P

MESH = pl.DeviceIdType.MESH
F32 = jnp.float32
BF16 = jnp.bfloat16
TEMPERATURE = 0.07
NT = (((1,), (1,)), ((), ()))
TN = (((0,), (0,)), ((), ()))


def dot(left, right, dims=None):
    if dims is None:
        return jnp.dot(left, right, preferred_element_type=F32)
    return lax.dot_general(left, right, dims, preferred_element_type=F32)


def one_hot(mask):
    return jnp.where(mask, 1.0, 0.0).astype(F32)


def fold(values):
    rows, width = values.shape
    return jnp.sum(values.reshape(rows // 8, 8, width), axis=0)


def remote(src, dst, sems, d, device):
    return pltpu.make_async_remote_copy(
        src_ref=src,
        dst_ref=dst,
        send_sem=sems.at[0, d],
        recv_sem=sems.at[1, d],
        device_id=device,
        device_id_type=MESH,
    )


def start_all(make, count, order=None):
    for d in order or range(1, count):
        make(d).start()


def wait_all(make, count):
    for d in range(1, count):
        make(d).wait()


def wait_sent(make, count):
    for d in range(1, count):
        make(d).wait_send()


def step_kernel(
    all_points,
    feat_a,
    feat_b,
    w_hidden_in,
    w_out_in,
    send_in,
    dest_in,
    counts_in,
    neg_in,
    loss_out,
    grad_feat_a,
    grad_feat_b,
    grads_out,
    w_hidden,
    w_out,
    send_row,
    dest_own,
    counts,
    neg_row,
    loss_o,
    grads_o,
    feat,
    feat_slot,
    lin,
    normed,
    embed,
    scale,
    acc,
    feat_acc,
    stat,
    near,
    part,
    far,
    total,
    stat2,
    near2,
    part2,
    far2,
    total2,
    msg,
    msg_in,
    send_col,
    dest_row,
    dest_col,
    live_col,
    query,
    negs,
    keys_in,
    expo,
    exp_sum,
    num,
    spread,
    grad_query,
    grad_out_slots,
    grad_in_slots,
    neg_out,
    low_in,
    high_in,
    low_mid,
    high_mid,
    low_end,
    high_end,
    neg_mine,
    grad_norm,
    wo_acc,
    wh_one,
    wh_two,
    loss_acc,
    grads,
    half,
    own,
    piece,
    chunk,
    stack_in,
    half_wo,
    own_wo,
    piece_wo,
    chunk_wo,
    stack_wo,
    sem_small,
    sem_result,
    sem_in,
    sem_out,
    sem_msg,
    sem_near,
    sem_far,
    sem_near2,
    sem_far2,
    sem_neg,
    sem_key,
    sem_grad,
    sem_negback,
    sem_pair,
    sem_piece,
    sem_stack,
    sem_gather,
):
    w = lax.axis_index("wide")
    n = lax.axis_index("narrow")
    n_wide = far.shape[0]
    n_narrow = near.shape[0]
    n_z = stack_in.shape[0]
    points, depth = feat_a.shape
    hidden = w_hidden.shape[1]
    width = w_out.shape[1]
    cap = points // n_narrow
    neg_count = neg_row.shape[1]
    block = min(512, points)
    small = min(256, points)
    blocks = points // block
    split = hidden // 2
    parts = hidden // width
    wh_first, wo_first = 0, parts * depth
    sets = (
        (half, own, piece, chunk, stack_in),
        (half_wo, own_wo, piece_wo, chunk_wo, stack_wo),
    )
    side = negs.shape[0]
    upper = neg_count // 2
    row, col = n // side, lax.rem(n, side)
    halves = (slice(0, upper), slice(upper, neg_count))

    def steps(d):
        if isinstance(d, int):
            return d // side, d % side
        return lax.div(d, side), lax.rem(d, side)

    def hops(d):
        return sum(min(k, side - k) for k in steps(d))

    far_first = sorted(range(1, n_narrow), key=hops, reverse=True)

    def target(d):
        down, right = steps(d)
        return lax.rem(row + down, side) * side + lax.rem(col + right, side)

    def peer(d):
        return (w, target(d))

    def along_row(d):
        return (w, row * side + lax.rem(col + d, side))

    def along_col(d):
        return (w, lax.rem(row + d, side) * side + col)

    def source(d):
        down, right = steps(d)
        return lax.rem(row + side - down, side) * side + lax.rem(col + side - right, side)

    def across(d):
        return (lax.rem(w + d, n_wide), n)

    def rows_of(i, size):
        return pl.ds(pl.multiple_of(i * size, size), size)

    barrier = pltpu.get_barrier_semaphore()

    for d in range(1, n_narrow):
        pl.semaphore_signal(barrier, inc=1, device_id=peer(d), device_id_type=MESH)
    for d in range(1, n_wide):
        pl.semaphore_signal(barrier, inc=1, device_id=across(d), device_id_type=MESH)

    small_loads = [
        pltpu.make_async_copy(src, dst, sem_small.at[k])
        for k, (src, dst) in enumerate(
            (
                (w_hidden_in, w_hidden),
                (w_out_in, w_out),
                (send_in, send_row),
                (dest_in, dest_own),
                (counts_in, counts),
                (neg_in, neg_row),
            )
        )
    ]
    small_loads[0].start()

    def load(v, i):
        ref = (feat_a, feat_b)[v]
        rows = rows_of(i, block)
        return pltpu.make_async_copy(ref.at[rows], feat.at[v, rows], sem_in.at[v, i])

    for v in (1, 0):
        for i in range(blocks):
            load(v, i).start()
    for copy in small_loads[1:]:
        copy.start()
    small_loads[0].wait()

    acc[...] = jnp.zeros_like(acc)
    feat_acc[...] = jnp.zeros_like(feat_acc)
    for v in (1, 0):

        @pl.loop(0, blocks)
        def _(i):
            load(v, i).wait()
            rows = rows_of(i, block)
            points_in = feat[v, rows, :]
            linear = dot(points_in, w_hidden[...])
            acc[2 * v] += fold(linear)
            acc[2 * v + 1] += fold(linear * linear)
            feat_acc[v] += fold(points_in.astype(F32))

    def put_sums(stat, sums):
        for r in range(4):
            stat[2 * r : 2 * r + 1, 0:split] = sums[r : r + 1, 0:split]
            stat[2 * r + 1 : 2 * r + 2, 0:split] = sums[r : r + 1, split:]

    def get_sum(total, r):
        return jnp.concatenate(
            [total[2 * r : 2 * r + 1, 0:split], total[2 * r + 1 : 2 * r + 2, 0:split]], axis=1
        )

    for copy in small_loads[1:]:
        copy.wait()
    put_sums(stat, jnp.sum(acc[...], axis=1))

    pl.semaphore_wait(barrier, n_narrow + n_wide - 2)

    def sum_all(stat, near, part, far, total, sem_near, sem_far, between=None, later=None):
        def to_near(d):
            return remote(stat, near.at[n], sem_near, d, peer(d))

        def to_far(d):
            return remote(part, far.at[w], sem_far, d, across(d))

        start_all(to_near, n_narrow, far_first)
        near[n] = stat[...]
        if between is not None:
            between()
        wait_all(to_near, n_narrow)
        part[...] = jnp.sum(near[...], axis=0)
        start_all(to_far, n_wide)
        far[w] = part[...]
        if later is not None:
            later()
        wait_all(to_far, n_wide)
        total[...] = jnp.sum(far[...], axis=0)

    def to_msg(d):
        return remote(msg.at[target(d)], msg_in.at[n], sem_msg, d, peer(d))

    def gather(ids, table, i):
        lanes = lax.broadcasted_iota(jnp.int32, (block, points), 1)
        return dot(one_hot(ids[rows_of(i, block), :] == lanes).astype(BF16), table)

    def columns(ids, ref):
        square = jnp.concatenate(
            [ids.astype(F32), jnp.zeros((cap - n_narrow, cap), F32)], axis=0
        ).T.astype(jnp.int32)
        for s in range(n_narrow):
            ref[s * cap : (s + 1) * cap, :] = square[:, s : s + 1]

    def spread_counts():
        across_lanes = lax.broadcasted_iota(jnp.int32, (n_narrow, n_narrow), 1)
        down = lax.broadcasted_iota(jnp.int32, (n_narrow, n_narrow), 0)
        here = jnp.broadcast_to(counts[...], (n_narrow, n_narrow)).astype(F32)
        return jnp.sum(jnp.where(across_lanes == down, here, 0.0), axis=1, keepdims=True)

    def slot_order():
        count = spread_counts().astype(jnp.int32)
        line = lax.broadcasted_iota(jnp.int32, (8, cap), 0)
        for s in range(n_narrow):
            msg[s] = jnp.where(line == 0, dest_own[s : s + 1, :], count[s : s + 1, :])
        start_all(to_msg, n_narrow, far_first)
        msg_in[n] = msg[n]
        columns(send_row[...], send_col)
        to_slots(0, blocks - 1)

    def to_slots(low, high):
        @pl.loop(low, high)
        def _(i):
            feat_slot[rows_of(i, block), :] = gather(send_col, feat[1], i).astype(BF16)

    def slot_linear():
        to_slots(blocks - 1, blocks)

        @pl.loop(0, blocks)
        def _(i):
            rows = rows_of(i, block)
            lin[rows, :] = dot(feat_slot[rows, :], w_hidden[...])

        wait_all(to_msg, n_narrow)
        ids = msg_in[:, 0, :]
        dest_row[...] = ids
        columns(ids, dest_col)
        line = lax.broadcasted_iota(jnp.int32, (cap, 1), 0)
        for s in range(n_narrow):
            live_col[s * cap : (s + 1) * cap, :] = one_hot(line < msg_in[s, 1:2, 0:1])

    sum_all(stat, near, part, far, total, sem_near, sem_far, slot_order, slot_linear)

    inv_count = 1.0 / all_points
    means, inverses = [], []
    for v in range(2):
        mean = get_sum(total, 2 * v) * inv_count
        square = get_sum(total, 2 * v + 1) * inv_count
        means.append(mean)
        inverses.append(lax.rsqrt(square - mean * mean + 1e-5))

    def finish(v):
        @pl.loop(0, blocks)
        def _(i):
            rows = rows_of(i, block)
            linear = lin[rows, :] if v else dot(feat[0, rows, :], w_hidden[...])
            value = ((linear - means[v]) * inverses[v]).astype(BF16)
            normed[v, rows, :] = value
            out = dot(jnp.maximum(value, 0), w_out[...])
            unit_scale = lax.rsqrt(jnp.sum(out * out, axis=1, keepdims=True) + 1e-6)
            embed[v, rows, :] = (out * unit_scale).astype(BF16)
            scale[v, rows, :] = unit_scale

    finish(1)
    neg_col = jnp.broadcast_to(neg_row[...].astype(F32), (cap, neg_count)).T.astype(jnp.int32)
    picks = [
        one_hot(send_row[s : s + 1, :] == neg_col).astype(BF16) for s in range(n_narrow)
    ]
    negs[row, col] = dot(jnp.concatenate(picks, axis=1), embed[1]).astype(BF16)

    def neg_first(d):
        low, high = negs.at[row, col, halves[0]], negs.at[row, col, halves[1]]
        return (
            remote(low, low, sem_neg, d, along_row(d)),
            remote(high, high, sem_neg, side + d, along_col(d)),
        )

    def neg_second(d):
        low, high = negs.at[row, :, halves[0]], negs.at[:, col, halves[1]]
        return (
            remote(low, low, sem_neg, 2 * side + d, along_col(d)),
            remote(high, high, sem_neg, 3 * side + d, along_row(d)),
        )

    def start_both(make):
        for d in range(1, side):
            for copy in make(d):
                copy.start()

    def wait_both(make):
        for d in range(1, side):
            for copy in make(d):
                copy.wait()

    start_both(neg_first)

    def to_key(d):
        return remote(
            embed.at[1, rows_of(target(d), cap)],
            keys_in.at[rows_of(n, cap)],
            sem_key,
            d,
            peer(d),
        )

    finish(0)

    wait_both(neg_first)
    start_both(neg_second)
    start_all(to_key, n_narrow, far_first)
    keys_in[rows_of(n, cap), :] = embed[1, rows_of(n, cap), :]

    @pl.loop(0, blocks)
    def _(i):
        query[rows_of(i, block), :] = gather(dest_col, embed[0], i).astype(BF16)

    wh_two[...] = jnp.zeros_like(wh_two)
    wh_one[...] = jnp.zeros_like(wh_one)

    def view_rows(v, rows):
        return feat_slot[rows, :] if v else feat[0, rows, :]

    for v in range(2):

        @pl.loop(0, blocks)
        def _(i):
            rows = rows_of(i, block)
            wh_two[v] += dot(view_rows(v, rows), normed[v, rows, :], TN)

    wait_both(neg_second)
    total_negs = n_narrow * neg_count

    to_exp2 = math.log2(math.e) / TEMPERATURE

    @pl.loop(0, points // small)
    def _(i):
        rows = rows_of(i, small)
        table = negs[...].reshape(total_negs, width)
        score = dot(query[rows, :], table, NT)
        power = jnp.exp2(score * to_exp2)
        exp_sum[rows, :] = jnp.sum(power, axis=1, keepdims=True)
        power = power.astype(BF16)
        expo[rows, :] = power
        num[rows, :] = dot(power, table)

    loss_acc[...] = jnp.zeros_like(loss_acc)

    def to_slot(d):
        rows = rows_of(source(d), cap)
        return remote(
            grad_out_slots.at[rows],
            grad_in_slots.at[rows_of(n, cap)],
            sem_grad,
            d,
            (w, source(d)),
        )

    def answer(d):
        rows = rows_of(source(d), cap)
        live = live_col[rows, :]
        key = keys_in[rows, :].astype(F32)
        asked = query[rows, :].astype(F32)
        positive = jnp.sum(asked * key, axis=1, keepdims=True) * (1.0 / TEMPERATURE)
        exp_pos = jnp.exp(positive)
        denominator = exp_pos + exp_sum[rows, :]
        term = live * (jnp.log(denominator) - positive)
        weight = live * (1.0 / TEMPERATURE)
        share = weight / denominator
        pair_coeff = share * exp_pos - weight
        grad_out_slots[rows, :] = (pair_coeff * asked).astype(BF16)
        grad_query[rows, :] = (pair_coeff * key + share * num[rows, :]).astype(BF16)
        spread[:, rows] = (share * asked).T.astype(BF16)
        return jnp.sum(term, axis=0, keepdims=True)

    pair = 2

    @pl.loop(0, n_narrow // pair)
    def _(i):
        for k in range(pair):
            d = i * pair + k

            @pl.when(d > 0)
            def _():
                to_key(d).wait_recv()

        loss_acc[...] += sum(answer(i * pair + k) for k in range(pair))
        for k in range(pair):
            d = i * pair + k

            @pl.when(d > 0)
            def _():
                to_slot(d).start()

    grad_in_slots[rows_of(n, cap), :] = grad_out_slots[rows_of(n, cap), :]

    def to_owner_row(q):
        d = lax.rem(q - row + side, side)
        return remote(
            neg_out.at[q, :, halves[0]], low_in.at[row], sem_negback, d, (w, q * side + col)
        )

    def to_owner_col(d):
        q = lax.rem(col + d, side)
        return remote(
            neg_out.at[:, q, halves[1]], high_in.at[col], sem_negback, side + d, along_row(d)
        )

    def to_owner_second(d):
        return (
            remote(
                low_mid.at[lax.rem(col + d, side)],
                low_end.at[col],
                sem_negback,
                2 * side + d,
                along_row(d),
            ),
            remote(
                high_mid.at[lax.rem(row + d, side)],
                high_end.at[row],
                sem_negback,
                3 * side + d,
                along_col(d),
            ),
        )

    @pl.loop(1, side + 1)
    def _(i):
        q = lax.rem(row + i, side)
        cols = rows_of(q, side * neg_count)
        neg_out[q] = (
            dot(spread[...], expo[:, cols]).T.astype(BF16).reshape(side, neg_count, width)
        )

        @pl.when(i < side)
        def _():
            to_owner_row(q).start()

    start_all(to_owner_col, side)
    low_in[row] = neg_out[row, :, halves[0]]
    high_in[col] = neg_out[:, col, halves[1]]

    def pass_on():
        @pl.loop(1, side)
        def _(i):
            to_owner_row(lax.rem(row + i, side)).wait()

        wait_all(to_owner_col, side)
        low_mid[...] = jnp.sum(low_in[...].astype(F32), axis=0).astype(BF16)
        high_mid[...] = jnp.sum(high_in[...].astype(F32), axis=0).astype(BF16)
        start_both(to_owner_second)
        low_end[col] = low_mid[col]
        high_end[row] = high_mid[row]

    def rows_one_hot(row_ids, i, size):
        place = lax.broadcasted_iota(jnp.int32, (size, cap), 0) + i * size
        picks = [
            one_hot(row_ids[s : s + 1, :] == place).astype(BF16) for s in range(n_narrow)
        ]
        return jnp.concatenate(picks, axis=1)

    acc[...] = jnp.zeros_like(acc)
    wo_acc[...] = jnp.zeros_like(wo_acc)

    def back_top(v, grad_embed):
        @pl.loop(0, blocks)
        def _(i):
            rows = rows_of(i, block)
            grad = grad_embed(i, rows)
            unit = embed[v, rows, :].astype(F32)
            inner = jnp.sum(unit * grad, axis=1, keepdims=True)
            grad_out = (scale[v, rows, :] * (grad - unit * inner)).astype(BF16)
            value = normed[v, rows, :]
            wo_acc[...] += dot(grad_out, jnp.maximum(value, 0), TN)
            value = value.astype(F32)
            grad_act = jnp.where(value > 0, dot(grad_out, w_out[...], NT), 0.0)
            acc[2 * v] += fold(grad_act)
            acc[2 * v + 1] += fold(grad_act * value)
            grad_norm[v, rows, :] = grad_act.astype(BF16)

    def first_product(v):
        @pl.loop(0, blocks)
        def _(i):
            rows = rows_of(i, block)
            wh_one[v] += dot(view_rows(v, rows), grad_norm[v, rows, :], TN)

    back_top(0, lambda i, rows: dot(rows_one_hot(dest_row, i, block), grad_query[...]))
    pass_on()
    first_product(0)

    wait_sent(to_key, n_narrow)
    wait_all(to_slot, n_narrow)
    wait_both(to_owner_second)
    neg_mine[halves[0], :] = jnp.sum(low_end[...].astype(F32), axis=0).astype(BF16)
    neg_mine[halves[1], :] = jnp.sum(high_end[...].astype(F32), axis=0).astype(BF16)

    def grad_b(i, rows):
        mask = one_hot(send_col[rows, :] == neg_row[...]).astype(BF16)
        return grad_in_slots[rows, :].astype(F32) + dot(mask, neg_mine[...])

    back_top(1, grad_b)

    z, c = w // 2, lax.rem(w, 2)
    partner = (2 * z + 1 - c, n)

    def sum_stages(k, first):
        half, own, piece, chunk, stack_in = sets[k]
        span, rows = half.shape[0], chunk.shape[0]
        mine = pl.multiple_of(first + c * span, 16)
        other = pl.multiple_of(first + (1 - c) * span, 16)
        place = pl.ds(pl.multiple_of(mine + n * rows, 16), rows)

        def swap():
            return remote(grads.at[pl.ds(other, span)], half, sem_pair.at[k], 0, partner)

        def to_piece(d):
            return remote(
                own.at[rows_of(target(d), rows)],
                piece.at[n],
                sem_piece.at[k],
                d,
                peer(d),
            )

        def start_piece():
            own[...] = (
                grads[pl.ds(mine, span), :].astype(F32) + half[...].astype(F32)
            ).astype(BF16)
            start_all(to_piece, n_narrow, far_first)
            piece[n] = own[rows_of(n, rows), :]

        def to_stack(d):
            return remote(
                chunk,
                stack_in.at[z],
                sem_stack.at[k],
                d,
                (2 * lax.rem(z + d, n_z) + c, n),
            )

        def start_stack():
            wait_all(to_piece, n_narrow)
            chunk[...] = jnp.sum(piece[...].astype(F32), axis=0).astype(BF16)
            start_all(to_stack, n_z)
            stack_in[z] = chunk[...]

        def to_gather(d):
            return remote(grads_o.at[place], grads_o.at[place], sem_gather.at[k], d, peer(d))

        def start_gather():
            wait_all(to_stack, n_z)
            grads_o[place, :] = jnp.sum(stack_in[...].astype(F32), axis=0).astype(BF16)
            start_all(to_gather, n_narrow, far_first)

        def last():
            part = grads_o.at[pl.ds(mine, span)]
            return remote(part, part, sem_pair.at[k], 1, partner)

        def write(k2, first):
            part = pl.ds(first, span)
            return pltpu.make_async_copy(
                grads_o.at[part], grads_out.at[part], sem_result.at[2 * k + k2]
            )

        def start_last():
            wait_all(to_gather, n_narrow)
            last().start()
            write(0, mine).start()

        def finish_last():
            last().wait()
            write(1, other).start()

        def end():
            write(0, mine).wait()
            write(1, other).wait()

        return swap, start_piece, start_stack, start_gather, start_last, finish_last, end

    grads[wo_first:, :] = wo_acc[...].T.astype(BF16)
    send_wo = sum_stages(1, wo_first)
    send_wo[0]().start()

    def wo_piece():
        send_wo[0]().wait()
        send_wo[1]()
        first_product(1)

    put_sums(stat2, jnp.sum(acc[...], axis=1))
    stat2[0:1, split:] = loss_acc[0:1, :]
    stat2[1:8, split:] = jnp.broadcast_to(
        jnp.sum(spread_counts(), axis=0, keepdims=True), (7, cap)
    )
    sum_all(
        stat2,
        near2,
        part2,
        far2,
        total2,
        sem_near2,
        sem_far2,
        wo_piece,
        send_wo[2],
    )

    pair_total = total2[1:2, split : split + 1]
    grad_weight = all_points / pair_total
    loss_o[0:1, :] = total2[0:1, split:] / pair_total
    mean_grads = [get_sum(total2, 2 * v) * inv_count for v in range(2)]
    mean_crosses = [get_sum(total2, 2 * v + 1) * inv_count for v in range(2)]
    scales = [inverses[v] * grad_weight for v in range(2)]
    loss_o[1:8, :] = jnp.broadcast_to(grad_weight, (7, cap))
    loss_write = pltpu.make_async_copy(loss_o, loss_out, sem_result.at[4])
    loss_write.start()
    totals = [jnp.sum(feat_acc[v], axis=0, keepdims=True) for v in range(2)]
    downs = [jnp.broadcast_to(row, (8, depth)).T[:, 0:1] for row in totals]
    for p in range(parts):
        cols = slice(p * width, (p + 1) * width)
        value = sum(
            scales[v][:, cols]
            * (
                wh_one[v, :, cols]
                - downs[v] * mean_grads[v][:, cols]
                - wh_two[v, :, cols] * mean_crosses[v][:, cols]
            )
            for v in range(2)
        )
        grads[p * depth : (p + 1) * depth, :] = value.astype(BF16)

    def store(v, i):
        ref = (grad_feat_a, grad_feat_b)[v]
        rows = rows_of(i, block)
        return pltpu.make_async_copy(normed.at[v, rows], ref.at[rows], sem_out.at[v, i])

    def feat_grad(v):
        @pl.loop(0, blocks)
        def _(i):
            rows = rows_of(i, block)
            grad = grad_norm[v, rows, :].astype(F32)
            value = normed[v, rows, :].astype(F32)
            grad = scales[v] * (grad - mean_grads[v] - value * mean_crosses[v])
            out = dot(grad.astype(BF16), w_hidden[...], NT).astype(BF16)
            if v:
                feat_slot[rows, :] = out
            else:
                normed[v, rows, :] = out
                store(v, i).start()

    def row_order():
        @pl.loop(0, blocks)
        def _(i):
            picks = rows_one_hot(send_row, i, block)
            normed[1, rows_of(i, block), :] = dot(picks, feat_slot[...]).astype(BF16)
            store(1, i).start()

    send_wh = sum_stages(0, wh_first)
    swap = send_wh[0]()
    swap.start()
    swap.wait()
    send_wh[1]()
    feat_grad(0)
    send_wh[2]()
    feat_grad(1)
    send_wo[3]()
    send_wh[3]()
    row_order()
    send_wo[4]()
    send_wh[4]()
    send_wo[5]()
    send_wh[5]()
    for v in range(2):
        for i in range(blocks):
            store(v, i).wait()
    send_wo[6]()
    send_wh[6]()
    loss_write.wait()


def deliver_kernel(
    loss_in,
    grad_a,
    grad_b,
    grads_in,
    loss_o,
    out_a,
    out_b,
    out_wh,
    out_wo,
    loss,
    grads,
    wh,
    wo,
    held,
    sem,
    read_sem,
    write_sem,
):
    pieces = read_sem.shape[1]
    rows = grad_a.shape[0] // pieces
    reads, writes = [], []
    for v, (src, dst) in enumerate(((grad_a, out_a), (grad_b, out_b))):
        for i in range(pieces):
            part = pl.ds(i * rows, rows)
            middle = held.at[v, part]
            reads.append(pltpu.make_async_copy(src.at[part], middle, read_sem.at[v, i]))
            writes.append(pltpu.make_async_copy(middle, dst.at[part], write_sem.at[v, i]))
    first = [
        pltpu.make_async_copy(grads_in, grads, sem.at[0]),
        pltpu.make_async_copy(loss_in, loss, sem.at[1]),
    ]
    for copy in first + reads:
        copy.start()
    for copy in first:
        copy.wait()
    depth, hidden = wh.shape
    width = wo.shape[1]
    for p in range(hidden // width):
        wh[:, p * width : (p + 1) * width] = grads[p * depth : (p + 1) * depth, :].astype(F32)
    writes.append(pltpu.make_async_copy(wh, out_wh, sem.at[2]))
    writes[-1].start()
    wo[...] = grads[hidden // width * depth :, :].astype(F32) * loss[1:2, 0:1]
    writes.append(pltpu.make_async_copy(wo, out_wo, sem.at[3]))
    writes[-1].start()
    for arrived, copy in zip(reads, writes):
        arrived.wait()
        copy.start()
    loss_o[...] = loss[0:1, 0:1]
    for copy in writes:
        copy.wait()

def body(feat_a, feat_b, w_hidden, w_out, send_rows, dest_rows, counts, neg_rows):
    points, depth = feat_a.shape[2:]
    hidden, width = w_out.shape
    n_wide, n_narrow = lax.axis_size("wide"), lax.axis_size("narrow")
    n_z = n_wide // 2
    side = math.isqrt(n_narrow)
    cap = send_rows.shape[3]
    neg_count = neg_rows.shape[2]
    total_negs = n_narrow * neg_count
    all_points = float(n_wide * n_narrow * points)
    blocks = points // min(512, points)
    stat = (8, hidden // 2)
    stat2 = (8, hidden // 2 + cap)
    grad_total = depth * hidden // width + hidden
    wh_rows = depth * hidden // width

    def sum_scratch(total):
        span = total // 2
        rows = span // n_narrow
        return (
            pltpu.VMEM((span, width), BF16),
            pltpu.VMEM((span, width), BF16),
            pltpu.VMEM((n_narrow, rows, width), BF16),
            pltpu.VMEM((rows, width), BF16),
            pltpu.VMEM((n_z, rows, width), BF16),
        )

    vmem = pl.BlockSpec(memory_space=pltpu.VMEM)
    anywhere = pl.BlockSpec(memory_space=pl.ANY)
    dma = pltpu.SemaphoreType.DMA
    out_shape = (
        jax.ShapeDtypeStruct((8, cap), F32),
        jax.ShapeDtypeStruct((points, depth), BF16),
        jax.ShapeDtypeStruct((points, depth), BF16),
        jax.ShapeDtypeStruct((grad_total, width), BF16),
    )
    scratch = [
        pltpu.VMEM((depth, hidden), BF16),
        pltpu.VMEM((hidden, width), BF16),
        pltpu.VMEM((n_narrow, cap), jnp.int32),
        pltpu.VMEM((n_narrow, cap), jnp.int32),
        pltpu.VMEM((1, n_narrow), jnp.int32),
        pltpu.VMEM((1, neg_count), jnp.int32),
        pltpu.VMEM((8, cap), F32),
        pltpu.VMEM((grad_total, width), BF16),
        pltpu.VMEM((2, points, depth), BF16),
        pltpu.VMEM((points, depth), BF16),
        pltpu.VMEM((points, hidden), F32),
        pltpu.VMEM((2, points, hidden), BF16),
        pltpu.VMEM((2, points, width), BF16),
        pltpu.VMEM((2, points, 1), F32),
        pltpu.VMEM((4, 8, hidden), F32),
        pltpu.VMEM((2, 8, depth), F32),
        pltpu.VMEM(stat, F32),
        pltpu.VMEM((n_narrow,) + stat, F32),
        pltpu.VMEM(stat, F32),
        pltpu.VMEM((n_wide,) + stat, F32),
        pltpu.VMEM(stat, F32),
        pltpu.VMEM(stat2, F32),
        pltpu.VMEM((n_narrow,) + stat2, F32),
        pltpu.VMEM(stat2, F32),
        pltpu.VMEM((n_wide,) + stat2, F32),
        pltpu.VMEM(stat2, F32),
        pltpu.VMEM((n_narrow, 8, cap), jnp.int32),
        pltpu.VMEM((n_narrow, 8, cap), jnp.int32),
        pltpu.VMEM((points, 1), jnp.int32),
        pltpu.VMEM((n_narrow, cap), jnp.int32),
        pltpu.VMEM((points, 1), jnp.int32),
        pltpu.VMEM((points, 1), F32),
        pltpu.VMEM((points, width), BF16),
        pltpu.VMEM((side, side, neg_count, width), BF16),
        pltpu.VMEM((points, width), BF16),
        pltpu.VMEM((points, total_negs), BF16),
        pltpu.VMEM((points, 1), F32),
        pltpu.VMEM((points, width), F32),
        pltpu.VMEM((width, points), BF16),
        pltpu.VMEM((points, width), BF16),
        pltpu.VMEM((points, width), BF16),
        pltpu.VMEM((points, width), BF16),
        pltpu.VMEM((side, side, neg_count, width), BF16),
        pltpu.VMEM((side, side, neg_count // 2, width), BF16),
        pltpu.VMEM((side, side, neg_count // 2, width), BF16),
        pltpu.VMEM((side, neg_count // 2, width), BF16),
        pltpu.VMEM((side, neg_count // 2, width), BF16),
        pltpu.VMEM((side, neg_count // 2, width), BF16),
        pltpu.VMEM((side, neg_count // 2, width), BF16),
        pltpu.VMEM((neg_count, width), BF16),
        pltpu.VMEM((2, points, hidden), BF16),
        pltpu.VMEM((width, hidden), F32),
        pltpu.VMEM((2, depth, hidden), F32),
        pltpu.VMEM((2, depth, hidden), F32),
        pltpu.VMEM((8, cap), F32),
        pltpu.VMEM((grad_total, width), BF16),
        *sum_scratch(wh_rows),
        *sum_scratch(hidden),
        dma((6,)),
        dma((5,)),
        dma((2, blocks)),
        dma((2, blocks)),
        dma((2, n_narrow)),
        dma((2, n_narrow)),
        dma((2, n_wide)),
        dma((2, n_narrow)),
        dma((2, n_wide)),
        dma((2, 4 * side)),
        dma((2, n_narrow)),
        dma((2, n_narrow)),
        dma((2, 4 * side)),
        dma((2, 2, 2)),
        dma((2, 2, n_narrow)),
        dma((2, 2, n_z)),
        dma((2, 2, n_narrow)),
    ]
    loss, grad_a, grad_b, grads = pl.pallas_call(
        functools.partial(step_kernel, all_points),
        out_shape=out_shape,
        in_specs=[anywhere] * 8,
        out_specs=(anywhere,) * 4,
        scratch_shapes=scratch,
        compiler_params=pltpu.CompilerParams(
            collective_id=1, has_side_effects=True, vmem_limit_bytes=63 * 1024 * 1024
        ),
        name="step",
    )(
        feat_a.reshape(points, depth),
        feat_b.reshape(points, depth),
        w_hidden,
        w_out,
        send_rows.reshape(n_narrow, cap),
        dest_rows.reshape(n_narrow, cap),
        counts.reshape(1, n_narrow),
        neg_rows.reshape(1, neg_count),
    )
    loss, grad_a, grad_b, grad_wh, grad_wo = pl.pallas_call(
        deliver_kernel,
        out_shape=(
            jax.ShapeDtypeStruct((1, 1), F32),
            jax.ShapeDtypeStruct((points, depth), BF16),
            jax.ShapeDtypeStruct((points, depth), BF16),
            jax.ShapeDtypeStruct((depth, hidden), F32),
            jax.ShapeDtypeStruct((hidden, width), F32),
        ),
        in_specs=[anywhere] * 4,
        out_specs=(vmem,) + (anywhere,) * 4,
        scratch_shapes=[
            pltpu.VMEM((8, cap), F32),
            pltpu.VMEM((grad_total, width), BF16),
            pltpu.VMEM((depth, hidden), F32),
            pltpu.VMEM((hidden, width), F32),
            pltpu.VMEM((2, points, depth), BF16),
            dma((4,)),
            dma((2, 4)),
            dma((2, 4)),
        ],
        compiler_params=pltpu.CompilerParams(vmem_limit_bytes=63 * 1024 * 1024),
        name="deliver",
    )(loss, grad_a, grad_b, grads)
    return (
        loss.reshape(()),
        grad_a.reshape(feat_a.shape),
        grad_b.reshape(feat_b.shape),
        grad_wh,
        grad_wo,
    )


def solution(mesh):
    placed = (
        P("wide", "narrow", None, None),
        P("wide", "narrow", None, None),
        P(),
        P(),
        P("wide", "narrow", None, None),
        P("wide", "narrow", None, None),
        P("wide", "narrow", None),
        P("wide", "narrow", None),
    )
    return jax.shard_map(
        body,
        mesh=mesh,
        in_specs=placed,
        out_specs=(P(), P("wide", "narrow", None, None), P("wide", "narrow", None, None), P(), P()),
        check_vma=False,
    )
```

```python
import functools
import math

import jax
import jax.numpy as jnp
from jax import lax
from jax.experimental import pallas as pl
from jax.experimental.pallas import tpu as pltpu
from jax.sharding import PartitionSpec as P

MESH = pl.DeviceIdType.MESH
F32 = jnp.float32
BF16 = jnp.bfloat16
TEMPERATURE = 0.07
NT = (((1,), (1,)), ((), ()))
TN = (((0,), (0,)), ((), ()))


def dot(left, right, dims=None):
    if dims is None:
        return jnp.dot(left, right, preferred_element_type=F32)
    return lax.dot_general(left, right, dims, preferred_element_type=F32)


def one_hot(mask):
    return jnp.where(mask, 1.0, 0.0).astype(F32)


def fold(values):
    rows, width = values.shape
    return jnp.sum(values.reshape(rows // 8, 8, width), axis=0)


def remote(src, dst, sems, d, device):
    return pltpu.make_async_remote_copy(
        src_ref=src,
        dst_ref=dst,
        send_sem=sems.at[0, d],
        recv_sem=sems.at[1, d],
        device_id=device,
        device_id_type=MESH,
    )


def start_all(make, count, order=None):
    for d in order or range(1, count):
        make(d).start()


def wait_all(make, count):
    for d in range(1, count):
        make(d).wait()


def wait_sent(make, count):
    for d in range(1, count):
        make(d).wait_send()


def step_kernel(
    all_points,
    feat_a,
    feat_b,
    w_hidden_in,
    w_out_in,
    send_in,
    dest_in,
    counts_in,
    neg_in,
    loss_out,
    grad_feat_a,
    grad_feat_b,
    grads_out,
    w_hidden,
    w_out,
    send_row,
    dest_own,
    counts,
    neg_row,
    loss_o,
    grads_o,
    feat,
    feat_slot,
    lin,
    normed,
    embed,
    scale,
    acc,
    feat_acc,
    stat,
    near,
    part,
    far,
    total,
    stat2,
    near2,
    part2,
    far2,
    total2,
    msg,
    msg_in,
    send_col,
    dest_row,
    dest_col,
    live_col,
    query,
    negs,
    keys_in,
    expo,
    exp_sum,
    num,
    spread,
    grad_query,
    grad_out_slots,
    grad_in_slots,
    neg_out,
    low_in,
    high_in,
    low_mid,
    high_mid,
    low_end,
    high_end,
    neg_mine,
    grad_norm,
    wo_acc,
    wh_one,
    wh_two,
    loss_acc,
    grads,
    half,
    own,
    piece,
    chunk,
    stack_in,
    half_wo,
    own_wo,
    piece_wo,
    chunk_wo,
    stack_wo,
    sem_small,
    sem_result,
    sem_in,
    sem_out,
    sem_msg,
    sem_near,
    sem_far,
    sem_near2,
    sem_far2,
    sem_neg,
    sem_key,
    sem_grad,
    sem_negback,
    sem_pair,
    sem_piece,
    sem_stack,
    sem_gather,
):
    w = lax.axis_index("wide")
    n = lax.axis_index("narrow")
    n_wide = far.shape[0]
    n_narrow = near.shape[0]
    n_z = stack_in.shape[0]
    points, depth = feat_a.shape
    hidden = w_hidden.shape[1]
    width = w_out.shape[1]
    cap = points // n_narrow
    neg_count = neg_row.shape[1]
    block = min(512, points)
    small = min(256, points)
    blocks = points // block
    split = hidden // 2
    parts = hidden // width
    wh_first, wo_first = 0, parts * depth
    sets = (
        (half, own, piece, chunk, stack_in),
        (half_wo, own_wo, piece_wo, chunk_wo, stack_wo),
    )
    side = negs.shape[0]
    upper = neg_count // 2
    row, col = n // side, lax.rem(n, side)
    halves = (slice(0, upper), slice(upper, neg_count))

    def steps(d):
        if isinstance(d, int):
            return d // side, d % side
        return lax.div(d, side), lax.rem(d, side)

    def hops(d):
        return sum(min(k, side - k) for k in steps(d))

    far_first = sorted(range(1, n_narrow), key=hops, reverse=True)

    def target(d):
        down, right = steps(d)
        return lax.rem(row + down, side) * side + lax.rem(col + right, side)

    def peer(d):
        return (w, target(d))

    def along_row(d):
        return (w, row * side + lax.rem(col + d, side))

    def along_col(d):
        return (w, lax.rem(row + d, side) * side + col)

    def source(d):
        down, right = steps(d)
        return lax.rem(row + side - down, side) * side + lax.rem(col + side - right, side)

    def across(d):
        return (lax.rem(w + d, n_wide), n)

    def rows_of(i, size):
        return pl.ds(pl.multiple_of(i * size, size), size)

    barrier = pltpu.get_barrier_semaphore()

    for d in range(1, n_narrow):
        pl.semaphore_signal(barrier, inc=1, device_id=peer(d), device_id_type=MESH)
    for d in range(1, n_wide):
        pl.semaphore_signal(barrier, inc=1, device_id=across(d), device_id_type=MESH)

    small_loads = [
        pltpu.make_async_copy(src, dst, sem_small.at[k])
        for k, (src, dst) in enumerate(
            (
                (w_hidden_in, w_hidden),
                (w_out_in, w_out),
                (send_in, send_row),
                (dest_in, dest_own),
                (counts_in, counts),
                (neg_in, neg_row),
            )
        )
    ]
    small_loads[0].start()

    def load(v, i):
        ref = (feat_a, feat_b)[v]
        rows = rows_of(i, block)
        return pltpu.make_async_copy(ref.at[rows], feat.at[v, rows], sem_in.at[v, i])

    for v in (1, 0):
        for i in range(blocks):
            load(v, i).start()
    for copy in small_loads[1:]:
        copy.start()
    small_loads[0].wait()

    acc[...] = jnp.zeros_like(acc)
    feat_acc[...] = jnp.zeros_like(feat_acc)
    for v in (1, 0):

        @pl.loop(0, blocks)
        def _(i):
            load(v, i).wait()
            rows = rows_of(i, block)
            points_in = feat[v, rows, :]
            linear = dot(points_in, w_hidden[...])
            acc[2 * v] += fold(linear)
            acc[2 * v + 1] += fold(linear * linear)
            feat_acc[v] += fold(points_in.astype(F32))

    def put_sums(stat, sums):
        for r in range(4):
            stat[2 * r : 2 * r + 1, 0:split] = sums[r : r + 1, 0:split]
            stat[2 * r + 1 : 2 * r + 2, 0:split] = sums[r : r + 1, split:]

    def get_sum(total, r):
        return jnp.concatenate(
            [total[2 * r : 2 * r + 1, 0:split], total[2 * r + 1 : 2 * r + 2, 0:split]], axis=1
        )

    for copy in small_loads[1:]:
        copy.wait()
    put_sums(stat, jnp.sum(acc[...], axis=1))

    pl.semaphore_wait(barrier, n_narrow + n_wide - 2)

    def sum_all(stat, near, part, far, total, sem_near, sem_far, between=None, later=None):
        def to_near(d):
            return remote(stat, near.at[n], sem_near, d, peer(d))

        def to_far(d):
            return remote(part, far.at[w], sem_far, d, across(d))

        start_all(to_near, n_narrow, far_first)
        near[n] = stat[...]
        if between is not None:
            between()
        wait_all(to_near, n_narrow)
        part[...] = jnp.sum(near[...], axis=0)
        start_all(to_far, n_wide)
        far[w] = part[...]
        if later is not None:
            later()
        wait_all(to_far, n_wide)
        total[...] = jnp.sum(far[...], axis=0)

    def to_msg(d):
        return remote(msg.at[target(d)], msg_in.at[n], sem_msg, d, peer(d))

    def gather(ids, table, i):
        lanes = lax.broadcasted_iota(jnp.int32, (block, points), 1)
        return dot(one_hot(ids[rows_of(i, block), :] == lanes).astype(BF16), table)

    def columns(ids, ref):
        square = jnp.concatenate(
            [ids.astype(F32), jnp.zeros((cap - n_narrow, cap), F32)], axis=0
        ).T.astype(jnp.int32)
        for s in range(n_narrow):
            ref[s * cap : (s + 1) * cap, :] = square[:, s : s + 1]

    def spread_counts():
        across_lanes = lax.broadcasted_iota(jnp.int32, (n_narrow, n_narrow), 1)
        down = lax.broadcasted_iota(jnp.int32, (n_narrow, n_narrow), 0)
        here = jnp.broadcast_to(counts[...], (n_narrow, n_narrow)).astype(F32)
        return jnp.sum(jnp.where(across_lanes == down, here, 0.0), axis=1, keepdims=True)

    def slot_order():
        count = spread_counts().astype(jnp.int32)
        line = lax.broadcasted_iota(jnp.int32, (8, cap), 0)
        for s in range(n_narrow):
            msg[s] = jnp.where(line == 0, dest_own[s : s + 1, :], count[s : s + 1, :])
        start_all(to_msg, n_narrow, far_first)
        msg_in[n] = msg[n]
        columns(send_row[...], send_col)
        to_slots(0, blocks - 1)

    def to_slots(low, high):
        @pl.loop(low, high)
        def _(i):
            feat_slot[rows_of(i, block), :] = gather(send_col, feat[1], i).astype(BF16)

    def slot_linear():
        to_slots(blocks - 1, blocks)

        @pl.loop(0, blocks)
        def _(i):
            rows = rows_of(i, block)
            lin[rows, :] = dot(feat_slot[rows, :], w_hidden[...])

        wait_all(to_msg, n_narrow)
        ids = msg_in[:, 0, :]
        dest_row[...] = ids
        columns(ids, dest_col)
        line = lax.broadcasted_iota(jnp.int32, (cap, 1), 0)
        for s in range(n_narrow):
            live_col[s * cap : (s + 1) * cap, :] = one_hot(line < msg_in[s, 1:2, 0:1])

    sum_all(stat, near, part, far, total, sem_near, sem_far, slot_order, slot_linear)

    inv_count = 1.0 / all_points
    means, inverses = [], []
    for v in range(2):
        mean = get_sum(total, 2 * v) * inv_count
        square = get_sum(total, 2 * v + 1) * inv_count
        means.append(mean)
        inverses.append(lax.rsqrt(square - mean * mean + 1e-5))

    def finish(v):
        @pl.loop(0, blocks)
        def _(i):
            rows = rows_of(i, block)
            linear = lin[rows, :] if v else dot(feat[0, rows, :], w_hidden[...])
            value = ((linear - means[v]) * inverses[v]).astype(BF16)
            normed[v, rows, :] = value
            out = dot(jnp.maximum(value, 0), w_out[...])
            unit_scale = lax.rsqrt(jnp.sum(out * out, axis=1, keepdims=True) + 1e-6)
            embed[v, rows, :] = (out * unit_scale).astype(BF16)
            scale[v, rows, :] = unit_scale

    finish(1)
    neg_col = jnp.broadcast_to(neg_row[...].astype(F32), (cap, neg_count)).T.astype(jnp.int32)
    picks = [
        one_hot(send_row[s : s + 1, :] == neg_col).astype(BF16) for s in range(n_narrow)
    ]
    negs[row, col] = dot(jnp.concatenate(picks, axis=1), embed[1]).astype(BF16)

    def neg_first(d):
        low, high = negs.at[row, col, halves[0]], negs.at[row, col, halves[1]]
        return (
            remote(low, low, sem_neg, d, along_row(d)),
            remote(high, high, sem_neg, side + d, along_col(d)),
        )

    def neg_second(d):
        low, high = negs.at[row, :, halves[0]], negs.at[:, col, halves[1]]
        return (
            remote(low, low, sem_neg, 2 * side + d, along_col(d)),
            remote(high, high, sem_neg, 3 * side + d, along_row(d)),
        )

    def start_both(make):
        for d in range(1, side):
            for copy in make(d):
                copy.start()

    def wait_both(make):
        for d in range(1, side):
            for copy in make(d):
                copy.wait()

    start_both(neg_first)

    def to_key(d):
        return remote(
            embed.at[1, rows_of(target(d), cap)],
            keys_in.at[rows_of(n, cap)],
            sem_key,
            d,
            peer(d),
        )

    finish(0)

    wait_both(neg_first)
    start_both(neg_second)
    start_all(to_key, n_narrow, far_first)
    keys_in[rows_of(n, cap), :] = embed[1, rows_of(n, cap), :]

    @pl.loop(0, blocks)
    def _(i):
        query[rows_of(i, block), :] = gather(dest_col, embed[0], i).astype(BF16)

    wh_two[...] = jnp.zeros_like(wh_two)
    wh_one[...] = jnp.zeros_like(wh_one)

    def view_rows(v, rows):
        return feat_slot[rows, :] if v else feat[0, rows, :]

    for v in range(2):

        @pl.loop(0, blocks)
        def _(i):
            rows = rows_of(i, block)
            wh_two[v] += dot(view_rows(v, rows), normed[v, rows, :], TN)

    wait_both(neg_second)
    total_negs = n_narrow * neg_count

    to_exp2 = math.log2(math.e) / TEMPERATURE

    @pl.loop(0, points // small)
    def _(i):
        rows = rows_of(i, small)
        table = negs[...].reshape(total_negs, width)
        score = dot(query[rows, :], table, NT)
        power = jnp.exp2(score * to_exp2)
        exp_sum[rows, :] = jnp.sum(power, axis=1, keepdims=True)
        power = power.astype(BF16)
        expo[rows, :] = power
        num[rows, :] = dot(power, table)

    loss_acc[...] = jnp.zeros_like(loss_acc)

    def to_slot(d):
        rows = rows_of(source(d), cap)
        return remote(
            grad_out_slots.at[rows],
            grad_in_slots.at[rows_of(n, cap)],
            sem_grad,
            d,
            (w, source(d)),
        )

    def answer(d):
        rows = rows_of(source(d), cap)
        live = live_col[rows, :]
        key = keys_in[rows, :].astype(F32)
        asked = query[rows, :].astype(F32)
        positive = jnp.sum(asked * key, axis=1, keepdims=True) * (1.0 / TEMPERATURE)
        exp_pos = jnp.exp(positive)
        denominator = exp_pos + exp_sum[rows, :]
        term = live * (jnp.log(denominator) - positive)
        weight = live * (1.0 / TEMPERATURE)
        share = weight / denominator
        pair_coeff = share * exp_pos - weight
        grad_out_slots[rows, :] = (pair_coeff * asked).astype(BF16)
        grad_query[rows, :] = (pair_coeff * key + share * num[rows, :]).astype(BF16)
        spread[:, rows] = (share * asked).T.astype(BF16)
        return jnp.sum(term, axis=0, keepdims=True)

    pair = min(4, n_narrow)

    @pl.loop(0, n_narrow // pair)
    def _(i):
        for k in range(pair):
            d = i * pair + k

            @pl.when(d > 0)
            def _():
                to_key(d).wait_recv()

        loss_acc[...] += sum(answer(i * pair + k) for k in range(pair))
        for k in range(pair):
            d = i * pair + k

            @pl.when(d > 0)
            def _():
                to_slot(d).start()

    grad_in_slots[rows_of(n, cap), :] = grad_out_slots[rows_of(n, cap), :]

    def to_owner_row(q):
        d = lax.rem(q - row + side, side)
        return remote(
            neg_out.at[q, :, halves[0]], low_in.at[row], sem_negback, d, (w, q * side + col)
        )

    def to_owner_col(d):
        q = lax.rem(col + d, side)
        return remote(
            neg_out.at[:, q, halves[1]], high_in.at[col], sem_negback, side + d, along_row(d)
        )

    def to_owner_second(d):
        return (
            remote(
                low_mid.at[lax.rem(col + d, side)],
                low_end.at[col],
                sem_negback,
                2 * side + d,
                along_row(d),
            ),
            remote(
                high_mid.at[lax.rem(row + d, side)],
                high_end.at[row],
                sem_negback,
                3 * side + d,
                along_col(d),
            ),
        )

    @pl.loop(1, side + 1)
    def _(i):
        q = lax.rem(row + i, side)
        cols = rows_of(q, side * neg_count)
        neg_out[q] = (
            dot(spread[...], expo[:, cols]).T.astype(BF16).reshape(side, neg_count, width)
        )

        @pl.when(i < side)
        def _():
            to_owner_row(q).start()

    start_all(to_owner_col, side)
    low_in[row] = neg_out[row, :, halves[0]]
    high_in[col] = neg_out[:, col, halves[1]]

    def pass_on():
        @pl.loop(1, side)
        def _(i):
            to_owner_row(lax.rem(row + i, side)).wait()

        wait_all(to_owner_col, side)
        low_mid[...] = jnp.sum(low_in[...].astype(F32), axis=0).astype(BF16)
        high_mid[...] = jnp.sum(high_in[...].astype(F32), axis=0).astype(BF16)
        start_both(to_owner_second)
        low_end[col] = low_mid[col]
        high_end[row] = high_mid[row]

    def rows_one_hot(row_ids, i, size):
        place = lax.broadcasted_iota(jnp.int32, (size, cap), 0) + i * size
        picks = [
            one_hot(row_ids[s : s + 1, :] == place).astype(BF16) for s in range(n_narrow)
        ]
        return jnp.concatenate(picks, axis=1)

    acc[...] = jnp.zeros_like(acc)
    wo_acc[...] = jnp.zeros_like(wo_acc)

    def back_top(v, grad_embed):
        @pl.loop(0, blocks)
        def _(i):
            rows = rows_of(i, block)
            grad = grad_embed(i, rows)
            unit = embed[v, rows, :].astype(F32)
            inner = jnp.sum(unit * grad, axis=1, keepdims=True)
            grad_out = (scale[v, rows, :] * (grad - unit * inner)).astype(BF16)
            value = normed[v, rows, :]
            wo_acc[...] += dot(grad_out, jnp.maximum(value, 0), TN)
            value = value.astype(F32)
            grad_act = jnp.where(value > 0, dot(grad_out, w_out[...], NT), 0.0)
            acc[2 * v] += fold(grad_act)
            acc[2 * v + 1] += fold(grad_act * value)
            grad_norm[v, rows, :] = grad_act.astype(BF16)

    def first_product(v):
        @pl.loop(0, blocks)
        def _(i):
            rows = rows_of(i, block)
            wh_one[v] += dot(view_rows(v, rows), grad_norm[v, rows, :], TN)

    back_top(0, lambda i, rows: dot(rows_one_hot(dest_row, i, block), grad_query[...]))
    pass_on()
    first_product(0)

    wait_sent(to_key, n_narrow)
    wait_all(to_slot, n_narrow)
    wait_both(to_owner_second)
    neg_mine[halves[0], :] = jnp.sum(low_end[...].astype(F32), axis=0).astype(BF16)
    neg_mine[halves[1], :] = jnp.sum(high_end[...].astype(F32), axis=0).astype(BF16)

    def grad_b(i, rows):
        mask = one_hot(send_col[rows, :] == neg_row[...]).astype(BF16)
        return grad_in_slots[rows, :].astype(F32) + dot(mask, neg_mine[...])

    back_top(1, grad_b)

    z, c = w // 2, lax.rem(w, 2)
    partner = (2 * z + 1 - c, n)

    def sum_stages(k, first):
        half, own, piece, chunk, stack_in = sets[k]
        span, rows = half.shape[0], chunk.shape[0]
        mine = pl.multiple_of(first + c * span, 16)
        other = pl.multiple_of(first + (1 - c) * span, 16)
        place = pl.ds(pl.multiple_of(mine + n * rows, 16), rows)

        def swap():
            return remote(grads.at[pl.ds(other, span)], half, sem_pair.at[k], 0, partner)

        def to_piece(d):
            return remote(
                own.at[rows_of(target(d), rows)],
                piece.at[n],
                sem_piece.at[k],
                d,
                peer(d),
            )

        def start_piece():
            own[...] = (
                grads[pl.ds(mine, span), :].astype(F32) + half[...].astype(F32)
            ).astype(BF16)
            start_all(to_piece, n_narrow, far_first)
            piece[n] = own[rows_of(n, rows), :]

        def to_stack(d):
            return remote(
                chunk,
                stack_in.at[z],
                sem_stack.at[k],
                d,
                (2 * lax.rem(z + d, n_z) + c, n),
            )

        def start_stack():
            wait_all(to_piece, n_narrow)
            chunk[...] = jnp.sum(piece[...].astype(F32), axis=0).astype(BF16)
            start_all(to_stack, n_z)
            stack_in[z] = chunk[...]

        def to_gather(d):
            return remote(grads_o.at[place], grads_o.at[place], sem_gather.at[k], d, peer(d))

        def start_gather():
            wait_all(to_stack, n_z)
            grads_o[place, :] = jnp.sum(stack_in[...].astype(F32), axis=0).astype(BF16)
            start_all(to_gather, n_narrow, far_first)

        def last():
            part = grads_o.at[pl.ds(mine, span)]
            return remote(part, part, sem_pair.at[k], 1, partner)

        def write(k2, first):
            part = pl.ds(first, span)
            return pltpu.make_async_copy(
                grads_o.at[part], grads_out.at[part], sem_result.at[2 * k + k2]
            )

        def start_last():
            wait_all(to_gather, n_narrow)
            last().start()
            write(0, mine).start()

        def finish_last():
            last().wait()
            write(1, other).start()

        def end():
            write(0, mine).wait()
            write(1, other).wait()

        return swap, start_piece, start_stack, start_gather, start_last, finish_last, end

    grads[wo_first:, :] = wo_acc[...].T.astype(BF16)
    send_wo = sum_stages(1, wo_first)
    send_wo[0]().start()

    def wo_piece():
        send_wo[0]().wait()
        send_wo[1]()
        first_product(1)

    put_sums(stat2, jnp.sum(acc[...], axis=1))
    stat2[0:1, split:] = loss_acc[0:1, :]
    stat2[1:8, split:] = jnp.broadcast_to(
        jnp.sum(spread_counts(), axis=0, keepdims=True), (7, cap)
    )
    sum_all(
        stat2,
        near2,
        part2,
        far2,
        total2,
        sem_near2,
        sem_far2,
        wo_piece,
        send_wo[2],
    )

    pair_total = total2[1:2, split : split + 1]
    grad_weight = all_points / pair_total
    loss_o[0:1, :] = total2[0:1, split:] / pair_total
    mean_grads = [get_sum(total2, 2 * v) * inv_count for v in range(2)]
    mean_crosses = [get_sum(total2, 2 * v + 1) * inv_count for v in range(2)]
    scales = [inverses[v] * grad_weight for v in range(2)]
    loss_o[1:8, :] = jnp.broadcast_to(grad_weight, (7, cap))
    loss_write = pltpu.make_async_copy(loss_o, loss_out, sem_result.at[4])
    loss_write.start()
    totals = [jnp.sum(feat_acc[v], axis=0, keepdims=True) for v in range(2)]
    downs = [jnp.broadcast_to(row, (8, depth)).T[:, 0:1] for row in totals]
    for p in range(parts):
        cols = slice(p * width, (p + 1) * width)
        value = sum(
            scales[v][:, cols]
            * (
                wh_one[v, :, cols]
                - downs[v] * mean_grads[v][:, cols]
                - wh_two[v, :, cols] * mean_crosses[v][:, cols]
            )
            for v in range(2)
        )
        grads[p * depth : (p + 1) * depth, :] = value.astype(BF16)

    def store(v, i):
        ref = (grad_feat_a, grad_feat_b)[v]
        rows = rows_of(i, block)
        return pltpu.make_async_copy(normed.at[v, rows], ref.at[rows], sem_out.at[v, i])

    def feat_grad(v):
        @pl.loop(0, blocks)
        def _(i):
            rows = rows_of(i, block)
            grad = grad_norm[v, rows, :].astype(F32)
            value = normed[v, rows, :].astype(F32)
            grad = scales[v] * (grad - mean_grads[v] - value * mean_crosses[v])
            out = dot(grad.astype(BF16), w_hidden[...], NT).astype(BF16)
            if v:
                feat_slot[rows, :] = out
            else:
                normed[v, rows, :] = out
                store(v, i).start()

    def row_order():
        @pl.loop(0, blocks)
        def _(i):
            picks = rows_one_hot(send_row, i, block)
            normed[1, rows_of(i, block), :] = dot(picks, feat_slot[...]).astype(BF16)
            store(1, i).start()

    send_wh = sum_stages(0, wh_first)
    swap = send_wh[0]()
    swap.start()
    swap.wait()
    send_wh[1]()
    feat_grad(0)
    send_wh[2]()
    feat_grad(1)
    send_wo[3]()
    send_wh[3]()
    row_order()
    send_wo[4]()
    send_wh[4]()
    send_wo[5]()
    send_wh[5]()
    for v in range(2):
        for i in range(blocks):
            store(v, i).wait()
    send_wo[6]()
    send_wh[6]()
    loss_write.wait()


def deliver_kernel(
    loss_in,
    grad_a,
    grad_b,
    grads_in,
    loss_o,
    out_a,
    out_b,
    out_wh,
    out_wo,
    loss,
    grads,
    wh,
    wo,
    held,
    sem,
    read_sem,
    write_sem,
):
    pieces = read_sem.shape[1]
    rows = grad_a.shape[0] // pieces
    reads, writes = [], []
    for v, (src, dst) in enumerate(((grad_a, out_a), (grad_b, out_b))):
        for i in range(pieces):
            part = pl.ds(i * rows, rows)
            middle = held.at[v, part]
            reads.append(pltpu.make_async_copy(src.at[part], middle, read_sem.at[v, i]))
            writes.append(pltpu.make_async_copy(middle, dst.at[part], write_sem.at[v, i]))
    first = [
        pltpu.make_async_copy(grads_in, grads, sem.at[0]),
        pltpu.make_async_copy(loss_in, loss, sem.at[1]),
    ]
    for copy in first + reads:
        copy.start()
    for copy in first:
        copy.wait()
    depth, hidden = wh.shape
    width = wo.shape[1]
    for p in range(hidden // width):
        wh[:, p * width : (p + 1) * width] = grads[p * depth : (p + 1) * depth, :].astype(F32)
    writes.append(pltpu.make_async_copy(wh, out_wh, sem.at[2]))
    writes[-1].start()
    wo[...] = grads[hidden // width * depth :, :].astype(F32) * loss[1:2, 0:1]
    writes.append(pltpu.make_async_copy(wo, out_wo, sem.at[3]))
    writes[-1].start()
    for arrived, copy in zip(reads, writes):
        arrived.wait()
        copy.start()
    loss_o[...] = loss[0:1, 0:1]
    for copy in writes:
        copy.wait()

def body(feat_a, feat_b, w_hidden, w_out, send_rows, dest_rows, counts, neg_rows):
    points, depth = feat_a.shape[2:]
    hidden, width = w_out.shape
    n_wide, n_narrow = lax.axis_size("wide"), lax.axis_size("narrow")
    n_z = n_wide // 2
    side = math.isqrt(n_narrow)
    cap = send_rows.shape[3]
    neg_count = neg_rows.shape[2]
    total_negs = n_narrow * neg_count
    all_points = float(n_wide * n_narrow * points)
    blocks = points // min(512, points)
    stat = (8, hidden // 2)
    stat2 = (8, hidden // 2 + cap)
    grad_total = depth * hidden // width + hidden
    wh_rows = depth * hidden // width

    def sum_scratch(total):
        span = total // 2
        rows = span // n_narrow
        return (
            pltpu.VMEM((span, width), BF16),
            pltpu.VMEM((span, width), BF16),
            pltpu.VMEM((n_narrow, rows, width), BF16),
            pltpu.VMEM((rows, width), BF16),
            pltpu.VMEM((n_z, rows, width), BF16),
        )

    vmem = pl.BlockSpec(memory_space=pltpu.VMEM)
    anywhere = pl.BlockSpec(memory_space=pl.ANY)
    dma = pltpu.SemaphoreType.DMA
    out_shape = (
        jax.ShapeDtypeStruct((8, cap), F32),
        jax.ShapeDtypeStruct((points, depth), BF16),
        jax.ShapeDtypeStruct((points, depth), BF16),
        jax.ShapeDtypeStruct((grad_total, width), BF16),
    )
    scratch = [
        pltpu.VMEM((depth, hidden), BF16),
        pltpu.VMEM((hidden, width), BF16),
        pltpu.VMEM((n_narrow, cap), jnp.int32),
        pltpu.VMEM((n_narrow, cap), jnp.int32),
        pltpu.VMEM((1, n_narrow), jnp.int32),
        pltpu.VMEM((1, neg_count), jnp.int32),
        pltpu.VMEM((8, cap), F32),
        pltpu.VMEM((grad_total, width), BF16),
        pltpu.VMEM((2, points, depth), BF16),
        pltpu.VMEM((points, depth), BF16),
        pltpu.VMEM((points, hidden), F32),
        pltpu.VMEM((2, points, hidden), BF16),
        pltpu.VMEM((2, points, width), BF16),
        pltpu.VMEM((2, points, 1), F32),
        pltpu.VMEM((4, 8, hidden), F32),
        pltpu.VMEM((2, 8, depth), F32),
        pltpu.VMEM(stat, F32),
        pltpu.VMEM((n_narrow,) + stat, F32),
        pltpu.VMEM(stat, F32),
        pltpu.VMEM((n_wide,) + stat, F32),
        pltpu.VMEM(stat, F32),
        pltpu.VMEM(stat2, F32),
        pltpu.VMEM((n_narrow,) + stat2, F32),
        pltpu.VMEM(stat2, F32),
        pltpu.VMEM((n_wide,) + stat2, F32),
        pltpu.VMEM(stat2, F32),
        pltpu.VMEM((n_narrow, 8, cap), jnp.int32),
        pltpu.VMEM((n_narrow, 8, cap), jnp.int32),
        pltpu.VMEM((points, 1), jnp.int32),
        pltpu.VMEM((n_narrow, cap), jnp.int32),
        pltpu.VMEM((points, 1), jnp.int32),
        pltpu.VMEM((points, 1), F32),
        pltpu.VMEM((points, width), BF16),
        pltpu.VMEM((side, side, neg_count, width), BF16),
        pltpu.VMEM((points, width), BF16),
        pltpu.VMEM((points, total_negs), BF16),
        pltpu.VMEM((points, 1), F32),
        pltpu.VMEM((points, width), F32),
        pltpu.VMEM((width, points), BF16),
        pltpu.VMEM((points, width), BF16),
        pltpu.VMEM((points, width), BF16),
        pltpu.VMEM((points, width), BF16),
        pltpu.VMEM((side, side, neg_count, width), BF16),
        pltpu.VMEM((side, side, neg_count // 2, width), BF16),
        pltpu.VMEM((side, side, neg_count // 2, width), BF16),
        pltpu.VMEM((side, neg_count // 2, width), BF16),
        pltpu.VMEM((side, neg_count // 2, width), BF16),
        pltpu.VMEM((side, neg_count // 2, width), BF16),
        pltpu.VMEM((side, neg_count // 2, width), BF16),
        pltpu.VMEM((neg_count, width), BF16),
        pltpu.VMEM((2, points, hidden), BF16),
        pltpu.VMEM((width, hidden), F32),
        pltpu.VMEM((2, depth, hidden), F32),
        pltpu.VMEM((2, depth, hidden), F32),
        pltpu.VMEM((8, cap), F32),
        pltpu.VMEM((grad_total, width), BF16),
        *sum_scratch(wh_rows),
        *sum_scratch(hidden),
        dma((6,)),
        dma((5,)),
        dma((2, blocks)),
        dma((2, blocks)),
        dma((2, n_narrow)),
        dma((2, n_narrow)),
        dma((2, n_wide)),
        dma((2, n_narrow)),
        dma((2, n_wide)),
        dma((2, 4 * side)),
        dma((2, n_narrow)),
        dma((2, n_narrow)),
        dma((2, 4 * side)),
        dma((2, 2, 2)),
        dma((2, 2, n_narrow)),
        dma((2, 2, n_z)),
        dma((2, 2, n_narrow)),
    ]
    loss, grad_a, grad_b, grads = pl.pallas_call(
        functools.partial(step_kernel, all_points),
        out_shape=out_shape,
        in_specs=[anywhere] * 8,
        out_specs=(anywhere,) * 4,
        scratch_shapes=scratch,
        compiler_params=pltpu.CompilerParams(
            collective_id=1, has_side_effects=True, vmem_limit_bytes=63 * 1024 * 1024
        ),
        name="step",
    )(
        feat_a.reshape(points, depth),
        feat_b.reshape(points, depth),
        w_hidden,
        w_out,
        send_rows.reshape(n_narrow, cap),
        dest_rows.reshape(n_narrow, cap),
        counts.reshape(1, n_narrow),
        neg_rows.reshape(1, neg_count),
    )
    loss, grad_a, grad_b, grad_wh, grad_wo = pl.pallas_call(
        deliver_kernel,
        out_shape=(
            jax.ShapeDtypeStruct((1, 1), F32),
            jax.ShapeDtypeStruct((points, depth), BF16),
            jax.ShapeDtypeStruct((points, depth), BF16),
            jax.ShapeDtypeStruct((depth, hidden), F32),
            jax.ShapeDtypeStruct((hidden, width), F32),
        ),
        in_specs=[anywhere] * 4,
        out_specs=(vmem,) + (anywhere,) * 4,
        scratch_shapes=[
            pltpu.VMEM((8, cap), F32),
            pltpu.VMEM((grad_total, width), BF16),
            pltpu.VMEM((depth, hidden), F32),
            pltpu.VMEM((hidden, width), F32),
            pltpu.VMEM((2, points, depth), BF16),
            dma((4,)),
            dma((2, 4)),
            dma((2, 4)),
        ],
        compiler_params=pltpu.CompilerParams(vmem_limit_bytes=63 * 1024 * 1024),
        name="deliver",
    )(loss, grad_a, grad_b, grads)
    return (
        loss.reshape(()),
        grad_a.reshape(feat_a.shape),
        grad_b.reshape(feat_b.shape),
        grad_wh,
        grad_wo,
    )


def solution(mesh):
    placed = (
        P("wide", "narrow", None, None),
        P("wide", "narrow", None, None),
        P(),
        P(),
        P("wide", "narrow", None, None),
        P("wide", "narrow", None, None),
        P("wide", "narrow", None),
        P("wide", "narrow", None),
    )
    return jax.shard_map(
        body,
        mesh=mesh,
        in_specs=placed,
        out_specs=(P(), P("wide", "narrow", None, None), P("wide", "narrow", None, None), P(), P()),
        check_vma=False,
    )
```
